32 devices in a mesh: seq: 8 (over z, y), head: 4 (over x, core).
Axes of the slice: x: 2, y: 2, z: 4, core: 2. Of those that a mesh axis runs over, the one named last changes fastest.
Arguments:
- queries: bfloat16 [2048, 4096], P('seq', 'head'), may hold values from -140 to 140
- key_rows: bfloat16 [2048, 1024], P('seq', 'head'), may hold values from -15 to 15
- value_rows: bfloat16 [2048, 1024], P('seq', 'head'), may hold values from -4.5 to 4.5
- span_place: int32 [16], replicated, may hold values from 0 to 15, as said below
- block_lists: int32 [16, 3], replicated, may hold values from 0 to 14, as said below
- cotangent: bfloat16 [2048, 4096], P(('seq', 'head')), may hold values from -4.5 to 4.5
Outputs:
- attended: bfloat16 [2048, 4096], P(('seq', 'head'))
- query_grad: bfloat16 [2048, 4096], P('seq', 'head')
- key_grad: bfloat16 [2048, 1024], P('seq', 'head')
- value_grad: bfloat16 [2048, 1024], P('seq', 'head')
The draws below stay inside these ranges and needn't reach their ends.
Inputs may be any that keep to these rules, and one draw needn't show every extreme that they name: `span_place`: storage slots 2i and 2i+1 hold blocks c and 15 - c for some c below 8; each block is held once. `block_lists`: call blocks c and 15 - c a pair. Each entry of row b is an earlier block or b itself. Among the entries of the two rows of one pair, those that are not their own row's block lie in distinct pairs, none of them that pair.
All inputs are finite; a program needn't handle non-finite values.
Results may differ from the reference program's by a relative error of at most 0.035.
Values may be sent and summed in bfloat16 or wider, within the bound.
A program may use at most 64 MiB of HBM per device.

```python
import math
import jax
import jax.numpy as jnp
from jax import lax

HEADS = 32
KV_HEADS = 8
HEAD_DIM = 128
SPAN = 128
TOPK = 3
TOKENS = 2048
N_SEQ = 8


def base_keys(key, spread):
    row_width = KV_HEADS * HEAD_DIM
    drawn_draw = jnp.clip(jax.random.normal(key, (TOKENS, row_width), jnp.float32), -4.5, 4.5)
    scale_key = jax.random.fold_in(key, 101)
    row_index = jnp.arange(TOKENS, dtype=jnp.int32)
    special = (row_index % 64 == 1) | (row_index % 64 == 2)
    row_scale = jnp.exp(spread * jax.random.uniform(scale_key, (TOKENS, 1), jnp.float32, -1.15, 1.15))
    row_scale = jnp.where(special[:, None], 1.0, row_scale)
    scaled = drawn_draw * row_scale
    target = (row_index % 64 == 1)[:, None]
    return jnp.where(target, scaled, scaled)


def draw_key_rows(key, part):
    shared = base_keys(key, 0.0)
    return shared.astype(jnp.bfloat16)


def draw_queries(key, part):
    key = jax.random.fold_in(key, 5)
    drawn_draw = jnp.clip(jax.random.normal(key, (TOKENS, HEADS * HEAD_DIM), jnp.float32), -4.5, 4.5)
    return drawn_draw.astype(jnp.bfloat16)


def draw_span_place(key, part):
    key = jax.random.fold_in(key, 7)
    order = jax.random.permutation(key, N_SEQ).astype(jnp.int32)
    return jnp.stack([order, 2 * N_SEQ - 1 - order], axis=1).reshape(-1)


def draw_block_lists(key, part):
    key = jax.random.fold_in(key, 11)
    pair_count = N_SEQ
    order_key, side_key = jax.random.split(key)
    row_keys = jax.random.split(order_key, pair_count)
    orders = jax.vmap(lambda item: jax.random.permutation(item, pair_count))(row_keys).astype(jnp.int32)
    early_block = jnp.arange(pair_count, dtype=jnp.int32)[:, None]
    position = jnp.arange(pair_count, dtype=jnp.int32)[None, :]
    first_score = position + pair_count * (orders >= early_block).astype(jnp.int32)
    first_rank = jnp.argsort(first_score, axis=1, stable=True)
    first_keys = jnp.take_along_axis(orders, first_rank[:, :TOPK], axis=1)
    first_keys = jnp.where(first_keys < early_block, first_keys, early_block)
    taken_keys = orders == early_block
    for column in range(TOPK):
        taken_keys = taken_keys | (orders == first_keys[:, column:column + 1])
    second_score = position + pair_count * taken_keys.astype(jnp.int32)
    second_rank = jnp.argsort(second_score, axis=1, stable=True)
    second_keys = jnp.take_along_axis(orders, second_rank[:, :TOPK], axis=1)
    flip_bits = jax.random.randint(side_key, (pair_count, TOPK), 0, 2)
    second_blocks = jnp.where((flip_bits == 1) & (second_keys > early_block), 2 * pair_count - 1 - second_keys, second_keys)
    return jnp.concatenate([first_keys, second_blocks[::-1]], axis=0).astype(jnp.int32)


def level_of(own_key, extent, pieces, least, top_value):
    factor_of, own = 1.0, jax.random.fold_in(own_key, 6)
    for axis_at, parts in pieces:
        steps = jnp.exp(jax.random.uniform(jax.random.fold_in(own, axis_at), (parts,), jnp.float32, least / len(pieces), top_value / len(pieces)))
        factor_of = factor_of * jnp.repeat(steps, extent[axis_at] // parts).reshape([-1 if axis == axis_at else 1 for axis in range(len(extent))])
    return factor_of


def centred(key, dims, scale, limit, shards=(), held_as=jnp.bfloat16):
    entries = scale * jax.random.normal(key, dims, jnp.float32)
    if shards:
        entries = entries * level_of(key, dims, shards, -0.22, 0.18)
    return jnp.clip(entries, -limit, limit).astype(held_as)


def setup_inputs(seed: int = 0) -> dict:
    key_list = jax.random.split(jax.random.key(seed), 7)
    return {
        "queries": draw_queries(jax.random.fold_in(key_list[6], 71), 0),
        "key_rows": draw_key_rows(jax.random.fold_in(key_list[6], 71), 0),
        "value_rows": centred(key_list[2], (TOKENS, KV_HEADS * HEAD_DIM), 1.0, 4.5, ((0, 8), (1, 4))),
        "span_place": draw_span_place(jax.random.fold_in(key_list[6], 71), 0),
        "block_lists": draw_block_lists(jax.random.fold_in(key_list[6], 71), 0),
        "cotangent": centred(key_list[5], (TOKENS, HEADS * HEAD_DIM), 1.0, 4.5, ((0, 32),)),
    }


def lookup(lookup_table, selector, table_rows):
    matches = selector[..., None] == jnp.arange(table_rows, dtype=jnp.int32)
    return lax.optimization_barrier(jnp.sum(jnp.where(matches[..., None], lookup_table, 0), axis=-2))

def block_layout(span_place, block_lists):
    slot_total = span_place.shape[0]
    slot_ids = jnp.arange(slot_total, dtype=jnp.int32)
    slot_of = lax.optimization_barrier(jnp.sum(jnp.where(span_place[:, None] == slot_ids[None, :], slot_ids[:, None], 0), axis=0))
    pick_blocks = lookup(block_lists, span_place, slot_total)
    valid_cols = []
    for column in range(pick_blocks.shape[1]):
        kept_pick = pick_blocks[:, column] != span_place
        for before in range(column):
            kept_pick = kept_pick & (pick_blocks[:, column] != pick_blocks[:, before])
        valid_cols.append(kept_pick)
    pick_valid = jnp.stack(valid_cols, axis=1)
    pick_slots = lookup(slot_of[:, None], pick_blocks, slot_total)[..., 0]
    return (pick_slots.astype(jnp.int32), pick_valid)

def attend_block(query_block, key_set, value_set, grad_block, visible_picks, score_scale):
    span_rows = query_block.shape[0]
    set_count = key_set.shape[0]
    query_wide = query_block.astype(jnp.float32)
    keys_wide = key_set.astype(jnp.float32)
    values_wide = value_set.astype(jnp.float32)
    grad_wide = grad_block.astype(jnp.float32)
    scores = jnp.einsum('ckgd,jekd->kgcje', query_wide, keys_wide) * score_scale
    causal = jnp.arange(span_rows)[None, :] <= jnp.arange(span_rows)[:, None]
    others = jnp.broadcast_to(visible_picks[None, :, None], (span_rows, set_count - 1, span_rows))
    allowed = jnp.concatenate([causal[:, None, :], others], axis=1)
    scores = jnp.where(allowed, scores, -jnp.inf)
    row_top = lax.optimization_barrier(jnp.max(scores, axis=(3, 4), keepdims=True))
    row_total = lax.optimization_barrier(jnp.sum(jnp.exp(scores - row_top), axis=(3, 4), keepdims=True))
    log_total = row_top + jnp.log(row_total)
    probabilities = jnp.exp(scores - log_total)
    weights = lax.optimization_barrier(probabilities.astype(jnp.bfloat16)).astype(jnp.float32)
    attended = jnp.einsum('kgcje,jekd->ckgd', weights, values_wide).astype(jnp.bfloat16)
    attended_wide = lax.optimization_barrier(attended).astype(jnp.float32)
    row_delta = lax.optimization_barrier(jnp.sum(grad_wide * attended_wide, axis=-1))
    slopes = jnp.einsum('ckgd,jekd->kgcje', grad_wide, values_wide)
    shifted = slopes - jnp.transpose(row_delta, (1, 2, 0))[..., None, None]
    dscores = (probabilities * shifted * score_scale).astype(jnp.bfloat16)
    dscores_wide = lax.optimization_barrier(dscores).astype(jnp.float32)
    query_grad = jnp.einsum('kgcje,jekd->ckgd', dscores_wide, keys_wide).astype(jnp.bfloat16)
    key_part = jnp.einsum('kgcje,ckgd->jekd', dscores_wide, query_wide)
    value_part = jnp.einsum('kgcje,ckgd->jekd', weights, grad_wide)
    return (attended, query_grad, key_part, value_part)

def reference(queries, key_rows, value_rows, span_place, block_lists, cotangent):
    slot_total = 2 * N_SEQ
    group_size = HEADS // KV_HEADS
    score_scale = 1.0 / math.sqrt(HEAD_DIM)
    pick_slots, pick_valid = block_layout(span_place, block_lists)
    query_blocks = queries.reshape(slot_total, SPAN, KV_HEADS, group_size, HEAD_DIM)
    key_blocks = key_rows.reshape(slot_total, SPAN, KV_HEADS, HEAD_DIM)
    value_blocks = value_rows.reshape(slot_total, SPAN, KV_HEADS, HEAD_DIM)
    grad_blocks = cotangent.reshape(slot_total, SPAN, KV_HEADS, group_size, HEAD_DIM)

    def slot_step(held_grads, slot_id):
        key_sum, value_sum = held_grads
        sources = jnp.concatenate([slot_id[None], pick_slots[slot_id]]).astype(jnp.int32)
        attended, query_grad, key_part, value_part = attend_block(query_blocks[slot_id], key_blocks[sources], value_blocks[sources], grad_blocks[slot_id], pick_valid[slot_id], score_scale)
        key_round, value_round = lax.optimization_barrier((key_part[1:].astype(jnp.bfloat16), value_part[1:].astype(jnp.bfloat16)))
        targets = pick_slots[slot_id]
        key_sum = key_sum.at[slot_id].add(key_part[0]).at[targets].add(key_round.astype(jnp.float32))
        value_sum = value_sum.at[slot_id].add(value_part[0]).at[targets].add(value_round.astype(jnp.float32))
        return ((key_sum, value_sum), (attended, query_grad))
    zero_grad = jnp.zeros((slot_total, SPAN, KV_HEADS, HEAD_DIM), jnp.float32)
    (key_sum, value_sum), (attended, query_grad) = lax.scan(slot_step, (zero_grad, zero_grad), jnp.arange(slot_total, dtype=jnp.int32))
    return (attended.reshape(TOKENS, HEADS * HEAD_DIM), query_grad.reshape(TOKENS, HEADS * HEAD_DIM), key_sum.astype(jnp.bfloat16).reshape(TOKENS, KV_HEADS * HEAD_DIM), value_sum.astype(jnp.bfloat16).reshape(TOKENS, KV_HEADS * HEAD_DIM))
```

```python
import functools
import math

import jax
import jax.numpy as jnp
from jax import lax
from jax.experimental import pallas as pl
from jax.experimental.pallas import tpu as pltpu
from jax.sharding import PartitionSpec as P

HEAD_DIM = 128
HIDDEN = -1e30


def dot(left, right, left_dim, right_dim):
    return lax.dot_general(
        left, right, (((left_dim,), (right_dim,)), ((), ())), preferred_element_type=jnp.float32
    )


def kernel(
    dims,
    place_ref,
    lists_ref,
    q_ref,
    k_ref,
    v_ref,
    cot_ref,
    att_ref,
    qg_ref,
    kg_ref,
    vg_ref,
    half_tab,
    owner_tab,
    valid_tab,
    do_buf,
    att_buf,
    kv_send,
    kv_recv,
    g_send,
    g_recv,
    parts,
    own_acc,
    local_sem,
    cot_ssem,
    cot_rsem,
    att_ssem,
    att_rsem,
    kv_ssem,
    kv_rsem,
    g_ssem,
    g_rsem,
):
    n, heads, span, picks, kv_local, group = dims
    me = lax.axis_index("seq")
    hd = lax.axis_index("head")
    rows = 2 * span // heads
    width = kv_local * group * HEAD_DIM
    gwidth = group * HEAD_DIM
    scale = 1.0 / math.sqrt(HEAD_DIM)

    barrier = pltpu.get_barrier_semaphore()

    def greet_seq(step, carry):
        peer = lax.rem(me + step, n)
        pl.semaphore_signal(barrier, inc=1, device_id={"seq": peer})
        return carry

    def greet_head(step, carry):
        peer = lax.rem(hd + step, heads)
        pl.semaphore_signal(barrier, inc=1, device_id={"head": peer})
        return carry

    lax.fori_loop(1, n, greet_seq, 0)
    lax.fori_loop(1, heads, greet_head, 0)

    my_second = place_ref[2 * me + 1]

    def fill_half(peer, carry):
        wants = jnp.int32(0)
        for side in range(2):
            block = place_ref[2 * peer + side]
            for pick in range(picks):
                wants = jnp.where(lists_ref[block, pick] == my_second, 1, wants)
        half_tab[peer] = wants
        return carry

    lax.fori_loop(0, n, fill_half, 0)

    spare = lax.rem(me + 1, n)
    for side in range(2):
        own = place_ref[2 * me + side]
        blocks = [lists_ref[own, pick] for pick in range(picks)]
        for pick in range(picks):
            block = blocks[pick]
            valid = jnp.where(block != own, 1, 0)
            for before in range(pick):
                valid = jnp.where(block == blocks[before], 0, valid)

            def find(at, owner, block=block):
                hit = (place_ref[2 * at] == block) | (place_ref[2 * at + 1] == block)
                return jnp.where(hit, at, owner)

            owner = lax.fori_loop(0, n, find, jnp.int32(0))
            owner_tab[side * picks + pick] = jnp.where(valid == 1, owner, spare)
            valid_tab[side * picks + pick] = valid

    pl.semaphore_wait(barrier, n - 1 + heads - 1)

    def cot_copy(peer, slot):
        return pltpu.make_async_remote_copy(
            src_ref=cot_ref.at[:, pl.ds(pl.multiple_of(peer * width, width), width)],
            dst_ref=do_buf.at[pl.ds(pl.multiple_of(slot * rows, rows), rows), :],
            send_sem=cot_ssem.at[peer],
            recv_sem=cot_rsem.at[slot],
            device_id={"head": peer},
        )

    def att_copy(peer, slot, g):
        return pltpu.make_async_remote_copy(
            src_ref=att_buf.at[
                pl.ds(pl.multiple_of(peer * rows, rows), rows), pl.ds(g * gwidth, gwidth)
            ],
            dst_ref=att_ref.at[
                :, pl.ds(pl.multiple_of(slot * width + g * gwidth, gwidth), gwidth)
            ],
            send_sem=att_ssem.at[g, peer],
            recv_sem=att_rsem.at[g, slot],
            device_id={"head": peer},
        )

    def kv_copy(peer, slot, g):
        return pltpu.make_async_remote_copy(
            src_ref=kv_send.at[g, peer],
            dst_ref=kv_recv[g].at[slot],
            send_sem=kv_ssem.at[g, peer],
            recv_sem=kv_rsem.at[g, slot],
            device_id={"seq": peer},
        )

    def grad_copy(peer, slot, g):
        return pltpu.make_async_remote_copy(
            src_ref=g_send.at[g, peer],
            dst_ref=g_recv.at[g, slot],
            send_sem=g_ssem.at[g, peer],
            recv_sem=g_rsem.at[g, slot],
            device_id={"seq": peer},
        )

    def over_seq(action):
        def one(step, carry):
            action(lax.rem(me + step, n))
            return carry

        lax.fori_loop(1, n, one, 0)

    def over_head(action):
        def one(step, carry):
            action(lax.rem(hd + step, heads))
            return carry

        lax.fori_loop(1, heads, one, 0)

    over_head(lambda peer: cot_copy(peer, hd).start())

    for g in range(kv_local):
        cols = slice(g * HEAD_DIM, (g + 1) * HEAD_DIM)

        def send_kv(peer, g=g, cols=cols):
            second = half_tab[peer] == 1
            kv_send[g, peer, :, :HEAD_DIM] = jnp.where(second, k_ref[span:, cols], k_ref[:span, cols])
            kv_send[g, peer, :, HEAD_DIM:] = jnp.where(second, v_ref[span:, cols], v_ref[:span, cols])
            kv_copy(peer, me, g).start()

        over_seq(send_kv)

    own_cot = pltpu.make_async_copy(
        cot_ref.at[:, pl.ds(pl.multiple_of(hd * width, width), width)],
        do_buf.at[pl.ds(pl.multiple_of(hd * rows, rows), rows), :],
        local_sem.at[0],
    )
    own_cot.start()
    own_cot.wait()
    over_head(lambda peer: cot_copy(hd, peer).wait_recv())

    pair = 2
    lanes = pair * span
    key_at = lax.broadcasted_iota(jnp.int32, (span, lanes), 0)
    query_at = lax.rem(lax.broadcasted_iota(jnp.int32, (span, lanes), 1), span)
    causal = key_at <= query_at

    for g in range(kv_local):
        cols = slice(g * HEAD_DIM, (g + 1) * HEAD_DIM)
        over_seq(lambda peer, g=g: kv_copy(me, peer, g).wait_recv())

        def attend(side, carry, g=g, cols=cols):
            base = pl.multiple_of(side * span, span)
            here = pl.ds(base, span)
            keys = [k_ref[here, cols]]
            values = [v_ref[here, cols]]
            valid = []
            for pick in range(picks):
                owner = owner_tab[side * picks + pick]
                keys.append(kv_recv[g][owner, :, :HEAD_DIM])
                values.append(kv_recv[g][owner, :, HEAD_DIM:])
                valid.append(valid_tab[side * picks + pick] == 1)
            keys = jnp.concatenate(keys, axis=0)
            values = jnp.concatenate(values, axis=0)
            key_sum = None
            for chunk in range(group // pair):
                first = g * group + chunk * pair
                spots = [
                    slice((first + at) * HEAD_DIM, (first + at + 1) * HEAD_DIM)
                    for at in range(pair)
                ]
                query = jnp.concatenate([q_ref[here, spot] for spot in spots], axis=0)
                grad = jnp.concatenate([do_buf[here, spot] for spot in spots], axis=0)
                scores = dot(keys, query, 1, 1) * scale
                masked = [jnp.where(causal, scores[:span], HIDDEN)]
                for pick in range(picks):
                    piece = scores[(pick + 1) * span : (pick + 2) * span]
                    masked.append(jnp.where(valid[pick], piece, HIDDEN))
                scores = jnp.concatenate(masked, axis=0)
                top = jnp.max(scores, axis=0, keepdims=True)
                probs = jnp.exp(scores - top)
                total = jnp.sum(probs, axis=0, keepdims=True)
                probs = probs * (1.0 / total)
                weights = probs.astype(jnp.bfloat16)
                attended = dot(values, weights, 0, 0)
                slopes = dot(values, grad, 1, 1)
                delta = jnp.sum(probs * slopes, axis=0, keepdims=True)
                dscores = (probs * ((slopes - delta) * scale)).astype(jnp.bfloat16)
                query_grad = dot(keys, dscores, 0, 0)
                attended = attended.T.astype(jnp.bfloat16)
                query_grad = query_grad.T.astype(jnp.bfloat16)
                for at in range(pair):
                    att_buf[here, spots[at]] = attended[at * span : (at + 1) * span]
                    qg_ref[here, spots[at]] = query_grad[at * span : (at + 1) * span]
                key_part = dot(dscores, query, 1, 0)
                value_part = dot(weights, grad, 1, 0)
                if key_sum is None:
                    key_sum, value_sum = key_part, value_part
                else:
                    key_sum, value_sum = key_sum + key_part, value_sum + value_part
            own_acc[g, side, :, :HEAD_DIM] = key_sum[:span]
            own_acc[g, side, :, HEAD_DIM:] = value_sum[:span]
            for pick in range(picks):
                piece = slice((pick + 1) * span, (pick + 2) * span)
                parts[g, side * picks + pick, :, :HEAD_DIM] = key_sum[piece].astype(jnp.bfloat16)
                parts[g, side * picks + pick, :, HEAD_DIM:] = value_sum[piece].astype(jnp.bfloat16)
            return carry

        lax.fori_loop(0, 2, attend, 0)

        def send_grad(peer, g=g):
            spot = jnp.int32(0)
            found = jnp.int32(0)
            for at in range(2 * picks):
                hit = (owner_tab[at] == peer) & (valid_tab[at] == 1)
                spot = jnp.where(hit, at, spot)
                found = jnp.where(hit, 1, found)
            part = parts[g, spot]
            g_send[g, peer] = jnp.where(found == 1, part, jnp.zeros_like(part))
            grad_copy(peer, me, g).start()

        over_seq(send_grad)
        over_head(lambda peer, g=g: att_copy(peer, hd, g).start())

    att_ref[:, pl.ds(pl.multiple_of(hd * width, width), width)] = att_buf[
        pl.ds(pl.multiple_of(hd * rows, rows), rows), :
    ]

    for g in range(kv_local):
        cols = slice(g * HEAD_DIM, (g + 1) * HEAD_DIM)

        def add_grad(peer, g=g):
            grad_copy(me, peer, g).wait_recv()
            part = g_recv[g, peer].astype(jnp.float32)
            second = half_tab[peer] == 1
            own_acc[g, 0] += jnp.where(second, 0.0, part)
            own_acc[g, 1] += jnp.where(second, part, 0.0)

        over_seq(add_grad)
        for side in range(2):
            here = slice(side * span, (side + 1) * span)
            kg_ref[here, cols] = own_acc[g, side, :, :HEAD_DIM].astype(jnp.bfloat16)
            vg_ref[here, cols] = own_acc[g, side, :, HEAD_DIM:].astype(jnp.bfloat16)

    over_head(lambda peer: cot_copy(peer, hd).wait_send())
    for g in range(kv_local):
        over_head(lambda peer, g=g: att_copy(hd, peer, g).wait_recv())
        over_head(lambda peer, g=g: att_copy(peer, hd, g).wait_send())
        over_seq(lambda peer, g=g: kv_copy(peer, me, g).wait_send())
        over_seq(lambda peer, g=g: grad_copy(peer, me, g).wait_send())


def body(queries, key_rows, value_rows, span_place, block_lists, cotangent):
    n = lax.axis_size("seq")
    heads = lax.axis_size("head")
    span = queries.shape[0] // 2
    picks = block_lists.shape[1]
    kv_local = key_rows.shape[1] // HEAD_DIM
    group = queries.shape[1] // key_rows.shape[1]
    bf16 = jnp.bfloat16
    vmem = pl.BlockSpec(memory_space=pltpu.VMEM)
    smem = pl.BlockSpec(memory_space=pltpu.SMEM)
    box = (kv_local, n, span, 2 * HEAD_DIM)
    dma = pltpu.SemaphoreType.DMA
    flops = 6 * 2 * 2 * span * span * (picks + 1) * queries.shape[1]
    return pl.pallas_call(
        functools.partial(kernel, (n, heads, span, picks, kv_local, group)),
        out_shape=[
            jax.ShapeDtypeStruct(cotangent.shape, bf16),
            jax.ShapeDtypeStruct(queries.shape, bf16),
            jax.ShapeDtypeStruct(key_rows.shape, bf16),
            jax.ShapeDtypeStruct(value_rows.shape, bf16),
        ],
        in_specs=[smem, smem, vmem, vmem, vmem, vmem],
        out_specs=[vmem] * 4,
        scratch_shapes=[
            pltpu.SMEM((n,), jnp.int32),
            pltpu.SMEM((2 * picks,), jnp.int32),
            pltpu.SMEM((2 * picks,), jnp.int32),
            pltpu.VMEM(queries.shape, bf16),
            pltpu.VMEM(queries.shape, bf16),
            pltpu.VMEM(box, bf16),
            [pltpu.VMEM(box[1:], bf16)] * kv_local,
            pltpu.VMEM(box, bf16),
            pltpu.VMEM(box, bf16),
            pltpu.VMEM((kv_local, 2 * picks, span, 2 * HEAD_DIM), bf16),
            pltpu.VMEM((kv_local, 2, span, 2 * HEAD_DIM), jnp.float32),
            dma((1,)),
            dma((heads,)),
            dma((heads,)),
            dma((kv_local, heads)),
            dma((kv_local, heads)),
            dma((kv_local, n)),
            dma((kv_local, n)),
            dma((kv_local, n)),
            dma((kv_local, n)),
        ],
        compiler_params=pltpu.CompilerParams(
            collective_id=0, has_side_effects=True, vmem_limit_bytes=48 * 1024 * 1024
        ),
        cost_estimate=pl.CostEstimate(
            flops=flops, bytes_accessed=4 * queries.size * 2, transcendentals=flops // 1536
        ),
    )(span_place, block_lists, queries, key_rows, value_rows, cotangent)


def solution(mesh):
    in_specs = (
        P("seq", "head"),
        P("seq", "head"),
        P("seq", "head"),
        P(),
        P(),
        P(("seq", "head"), None),
    )
    out_specs = (P(("seq", "head"), None), P("seq", "head"), P("seq", "head"), P("seq", "head"))
    return jax.shard_map(body, mesh=mesh, in_specs=in_specs, out_specs=out_specs, check_vma=False)
```

```python
import functools
import math

import jax
import jax.numpy as jnp
from jax import lax
from jax.experimental import pallas as pl
from jax.experimental.pallas import tpu as pltpu
from jax.sharding import PartitionSpec as P

HEAD_DIM = 128
HIDDEN = -1e30
VMEM_BYTES = 64 * 1024 * 1024


def dot(left, right, left_dim, right_dim):
    return lax.dot_general(
        left, right, (((left_dim,), (right_dim,)), ((), ())), preferred_element_type=jnp.float32
    )


def kernel(
    dims,
    place_ref,
    lists_ref,
    q_in,
    k_in,
    v_in,
    cot_ref,
    att_ref,
    qg_out,
    kg_out,
    vg_out,
    half_tab,
    owner_tab,
    valid_tab,
    q_ref,
    k_ref,
    v_ref,
    qg_ref,
    kg_ref,
    vg_ref,
    do_buf,
    att_buf,
    kv_send,
    kv_recv,
    g_send,
    g_recv,
    parts,
    own_acc,
    local_sem,
    cot_ssem,
    cot_rsem,
    att_ssem,
    att_rsem,
    kv_ssem,
    kv_rsem,
    g_ssem,
    g_rsem,
):
    n, heads, span, picks, kv_local, group = dims
    me = lax.axis_index("seq")
    hd = lax.axis_index("head")
    rows = 2 * span // heads
    width = kv_local * group * HEAD_DIM
    gwidth = group * HEAD_DIM
    scale = 1.0 / math.sqrt(HEAD_DIM)

    fetches = [
        pltpu.make_async_copy(source, target, local_sem.at[at])
        for at, (source, target) in enumerate(((k_in, k_ref), (v_in, v_ref), (q_in, q_ref)))
    ]
    fetches.append(
        pltpu.make_async_copy(
            cot_ref.at[:, pl.ds(pl.multiple_of(hd * width, width), width)],
            do_buf.at[pl.ds(pl.multiple_of(hd * rows, rows), rows), :],
            local_sem.at[3],
        )
    )
    for fetch in fetches:
        fetch.start()

    barrier = pltpu.get_barrier_semaphore()

    def greet_seq(step, carry):
        peer = lax.rem(me + step, n)
        pl.semaphore_signal(barrier, inc=1, device_id={"seq": peer})
        return carry

    def greet_head(step, carry):
        peer = lax.rem(hd + step, heads)
        pl.semaphore_signal(barrier, inc=1, device_id={"head": peer})
        return carry

    lax.fori_loop(1, n, greet_seq, 0)
    lax.fori_loop(1, heads, greet_head, 0)

    my_second = place_ref[2 * me + 1]

    def fill_half(peer, carry):
        wants = jnp.int32(0)
        for side in range(2):
            block = place_ref[2 * peer + side]
            for pick in range(picks):
                wants = jnp.where(lists_ref[pick, block] == my_second, 1, wants)
        half_tab[peer] = wants
        return carry

    lax.fori_loop(0, n, fill_half, 0)

    spare = lax.rem(me + 1, n)
    for side in range(2):
        own = place_ref[2 * me + side]
        blocks = [lists_ref[pick, own] for pick in range(picks)]
        for pick in range(picks):
            block = blocks[pick]
            valid = jnp.where(block != own, 1, 0)
            for before in range(pick):
                valid = jnp.where(block == blocks[before], 0, valid)

            def find(at, owner, block=block):
                hit = (place_ref[2 * at] == block) | (place_ref[2 * at + 1] == block)
                return jnp.where(hit, at, owner)

            owner = lax.fori_loop(0, n, find, jnp.int32(0))
            owner_tab[side * picks + pick] = jnp.where(valid == 1, owner, spare)
            valid_tab[side * picks + pick] = valid

    pl.semaphore_wait(barrier, n - 1 + heads - 1)

    def cot_copy(peer, slot):
        return pltpu.make_async_remote_copy(
            src_ref=cot_ref.at[:, pl.ds(pl.multiple_of(peer * width, width), width)],
            dst_ref=do_buf.at[pl.ds(pl.multiple_of(slot * rows, rows), rows), :],
            send_sem=cot_ssem.at[peer],
            recv_sem=cot_rsem.at[slot],
            device_id={"head": peer},
        )

    def att_copy(peer, slot, g):
        return pltpu.make_async_remote_copy(
            src_ref=att_buf.at[
                pl.ds(pl.multiple_of(peer * rows, rows), rows), pl.ds(g * gwidth, gwidth)
            ],
            dst_ref=att_ref.at[
                :, pl.ds(pl.multiple_of(slot * width + g * gwidth, gwidth), gwidth)
            ],
            send_sem=att_ssem.at[g, peer],
            recv_sem=att_rsem.at[g, slot],
            device_id={"head": peer},
        )

    def kv_copy(peer, slot, g):
        return pltpu.make_async_remote_copy(
            src_ref=kv_send.at[g, peer],
            dst_ref=kv_recv[g].at[slot],
            send_sem=kv_ssem.at[g, peer],
            recv_sem=kv_rsem.at[g, slot],
            device_id={"seq": peer},
        )

    def grad_copy(peer, slot, g):
        return pltpu.make_async_remote_copy(
            src_ref=g_send.at[g, peer],
            dst_ref=g_recv.at[g, slot],
            send_sem=g_ssem.at[g, peer],
            recv_sem=g_rsem.at[g, slot],
            device_id={"seq": peer},
        )

    def over_seq(action):
        def one(step, carry):
            action(lax.rem(me + step, n))
            return carry

        lax.fori_loop(1, n, one, 0)

    def over_head(action):
        def one(step, carry):
            action(lax.rem(hd + step, heads))
            return carry

        lax.fori_loop(1, heads, one, 0)

    over_head(lambda peer: cot_copy(peer, hd).start())
    fetches[0].wait()
    fetches[1].wait()

    for g in range(kv_local):
        cols = slice(g * HEAD_DIM, (g + 1) * HEAD_DIM)

        def send_kv(peer, g=g, cols=cols):
            second = half_tab[peer] == 1
            kv_send[g, peer, :, :HEAD_DIM] = jnp.where(second, k_ref[span:, cols], k_ref[:span, cols])
            kv_send[g, peer, :, HEAD_DIM:] = jnp.where(second, v_ref[span:, cols], v_ref[:span, cols])
            kv_copy(peer, me, g).start()

        over_seq(send_kv)

    fetches[2].wait()
    fetches[3].wait()
    over_head(lambda peer: cot_copy(hd, peer).wait_recv())

    pair = 2
    lanes = pair * span
    key_at = lax.broadcasted_iota(jnp.int32, (span, lanes), 0)
    query_at = lax.rem(lax.broadcasted_iota(jnp.int32, (span, lanes), 1), span)
    causal = key_at <= query_at

    for g in range(kv_local):
        cols = slice(g * HEAD_DIM, (g + 1) * HEAD_DIM)
        over_seq(lambda peer, g=g: kv_copy(me, peer, g).wait_recv())

        def attend(side, carry, g=g, cols=cols):
            base = pl.multiple_of(side * span, span)
            here = pl.ds(base, span)
            keys = [k_ref[here, cols]]
            values = [v_ref[here, cols]]
            valid = []
            for pick in range(picks):
                owner = owner_tab[side * picks + pick]
                keys.append(kv_recv[g][owner, :, :HEAD_DIM])
                values.append(kv_recv[g][owner, :, HEAD_DIM:])
                valid.append(valid_tab[side * picks + pick] == 1)
            keys = jnp.concatenate(keys, axis=0)
            values = jnp.concatenate(values, axis=0)
            key_sum = None
            for chunk in range(group // pair):
                first = g * group + chunk * pair
                spots = [
                    slice((first + at) * HEAD_DIM, (first + at + 1) * HEAD_DIM)
                    for at in range(pair)
                ]
                query = jnp.concatenate([q_ref[here, spot] for spot in spots], axis=0)
                grad = jnp.concatenate([do_buf[here, spot] for spot in spots], axis=0)
                scores = dot(keys, query, 1, 1) * scale
                masked = [jnp.where(causal, scores[:span], HIDDEN)]
                for pick in range(picks):
                    piece = scores[(pick + 1) * span : (pick + 2) * span]
                    masked.append(jnp.where(valid[pick], piece, HIDDEN))
                scores = jnp.concatenate(masked, axis=0)
                top = jnp.max(scores, axis=0, keepdims=True)
                probs = jnp.exp(scores - top)
                total = jnp.sum(probs, axis=0, keepdims=True)
                probs = probs * (1.0 / total)
                weights = probs.astype(jnp.bfloat16)
                attended = dot(values, weights, 0, 0)
                slopes = dot(values, grad, 1, 1)
                delta = jnp.sum(probs * slopes, axis=0, keepdims=True)
                dscores = (probs * ((slopes - delta) * scale)).astype(jnp.bfloat16)
                query_grad = dot(keys, dscores, 0, 0)
                attended = attended.T.astype(jnp.bfloat16)
                query_grad = query_grad.T.astype(jnp.bfloat16)
                for at in range(pair):
                    att_buf[here, spots[at]] = attended[at * span : (at + 1) * span]
                    qg_ref[here, spots[at]] = query_grad[at * span : (at + 1) * span]
                key_part = dot(dscores, query, 1, 0)
                value_part = dot(weights, grad, 1, 0)
                if key_sum is None:
                    key_sum, value_sum = key_part, value_part
                else:
                    key_sum, value_sum = key_sum + key_part, value_sum + value_part
            own_acc[g, side, :, :HEAD_DIM] = key_sum[:span]
            own_acc[g, side, :, HEAD_DIM:] = value_sum[:span]
            for pick in range(picks):
                piece = slice((pick + 1) * span, (pick + 2) * span)
                parts[g, side * picks + pick, :, :HEAD_DIM] = key_sum[piece].astype(jnp.bfloat16)
                parts[g, side * picks + pick, :, HEAD_DIM:] = value_sum[piece].astype(jnp.bfloat16)
            return carry

        lax.fori_loop(0, 2, attend, 0)

        def send_grad(peer, g=g):
            spot = jnp.int32(0)
            found = jnp.int32(0)
            for at in range(2 * picks):
                hit = (owner_tab[at] == peer) & (valid_tab[at] == 1)
                spot = jnp.where(hit, at, spot)
                found = jnp.where(hit, 1, found)
            part = parts[g, spot]
            g_send[g, peer] = jnp.where(found == 1, part, jnp.zeros_like(part))
            grad_copy(peer, me, g).start()

        over_seq(send_grad)
        over_head(lambda peer, g=g: att_copy(peer, hd, g).start())

    leaving = [
        pltpu.make_async_copy(source, target, local_sem.at[at])
        for at, (source, target) in enumerate(
            (
                (
                    att_buf.at[pl.ds(pl.multiple_of(hd * rows, rows), rows), :],
                    att_ref.at[:, pl.ds(pl.multiple_of(hd * width, width), width)],
                ),
                (qg_ref, qg_out),
                (kg_ref, kg_out),
                (vg_ref, vg_out),
            )
        )
    ]
    leaving[0].start()
    leaving[1].start()

    for g in range(kv_local):
        cols = slice(g * HEAD_DIM, (g + 1) * HEAD_DIM)

        def add_grad(peer, g=g):
            grad_copy(me, peer, g).wait_recv()
            part = g_recv[g, peer].astype(jnp.float32)
            second = half_tab[peer] == 1
            own_acc[g, 0] += jnp.where(second, 0.0, part)
            own_acc[g, 1] += jnp.where(second, part, 0.0)

        over_seq(add_grad)
        for side in range(2):
            here = slice(side * span, (side + 1) * span)
            kg_ref[here, cols] = own_acc[g, side, :, :HEAD_DIM].astype(jnp.bfloat16)
            vg_ref[here, cols] = own_acc[g, side, :, HEAD_DIM:].astype(jnp.bfloat16)

    leaving[2].start()
    leaving[3].start()
    over_head(lambda peer: cot_copy(peer, hd).wait_send())
    for g in range(kv_local):
        over_head(lambda peer, g=g: att_copy(hd, peer, g).wait_recv())
        over_head(lambda peer, g=g: att_copy(peer, hd, g).wait_send())
        over_seq(lambda peer, g=g: kv_copy(peer, me, g).wait_send())
        over_seq(lambda peer, g=g: grad_copy(peer, me, g).wait_send())
    for copy in leaving:
        copy.wait()


def write_out(*refs):
    sources, targets, sems = refs[:4], refs[4:8], refs[8]
    copies = [
        pltpu.make_async_copy(source, target, sems.at[at])
        for at, (source, target) in enumerate(zip(sources, targets))
    ]
    for copy in copies:
        copy.start()
    for copy in copies:
        copy.wait()


def body(queries, key_rows, value_rows, span_place, block_lists, cotangent):
    n = lax.axis_size("seq")
    heads = lax.axis_size("head")
    span = queries.shape[0] // 2
    picks = block_lists.shape[1]
    kv_local = key_rows.shape[1] // HEAD_DIM
    group = queries.shape[1] // key_rows.shape[1]
    bf16 = jnp.bfloat16
    hbm = pl.BlockSpec(memory_space=pltpu.HBM)
    smem = pl.BlockSpec(memory_space=pltpu.SMEM)
    box = (kv_local, n, span, 2 * HEAD_DIM)
    dma = pltpu.SemaphoreType.DMA
    flops = 6 * 2 * 2 * span * span * (picks + 1) * queries.shape[1]
    results = pl.pallas_call(
        functools.partial(kernel, (n, heads, span, picks, kv_local, group)),
        out_shape=[
            jax.ShapeDtypeStruct(cotangent.shape, bf16),
            jax.ShapeDtypeStruct(queries.shape, bf16),
            jax.ShapeDtypeStruct(key_rows.shape, bf16),
            jax.ShapeDtypeStruct(value_rows.shape, bf16),
        ],
        in_specs=[smem, smem, hbm, hbm, hbm, hbm],
        out_specs=[hbm] * 4,
        scratch_shapes=[
            pltpu.SMEM((n,), jnp.int32),
            pltpu.SMEM((2 * picks,), jnp.int32),
            pltpu.SMEM((2 * picks,), jnp.int32),
            pltpu.VMEM(queries.shape, bf16),
            pltpu.VMEM(key_rows.shape, bf16),
            pltpu.VMEM(value_rows.shape, bf16),
            pltpu.VMEM(queries.shape, bf16),
            pltpu.VMEM(key_rows.shape, bf16),
            pltpu.VMEM(value_rows.shape, bf16),
            pltpu.VMEM(queries.shape, bf16),
            pltpu.VMEM(queries.shape, bf16),
            pltpu.VMEM(box, bf16),
            [pltpu.VMEM(box[1:], bf16)] * kv_local,
            pltpu.VMEM(box, bf16),
            pltpu.VMEM(box, bf16),
            pltpu.VMEM((kv_local, 2 * picks, span, 2 * HEAD_DIM), bf16),
            pltpu.VMEM((kv_local, 2, span, 2 * HEAD_DIM), jnp.float32),
            dma((4,)),
            dma((heads,)),
            dma((heads,)),
            dma((kv_local, heads)),
            dma((kv_local, heads)),
            dma((kv_local, n)),
            dma((kv_local, n)),
            dma((kv_local, n)),
            dma((kv_local, n)),
        ],
        compiler_params=pltpu.CompilerParams(
            collective_id=0, has_side_effects=True, vmem_limit_bytes=VMEM_BYTES
        ),
        cost_estimate=pl.CostEstimate(
            flops=flops, bytes_accessed=4 * queries.size * 2, transcendentals=flops // 1536
        ),
    )(span_place, block_lists.T, queries, key_rows, value_rows, cotangent)
    return tuple(
        pl.pallas_call(
            write_out,
            out_shape=[jax.ShapeDtypeStruct(item.shape, item.dtype) for item in results],
            in_specs=[hbm] * 4,
            out_specs=[hbm] * 4,
            scratch_shapes=[dma((4,))],
            compiler_params=pltpu.CompilerParams(vmem_limit_bytes=VMEM_BYTES),
        )(*results)
    )


def solution(mesh):
    in_specs = (
        P("seq", "head"),
        P("seq", "head"),
        P("seq", "head"),
        P(),
        P(),
        P(("seq", "head"), None),
    )
    out_specs = (P(("seq", "head"), None), P("seq", "head"), P("seq", "head"), P("seq", "head"))
    return jax.shard_map(body, mesh=mesh, in_specs=in_specs, out_specs=out_specs, check_vma=False)
```

```python
import functools
import math

import jax
import jax.numpy as jnp
from jax import lax
from jax.experimental import pallas as pl
from jax.experimental.pallas import tpu as pltpu
from jax.sharding import PartitionSpec as P

HEAD_DIM = 128
HIDDEN = -1e30
VMEM_BYTES = 64 * 1024 * 1024


def dot(left, right, left_dim, right_dim):
    return lax.dot_general(
        left, right, (((left_dim,), (right_dim,)), ((), ())), preferred_element_type=jnp.float32
    )


def kernel(
    dims,
    place_ref,
    lists_ref,
    q_in,
    k_in,
    v_in,
    cot_ref,
    att_ref,
    qg_out,
    kg_out,
    vg_out,
    half_tab,
    owner_tab,
    valid_tab,
    q_ref,
    k_ref,
    v_ref,
    qg_ref,
    kg_ref,
    vg_ref,
    do_buf,
    att_buf,
    kv_send,
    kv_recv,
    g_send,
    g_recv,
    parts,
    own_acc,
    local_sem,
    cot_ssem,
    cot_rsem,
    att_ssem,
    att_rsem,
    kv_ssem,
    kv_rsem,
    g_ssem,
    g_rsem,
):
    n, heads, span, picks, kv_local, group = dims
    me = lax.axis_index("seq")
    hd = lax.axis_index("head")
    rows = 2 * span // heads
    width = kv_local * group * HEAD_DIM
    gwidth = group * HEAD_DIM
    scale = 1.0 / math.sqrt(HEAD_DIM)

    fetches = [
        pltpu.make_async_copy(source, target, local_sem.at[at])
        for at, (source, target) in enumerate(((k_in, k_ref), (v_in, v_ref), (q_in, q_ref)))
    ]
    fetches.append(
        pltpu.make_async_copy(
            cot_ref.at[:, pl.ds(pl.multiple_of(hd * width, width), width)],
            do_buf.at[pl.ds(pl.multiple_of(hd * rows, rows), rows), :],
            local_sem.at[3],
        )
    )
    for fetch in fetches:
        fetch.start()

    barrier = pltpu.get_barrier_semaphore()

    def greet_seq(step, carry):
        peer = lax.rem(me + step, n)
        pl.semaphore_signal(barrier, inc=1, device_id={"seq": peer})
        return carry

    def greet_head(step, carry):
        peer = lax.rem(hd + step, heads)
        pl.semaphore_signal(barrier, inc=1, device_id={"head": peer})
        return carry

    lax.fori_loop(1, n, greet_seq, 0)
    lax.fori_loop(1, heads, greet_head, 0)

    my_second = place_ref[2 * me + 1]

    def fill_half(peer, carry):
        wants = jnp.int32(0)
        for side in range(2):
            block = place_ref[2 * peer + side]
            for pick in range(picks):
                wants = jnp.where(lists_ref[pick, block] == my_second, 1, wants)
        half_tab[peer] = wants
        return carry

    lax.fori_loop(0, n, fill_half, 0)

    spare = lax.rem(me + 1, n)
    for side in range(2):
        own = place_ref[2 * me + side]
        blocks = [lists_ref[pick, own] for pick in range(picks)]
        for pick in range(picks):
            block = blocks[pick]
            valid = jnp.where(block != own, 1, 0)
            for before in range(pick):
                valid = jnp.where(block == blocks[before], 0, valid)

            def find(at, owner, block=block):
                hit = (place_ref[2 * at] == block) | (place_ref[2 * at + 1] == block)
                return jnp.where(hit, at, owner)

            owner = lax.fori_loop(0, n, find, jnp.int32(0))
            owner_tab[side * picks + pick] = jnp.where(valid == 1, owner, spare)
            valid_tab[side * picks + pick] = valid

    pl.semaphore_wait(barrier, n - 1 + heads - 1)

    def cot_copy(peer, slot):
        return pltpu.make_async_remote_copy(
            src_ref=cot_ref.at[:, pl.ds(pl.multiple_of(peer * width, width), width)],
            dst_ref=do_buf.at[pl.ds(pl.multiple_of(slot * rows, rows), rows), :],
            send_sem=cot_ssem.at[peer],
            recv_sem=cot_rsem.at[slot],
            device_id={"head": peer},
        )

    def att_copy(peer, slot, g):
        return pltpu.make_async_remote_copy(
            src_ref=att_buf.at[
                pl.ds(pl.multiple_of(peer * rows, rows), rows), pl.ds(g * gwidth, gwidth)
            ],
            dst_ref=att_ref.at[
                :, pl.ds(pl.multiple_of(slot * width + g * gwidth, gwidth), gwidth)
            ],
            send_sem=att_ssem.at[g, peer],
            recv_sem=att_rsem.at[g, slot],
            device_id={"head": peer},
        )

    def kv_copy(peer, slot, g):
        return pltpu.make_async_remote_copy(
            src_ref=kv_send.at[g, peer],
            dst_ref=kv_recv[g].at[slot],
            send_sem=kv_ssem.at[g, peer],
            recv_sem=kv_rsem.at[g, slot],
            device_id={"seq": peer},
        )

    def grad_copy(peer, slot, g):
        return pltpu.make_async_remote_copy(
            src_ref=g_send.at[g, peer],
            dst_ref=g_recv.at[g, slot],
            send_sem=g_ssem.at[g, peer],
            recv_sem=g_rsem.at[g, slot],
            device_id={"seq": peer},
        )

    def over_seq(action):
        def one(step, carry):
            action(lax.rem(me + step, n))
            return carry

        lax.fori_loop(1, n, one, 0)

    def over_head(action):
        def one(step, carry):
            action(lax.rem(hd + step, heads))
            return carry

        lax.fori_loop(1, heads, one, 0)

    over_head(lambda peer: cot_copy(peer, hd).start())
    fetches[0].wait()
    fetches[1].wait()

    for g in range(kv_local):
        cols = slice(g * HEAD_DIM, (g + 1) * HEAD_DIM)

        def send_kv(peer, g=g, cols=cols):
            second = half_tab[peer] == 1
            kv_send[g, peer, :, :HEAD_DIM] = jnp.where(second, k_ref[span:, cols], k_ref[:span, cols])
            kv_send[g, peer, :, HEAD_DIM:] = jnp.where(second, v_ref[span:, cols], v_ref[:span, cols])
            kv_copy(peer, me, g).start()

        over_seq(send_kv)

    fetches[2].wait()
    fetches[3].wait()
    over_head(lambda peer: cot_copy(hd, peer).wait_recv())

    pair = 2
    lanes = pair * span
    key_at = lax.broadcasted_iota(jnp.int32, (span, lanes), 0)
    query_at = lax.rem(lax.broadcasted_iota(jnp.int32, (span, lanes), 1), span)
    causal = key_at <= query_at

    for g in range(kv_local):
        cols = slice(g * HEAD_DIM, (g + 1) * HEAD_DIM)
        over_seq(lambda peer, g=g: kv_copy(me, peer, g).wait_recv())

        def attend(side, carry, g=g, cols=cols):
            base = pl.multiple_of(side * span, span)
            here = pl.ds(base, span)
            keys = [k_ref[here, cols]]
            values = [v_ref[here, cols]]
            valid = []
            for pick in range(picks):
                owner = owner_tab[side * picks + pick]
                keys.append(kv_recv[g][owner, :, :HEAD_DIM])
                values.append(kv_recv[g][owner, :, HEAD_DIM:])
                valid.append(valid_tab[side * picks + pick] == 1)
            keys = jnp.concatenate(keys, axis=0)
            values = jnp.concatenate(values, axis=0)
            key_sum = None
            for chunk in range(group // pair):
                first = g * group + chunk * pair
                spots = [
                    slice((first + at) * HEAD_DIM, (first + at + 1) * HEAD_DIM)
                    for at in range(pair)
                ]
                query = jnp.concatenate([q_ref[here, spot] for spot in spots], axis=0)
                grad = jnp.concatenate([do_buf[here, spot] for spot in spots], axis=0)
                scores = dot(keys, query, 1, 1) * scale
                masked = [jnp.where(causal, scores[:span], HIDDEN)]
                for pick in range(picks):
                    piece = scores[(pick + 1) * span : (pick + 2) * span]
                    masked.append(jnp.where(valid[pick], piece, HIDDEN))
                scores = jnp.concatenate(masked, axis=0)
                top = jnp.max(scores, axis=0, keepdims=True)
                probs = jnp.exp(scores - top)
                total = jnp.sum(probs, axis=0, keepdims=True)
                probs = probs * (1.0 / total)
                weights = probs.astype(jnp.bfloat16)
                attended = dot(values, weights, 0, 0)
                slopes = dot(values, grad, 1, 1)
                delta = jnp.sum(probs * slopes, axis=0, keepdims=True)
                dscores = (probs * ((slopes - delta) * scale)).astype(jnp.bfloat16)
                query_grad = dot(keys, dscores, 0, 0)
                attended = attended.T.astype(jnp.bfloat16)
                query_grad = query_grad.T.astype(jnp.bfloat16)
                for at in range(pair):
                    att_buf[here, spots[at]] = attended[at * span : (at + 1) * span]
                    qg_ref[here, spots[at]] = query_grad[at * span : (at + 1) * span]
                key_part = dot(dscores, query, 1, 0)
                value_part = dot(weights, grad, 1, 0)
                if key_sum is None:
                    key_sum, value_sum = key_part, value_part
                else:
                    key_sum, value_sum = key_sum + key_part, value_sum + value_part
            own_acc[g, side, :, :HEAD_DIM] = key_sum[:span]
            own_acc[g, side, :, HEAD_DIM:] = value_sum[:span]
            for pick in range(picks):
                piece = slice((pick + 1) * span, (pick + 2) * span)
                parts[g, side * picks + pick, :, :HEAD_DIM] = key_sum[piece].astype(jnp.bfloat16)
                parts[g, side * picks + pick, :, HEAD_DIM:] = value_sum[piece].astype(jnp.bfloat16)
            return carry

        lax.fori_loop(0, 2, attend, 0)

        def send_grad(peer, g=g):
            spot = jnp.int32(0)
            found = jnp.int32(0)
            for at in range(2 * picks):
                hit = (owner_tab[at] == peer) & (valid_tab[at] == 1)
                spot = jnp.where(hit, at, spot)
                found = jnp.where(hit, 1, found)
            part = parts[g, spot]
            g_send[g, peer] = jnp.where(found == 1, part, jnp.zeros_like(part))
            grad_copy(peer, me, g).start()

        over_seq(send_grad)
        over_head(lambda peer, g=g: att_copy(peer, hd, g).start())

    leaving = [
        pltpu.make_async_copy(source, target, local_sem.at[at])
        for at, (source, target) in enumerate(
            (
                (
                    att_buf.at[pl.ds(pl.multiple_of(hd * rows, rows), rows), :],
                    att_ref.at[:, pl.ds(pl.multiple_of(hd * width, width), width)],
                ),
                (qg_ref, qg_out),
                (kg_ref, kg_out),
                (vg_ref, vg_out),
            )
        )
    ]
    leaving[0].start()
    leaving[1].start()

    for g in range(kv_local):
        cols = slice(g * HEAD_DIM, (g + 1) * HEAD_DIM)

        def add_grad(peer, g=g):
            grad_copy(me, peer, g).wait_recv()
            part = g_recv[g, peer].astype(jnp.float32)
            second = half_tab[peer] == 1
            own_acc[g, 0] += jnp.where(second, 0.0, part)
            own_acc[g, 1] += jnp.where(second, part, 0.0)

        over_seq(add_grad)
        for side in range(2):
            here = slice(side * span, (side + 1) * span)
            kg_ref[here, cols] = own_acc[g, side, :, :HEAD_DIM].astype(jnp.bfloat16)
            vg_ref[here, cols] = own_acc[g, side, :, HEAD_DIM:].astype(jnp.bfloat16)

    leaving[2].start()
    leaving[3].start()
    over_head(lambda peer: cot_copy(peer, hd).wait_send())
    for g in range(kv_local):
        over_head(lambda peer, g=g: att_copy(hd, peer, g).wait_recv())
        over_head(lambda peer, g=g: att_copy(peer, hd, g).wait_send())
        over_seq(lambda peer, g=g: kv_copy(peer, me, g).wait_send())
        over_seq(lambda peer, g=g: grad_copy(peer, me, g).wait_send())
    for copy in leaving:
        copy.wait()


def write_out(*refs):
    sources, targets, stages, sems = refs[:4], refs[4:8], refs[8:12], refs[12]
    arrive = [
        pltpu.make_async_copy(source, stage, sems.at[0, at])
        for at, (source, stage) in enumerate(zip(sources, stages))
    ]
    leave = [
        pltpu.make_async_copy(stage, target, sems.at[1, at])
        for at, (stage, target) in enumerate(zip(stages, targets))
    ]
    for copy in arrive:
        copy.start()
    for at in range(4):
        arrive[at].wait()
        leave[at].start()
    for copy in leave:
        copy.wait()


def body(queries, key_rows, value_rows, span_place, block_lists, cotangent):
    n = lax.axis_size("seq")
    heads = lax.axis_size("head")
    span = queries.shape[0] // 2
    picks = block_lists.shape[1]
    kv_local = key_rows.shape[1] // HEAD_DIM
    group = queries.shape[1] // key_rows.shape[1]
    bf16 = jnp.bfloat16
    hbm = pl.BlockSpec(memory_space=pltpu.HBM)
    smem = pl.BlockSpec(memory_space=pltpu.SMEM)
    box = (kv_local, n, span, 2 * HEAD_DIM)
    dma = pltpu.SemaphoreType.DMA
    flops = 6 * 2 * 2 * span * span * (picks + 1) * queries.shape[1]
    results = pl.pallas_call(
        functools.partial(kernel, (n, heads, span, picks, kv_local, group)),
        out_shape=[
            jax.ShapeDtypeStruct(cotangent.shape, bf16),
            jax.ShapeDtypeStruct(queries.shape, bf16),
            jax.ShapeDtypeStruct(key_rows.shape, bf16),
            jax.ShapeDtypeStruct(value_rows.shape, bf16),
        ],
        in_specs=[smem, smem, hbm, hbm, hbm, hbm],
        out_specs=[hbm] * 4,
        scratch_shapes=[
            pltpu.SMEM((n,), jnp.int32),
            pltpu.SMEM((2 * picks,), jnp.int32),
            pltpu.SMEM((2 * picks,), jnp.int32),
            pltpu.VMEM(queries.shape, bf16),
            pltpu.VMEM(key_rows.shape, bf16),
            pltpu.VMEM(value_rows.shape, bf16),
            pltpu.VMEM(queries.shape, bf16),
            pltpu.VMEM(key_rows.shape, bf16),
            pltpu.VMEM(value_rows.shape, bf16),
            pltpu.VMEM(queries.shape, bf16),
            pltpu.VMEM(queries.shape, bf16),
            pltpu.VMEM(box, bf16),
            [pltpu.VMEM(box[1:], bf16)] * kv_local,
            pltpu.VMEM(box, bf16),
            pltpu.VMEM(box, bf16),
            pltpu.VMEM((kv_local, 2 * picks, span, 2 * HEAD_DIM), bf16),
            pltpu.VMEM((kv_local, 2, span, 2 * HEAD_DIM), jnp.float32),
            dma((4,)),
            dma((heads,)),
            dma((heads,)),
            dma((kv_local, heads)),
            dma((kv_local, heads)),
            dma((kv_local, n)),
            dma((kv_local, n)),
            dma((kv_local, n)),
            dma((kv_local, n)),
        ],
        compiler_params=pltpu.CompilerParams(
            collective_id=0, has_side_effects=True, vmem_limit_bytes=VMEM_BYTES
        ),
        cost_estimate=pl.CostEstimate(
            flops=flops, bytes_accessed=4 * queries.size * 2, transcendentals=flops // 1536
        ),
    )(span_place, block_lists.T, queries, key_rows, value_rows, cotangent)
    return tuple(
        pl.pallas_call(
            write_out,
            out_shape=[jax.ShapeDtypeStruct(item.shape, item.dtype) for item in results],
            in_specs=[hbm] * 4,
            out_specs=[hbm] * 4,
            scratch_shapes=[pltpu.VMEM(item.shape, item.dtype) for item in results]
            + [dma((2, 4))],
            compiler_params=pltpu.CompilerParams(vmem_limit_bytes=VMEM_BYTES),
        )(*results)
    )


def solution(mesh):
    in_specs = (
        P("seq", "head"),
        P("seq", "head"),
        P("seq", "head"),
        P(),
        P(),
        P(("seq", "head"), None),
    )
    out_specs = (P(("seq", "head"), None), P("seq", "head"), P("seq", "head"), P("seq", "head"))
    return jax.shard_map(body, mesh=mesh, in_specs=in_specs, out_specs=out_specs, check_vma=False)
```

```python
import functools
import math

import jax
import jax.numpy as jnp
from jax import lax
from jax.experimental import pallas as pl
from jax.experimental.pallas import tpu as pltpu
from jax.sharding import PartitionSpec as P

HEAD_DIM = 128
HIDDEN = -1e30
VMEM_BYTES = 64 * 1024 * 1024


def dot(left, right, left_dim, right_dim):
    return lax.dot_general(
        left, right, (((left_dim,), (right_dim,)), ((), ())), preferred_element_type=jnp.float32
    )


def kernel(
    dims,
    place_ref,
    lists_ref,
    q_in,
    k_in,
    v_in,
    cot_ref,
    att_ref,
    qg_out,
    kg_out,
    vg_out,
    half_tab,
    owner_tab,
    valid_tab,
    q_ref,
    k_ref,
    v_ref,
    qg_ref,
    kg_ref,
    vg_ref,
    do_buf,
    att_buf,
    kv_send,
    kv_recv,
    g_send,
    g_recv,
    parts,
    own_acc,
    local_sem,
    cot_ssem,
    cot_rsem,
    att_ssem,
    att_rsem,
    kv_ssem,
    kv_rsem,
    g_ssem,
    g_rsem,
    sel_tab,
    full_send,
    full_recv,
    fwd_send,
    col_recv,
    comb_send,
    comb_recv,
    full_sem,
    fwd_sem,
    col_rsem,
    comb_sem,
):
    n, heads, span, picks, kv_local, group = dims
    me = lax.axis_index("seq")
    hd = lax.axis_index("head")
    rows = 2 * span // heads
    width = kv_local * group * HEAD_DIM
    gwidth = group * HEAD_DIM
    scale = 1.0 / math.sqrt(HEAD_DIM)

    relay = n == 8
    z, y = me // 2, lax.rem(me, 2)
    is_end = (z == 0) | (z == 3)
    is_inner = jnp.logical_not(is_end)
    via = jnp.where(z == 0, 4, 2) + y
    served = jnp.where(z == 2, 0, 6) + y
    far_end = jnp.where(z == 2, 6, 0)
    helped = (2 * z + 1 - y, far_end + y, far_end + 1 - y)

    def far(peer):
        apart = peer // 2 - z
        return (apart >= 2) | (apart <= -2)

    def peer_is_end(peer):
        return (peer // 2 == 0) | (peer // 2 == 3)

    def only(condition, action):
        if relay:
            pl.when(condition)(action)
        else:
            action()

    fetches = [
        pltpu.make_async_copy(source, target, local_sem.at[at])
        for at, (source, target) in enumerate(((k_in, k_ref), (v_in, v_ref), (q_in, q_ref)))
    ]
    fetches.append(
        pltpu.make_async_copy(
            cot_ref.at[:, pl.ds(pl.multiple_of(hd * width, width), width)],
            do_buf.at[pl.ds(pl.multiple_of(hd * rows, rows), rows), :],
            local_sem.at[3],
        )
    )
    for fetch in fetches:
        fetch.start()

    barrier = pltpu.get_barrier_semaphore()

    def greet_seq(step, carry):
        peer = lax.rem(me + step, n)
        pl.semaphore_signal(barrier, inc=1, device_id={"seq": peer})
        return carry

    def greet_head(step, carry):
        peer = lax.rem(hd + step, heads)
        pl.semaphore_signal(barrier, inc=1, device_id={"head": peer})
        return carry

    lax.fori_loop(1, n, greet_seq, 0)
    lax.fori_loop(1, heads, greet_head, 0)

    my_second = place_ref[2 * me + 1]

    def fill_half(peer, carry):
        wants = jnp.int32(0)
        for side in range(2):
            block = place_ref[2 * peer + side]
            for pick in range(picks):
                wants = jnp.where(lists_ref[pick, block] == my_second, 1, wants)
        half_tab[peer] = wants
        return carry

    lax.fori_loop(0, n, fill_half, 0)

    if relay:
        end_second = place_ref[2 * served + 1]
        for at, who in enumerate(helped + (me,)):
            wants = jnp.int32(0)
            for side in range(2):
                block = place_ref[2 * who + side]
                for pick in range(picks):
                    wants = jnp.where(lists_ref[pick, block] == end_second, 1, wants)
            sel_tab[at] = wants

    spare = lax.rem(me + 1, n)
    for side in range(2):
        own = place_ref[2 * me + side]
        blocks = [lists_ref[pick, own] for pick in range(picks)]
        for pick in range(picks):
            block = blocks[pick]
            valid = jnp.where(block != own, 1, 0)
            for before in range(pick):
                valid = jnp.where(block == blocks[before], 0, valid)

            def find(at, owner, block=block):
                hit = (place_ref[2 * at] == block) | (place_ref[2 * at + 1] == block)
                return jnp.where(hit, at, owner)

            owner = lax.fori_loop(0, n, find, jnp.int32(0))
            owner_tab[side * picks + pick] = jnp.where(valid == 1, owner, spare)
            valid_tab[side * picks + pick] = valid

    pl.semaphore_wait(barrier, n - 1 + heads - 1)

    def cot_copy(peer, slot):
        return pltpu.make_async_remote_copy(
            src_ref=cot_ref.at[:, pl.ds(pl.multiple_of(peer * width, width), width)],
            dst_ref=do_buf.at[pl.ds(pl.multiple_of(slot * rows, rows), rows), :],
            send_sem=cot_ssem.at[peer],
            recv_sem=cot_rsem.at[slot],
            device_id={"head": peer},
        )

    def att_copy(peer, slot, g):
        return pltpu.make_async_remote_copy(
            src_ref=att_buf.at[
                pl.ds(pl.multiple_of(peer * rows, rows), rows), pl.ds(g * gwidth, gwidth)
            ],
            dst_ref=att_ref.at[
                :, pl.ds(pl.multiple_of(slot * width + g * gwidth, gwidth), gwidth)
            ],
            send_sem=att_ssem.at[g, peer],
            recv_sem=att_rsem.at[g, slot],
            device_id={"head": peer},
        )

    def kv_copy(peer, slot, g):
        return pltpu.make_async_remote_copy(
            src_ref=kv_send.at[g, peer],
            dst_ref=kv_recv[g].at[slot],
            send_sem=kv_ssem.at[g, peer],
            recv_sem=kv_rsem.at[g, slot],
            device_id={"seq": peer},
        )

    def grad_copy(peer, slot, g):
        return pltpu.make_async_remote_copy(
            src_ref=g_send.at[g, peer],
            dst_ref=g_recv.at[g, slot],
            send_sem=g_ssem.at[g, peer],
            recv_sem=g_rsem.at[g, slot],
            device_id={"seq": peer},
        )

    def full_copy(g):
        return pltpu.make_async_remote_copy(
            src_ref=full_send.at[g],
            dst_ref=full_recv.at[g],
            send_sem=full_sem.at[0, g],
            recv_sem=full_sem.at[1, g],
            device_id={"seq": via},
        )

    def forward_copy(g, at):
        return pltpu.make_async_remote_copy(
            src_ref=fwd_send.at[g, at],
            dst_ref=kv_recv[g].at[served],
            send_sem=fwd_sem.at[g, at],
            recv_sem=kv_rsem.at[g, served],
            device_id={"seq": helped[at]},
        )

    def collect_copy(peer, slot, g):
        through = jnp.where(peer // 2 == 0, 4, 2) + lax.rem(peer, 2)
        return pltpu.make_async_remote_copy(
            src_ref=g_send.at[g, peer],
            dst_ref=col_recv.at[g, slot],
            send_sem=g_ssem.at[g, peer],
            recv_sem=col_rsem.at[g, slot],
            device_id={"seq": through},
        )

    def combined_copy(g):
        return pltpu.make_async_remote_copy(
            src_ref=comb_send.at[g],
            dst_ref=comb_recv.at[g],
            send_sem=comb_sem.at[0, g],
            recv_sem=comb_sem.at[1, g],
            device_id={"seq": served},
        )

    def over_seq(action):
        def one(step, carry):
            action(lax.rem(me + step, n))
            return carry

        lax.fori_loop(1, n, one, 0)

    def over_head(action):
        def one(step, carry):
            action(lax.rem(hd + step, heads))
            return carry

        lax.fori_loop(1, heads, one, 0)

    over_head(lambda peer: cot_copy(peer, hd).start())
    fetches[0].wait()
    fetches[1].wait()

    for g in range(kv_local):
        cols = slice(g * HEAD_DIM, (g + 1) * HEAD_DIM)

        if relay:

            @pl.when(is_end)
            def _(g=g, cols=cols):
                full_send[g, :, :HEAD_DIM] = k_ref[:, cols]
                full_send[g, :, HEAD_DIM:] = v_ref[:, cols]
                full_copy(g).start()

        def send_kv(peer, g=g, cols=cols):
            second = half_tab[peer] == 1
            kv_send[g, peer, :, :HEAD_DIM] = jnp.where(second, k_ref[span:, cols], k_ref[:span, cols])
            kv_send[g, peer, :, HEAD_DIM:] = jnp.where(second, v_ref[span:, cols], v_ref[:span, cols])
            only(jnp.logical_not(is_end & far(peer)), kv_copy(peer, me, g).start)

        over_seq(send_kv)

    fetches[2].wait()
    fetches[3].wait()
    if relay:
        for g in range(kv_local):

            @pl.when(is_inner)
            def _(g=g):
                full_copy(g).wait_recv()
                for at in range(4):
                    second = sel_tab[at] == 1
                    block = jnp.where(second, full_recv[g, span:], full_recv[g, :span])
                    if at < 3:
                        fwd_send[g, at] = block
                        forward_copy(g, at).start()
                    else:
                        kv_recv[g][served] = block

    over_head(lambda peer: cot_copy(hd, peer).wait_recv())

    pair = 2
    lanes = pair * span
    key_at = lax.broadcasted_iota(jnp.int32, (span, lanes), 0)
    query_at = lax.rem(lax.broadcasted_iota(jnp.int32, (span, lanes), 1), span)
    causal = key_at <= query_at

    for g in range(kv_local):
        cols = slice(g * HEAD_DIM, (g + 1) * HEAD_DIM)
        over_seq(
            lambda peer, g=g: only(
                jnp.logical_not(is_inner & (peer == served)), kv_copy(me, peer, g).wait_recv
            )
        )

        def attend(side, carry, g=g, cols=cols):
            base = pl.multiple_of(side * span, span)
            here = pl.ds(base, span)
            keys = [k_ref[here, cols]]
            values = [v_ref[here, cols]]
            valid = []
            for pick in range(picks):
                owner = owner_tab[side * picks + pick]
                keys.append(kv_recv[g][owner, :, :HEAD_DIM])
                values.append(kv_recv[g][owner, :, HEAD_DIM:])
                valid.append(valid_tab[side * picks + pick] == 1)
            keys = jnp.concatenate(keys, axis=0)
            values = jnp.concatenate(values, axis=0)
            key_sum = None
            for chunk in range(group // pair):
                first = g * group + chunk * pair
                spots = [
                    slice((first + at) * HEAD_DIM, (first + at + 1) * HEAD_DIM)
                    for at in range(pair)
                ]
                query = jnp.concatenate([q_ref[here, spot] for spot in spots], axis=0)
                grad = jnp.concatenate([do_buf[here, spot] for spot in spots], axis=0)
                scores = dot(keys, query, 1, 1) * scale
                masked = [jnp.where(causal, scores[:span], HIDDEN)]
                for pick in range(picks):
                    piece = scores[(pick + 1) * span : (pick + 2) * span]
                    masked.append(jnp.where(valid[pick], piece, HIDDEN))
                scores = jnp.concatenate(masked, axis=0)
                top = jnp.max(scores, axis=0, keepdims=True)
                probs = jnp.exp(scores - top)
                total = jnp.sum(probs, axis=0, keepdims=True)
                probs = probs * (1.0 / total)
                weights = probs.astype(jnp.bfloat16)
                attended = dot(values, weights, 0, 0)
                slopes = dot(values, grad, 1, 1)
                delta = jnp.sum(probs * slopes, axis=0, keepdims=True)
                dscores = (probs * ((slopes - delta) * scale)).astype(jnp.bfloat16)
                query_grad = dot(keys, dscores, 0, 0)
                attended = attended.T.astype(jnp.bfloat16)
                query_grad = query_grad.T.astype(jnp.bfloat16)
                for at in range(pair):
                    att_buf[here, spots[at]] = attended[at * span : (at + 1) * span]
                    qg_ref[here, spots[at]] = query_grad[at * span : (at + 1) * span]
                key_part = dot(dscores, query, 1, 0)
                value_part = dot(weights, grad, 1, 0)
                if key_sum is None:
                    key_sum, value_sum = key_part, value_part
                else:
                    key_sum, value_sum = key_sum + key_part, value_sum + value_part
            own_acc[g, side, :, :HEAD_DIM] = key_sum[:span]
            own_acc[g, side, :, HEAD_DIM:] = value_sum[:span]
            for pick in range(picks):
                piece = slice((pick + 1) * span, (pick + 2) * span)
                parts[g, side * picks + pick, :, :HEAD_DIM] = key_sum[piece].astype(jnp.bfloat16)
                parts[g, side * picks + pick, :, HEAD_DIM:] = value_sum[piece].astype(jnp.bfloat16)
            return carry

        lax.fori_loop(0, 2, attend, 0)

        def send_grad(peer, g=g):
            spot = jnp.int32(0)
            found = jnp.int32(0)
            for at in range(2 * picks):
                hit = (owner_tab[at] == peer) & (valid_tab[at] == 1)
                spot = jnp.where(hit, at, spot)
                found = jnp.where(hit, 1, found)
            part = parts[g, spot]
            g_send[g, peer] = jnp.where(found == 1, part, jnp.zeros_like(part))
            through_other = peer_is_end(peer) & far(peer)
            only(jnp.logical_not(through_other), grad_copy(peer, me, g).start)
            if relay:
                slot = jnp.where(is_inner, 0, jnp.where(lax.rem(peer, 2) == y, 1, 2))
                here = is_inner & (peer == served)

                @pl.when(through_other & jnp.logical_not(here))
                def _():
                    collect_copy(peer, slot, g).start()

        over_seq(send_grad)
        over_head(lambda peer, g=g: att_copy(peer, hd, g).start())

    if relay:
        for g in range(kv_local):

            @pl.when(is_inner)
            def _(g=g):
                sums = [jnp.zeros((span, 2 * HEAD_DIM), jnp.float32)] * 2
                for at in range(4):
                    if at < 3:
                        collect_copy(served, at, g).wait_recv()
                        part = col_recv[g, at].astype(jnp.float32)
                    else:
                        part = g_send[g, served].astype(jnp.float32)
                    second = sel_tab[at] == 1
                    sums[0] = sums[0] + jnp.where(second, 0.0, part)
                    sums[1] = sums[1] + jnp.where(second, part, 0.0)
                for side in range(2):
                    comb_send[g, side] = sums[side].astype(jnp.bfloat16)
                combined_copy(g).start()

    leaving = [
        pltpu.make_async_copy(source, target, local_sem.at[at])
        for at, (source, target) in enumerate(
            (
                (
                    att_buf.at[pl.ds(pl.multiple_of(hd * rows, rows), rows), :],
                    att_ref.at[:, pl.ds(pl.multiple_of(hd * width, width), width)],
                ),
                (qg_ref, qg_out),
                (kg_ref, kg_out),
                (vg_ref, vg_out),
            )
        )
    ]
    leaving[0].start()
    leaving[1].start()

    for g in range(kv_local):
        cols = slice(g * HEAD_DIM, (g + 1) * HEAD_DIM)

        def add_grad(peer, g=g):
            def arrived():
                grad_copy(me, peer, g).wait_recv()
                part = g_recv[g, peer].astype(jnp.float32)
                second = half_tab[peer] == 1
                own_acc[g, 0] += jnp.where(second, 0.0, part)
                own_acc[g, 1] += jnp.where(second, part, 0.0)

            only(jnp.logical_not(is_end & far(peer)), arrived)

        over_seq(add_grad)
        if relay:

            @pl.when(is_end)
            def _(g=g):
                combined_copy(g).wait_recv()
                for side in range(2):
                    own_acc[g, side] += comb_recv[g, side].astype(jnp.float32)

        for side in range(2):
            here = slice(side * span, (side + 1) * span)
            kg_ref[here, cols] = own_acc[g, side, :, :HEAD_DIM].astype(jnp.bfloat16)
            vg_ref[here, cols] = own_acc[g, side, :, HEAD_DIM:].astype(jnp.bfloat16)

    leaving[2].start()
    leaving[3].start()
    over_head(lambda peer: cot_copy(peer, hd).wait_send())
    for g in range(kv_local):
        over_head(lambda peer, g=g: att_copy(hd, peer, g).wait_recv())
        over_head(lambda peer, g=g: att_copy(peer, hd, g).wait_send())
        over_seq(
            lambda peer, g=g: only(
                jnp.logical_not(is_end & far(peer)), kv_copy(peer, me, g).wait_send
            )
        )
        over_seq(
            lambda peer, g=g: only(
                jnp.logical_not(is_inner & (peer == served)), grad_copy(peer, me, g).wait_send
            )
        )
        if relay:

            @pl.when(is_end)
            def _(g=g):
                full_copy(g).wait_send()

            @pl.when(is_inner)
            def _(g=g):
                for at in range(3):
                    forward_copy(g, at).wait_send()
                combined_copy(g).wait_send()

    for copy in leaving:
        copy.wait()


def write_out(*refs):
    sources, targets, stages, sems = refs[:4], refs[4:8], refs[8:12], refs[12]
    arrive = [
        pltpu.make_async_copy(source, stage, sems.at[0, at])
        for at, (source, stage) in enumerate(zip(sources, stages))
    ]
    leave = [
        pltpu.make_async_copy(stage, target, sems.at[1, at])
        for at, (stage, target) in enumerate(zip(stages, targets))
    ]
    for copy in arrive:
        copy.start()
    for at in range(4):
        arrive[at].wait()
        leave[at].start()
    for copy in leave:
        copy.wait()


def body(queries, key_rows, value_rows, span_place, block_lists, cotangent):
    n = lax.axis_size("seq")
    heads = lax.axis_size("head")
    span = queries.shape[0] // 2
    picks = block_lists.shape[1]
    kv_local = key_rows.shape[1] // HEAD_DIM
    group = queries.shape[1] // key_rows.shape[1]
    bf16 = jnp.bfloat16
    hbm = pl.BlockSpec(memory_space=pltpu.HBM)
    smem = pl.BlockSpec(memory_space=pltpu.SMEM)
    box = (kv_local, n, span, 2 * HEAD_DIM)
    dma = pltpu.SemaphoreType.DMA
    flops = 6 * 2 * 2 * span * span * (picks + 1) * queries.shape[1]
    results = pl.pallas_call(
        functools.partial(kernel, (n, heads, span, picks, kv_local, group)),
        out_shape=[
            jax.ShapeDtypeStruct(cotangent.shape, bf16),
            jax.ShapeDtypeStruct(queries.shape, bf16),
            jax.ShapeDtypeStruct(key_rows.shape, bf16),
            jax.ShapeDtypeStruct(value_rows.shape, bf16),
        ],
        in_specs=[smem, smem, hbm, hbm, hbm, hbm],
        out_specs=[hbm] * 4,
        scratch_shapes=[
            pltpu.SMEM((n,), jnp.int32),
            pltpu.SMEM((2 * picks,), jnp.int32),
            pltpu.SMEM((2 * picks,), jnp.int32),
            pltpu.VMEM(queries.shape, bf16),
            pltpu.VMEM(key_rows.shape, bf16),
            pltpu.VMEM(value_rows.shape, bf16),
            pltpu.VMEM(queries.shape, bf16),
            pltpu.VMEM(key_rows.shape, bf16),
            pltpu.VMEM(value_rows.shape, bf16),
            pltpu.VMEM(queries.shape, bf16),
            pltpu.VMEM(queries.shape, bf16),
            pltpu.VMEM(box, bf16),
            [pltpu.VMEM(box[1:], bf16)] * kv_local,
            pltpu.VMEM(box, bf16),
            pltpu.VMEM(box, bf16),
            pltpu.VMEM((kv_local, 2 * picks, span, 2 * HEAD_DIM), bf16),
            pltpu.VMEM((kv_local, 2, span, 2 * HEAD_DIM), jnp.float32),
            dma((4,)),
            dma((heads,)),
            dma((heads,)),
            dma((kv_local, heads)),
            dma((kv_local, heads)),
            dma((kv_local, n)),
            dma((kv_local, n)),
            dma((kv_local, n)),
            dma((kv_local, n)),
            pltpu.SMEM((4,), jnp.int32),
            pltpu.VMEM((kv_local, 2 * span, 2 * HEAD_DIM), bf16),
            pltpu.VMEM((kv_local, 2 * span, 2 * HEAD_DIM), bf16),
            pltpu.VMEM((kv_local, 3, span, 2 * HEAD_DIM), bf16),
            pltpu.VMEM((kv_local, 3, span, 2 * HEAD_DIM), bf16),
            pltpu.VMEM((kv_local, 2, span, 2 * HEAD_DIM), bf16),
            pltpu.VMEM((kv_local, 2, span, 2 * HEAD_DIM), bf16),
            dma((2, kv_local)),
            dma((kv_local, 3)),
            dma((kv_local, 3)),
            dma((2, kv_local)),
        ],
        compiler_params=pltpu.CompilerParams(
            collective_id=0, has_side_effects=True, vmem_limit_bytes=VMEM_BYTES
        ),
        cost_estimate=pl.CostEstimate(
            flops=flops, bytes_accessed=4 * queries.size * 2, transcendentals=flops // 1536
        ),
    )(span_place, block_lists.T, queries, key_rows, value_rows, cotangent)
    return tuple(
        pl.pallas_call(
            write_out,
            out_shape=[jax.ShapeDtypeStruct(item.shape, item.dtype) for item in results],
            in_specs=[hbm] * 4,
            out_specs=[hbm] * 4,
            scratch_shapes=[pltpu.VMEM(item.shape, item.dtype) for item in results]
            + [dma((2, 4))],
            compiler_params=pltpu.CompilerParams(vmem_limit_bytes=VMEM_BYTES),
        )(*results)
    )


def solution(mesh):
    in_specs = (
        P("seq", "head"),
        P("seq", "head"),
        P("seq", "head"),
        P(),
        P(),
        P(("seq", "head"), None),
    )
    out_specs = (P(("seq", "head"), None), P("seq", "head"), P("seq", "head"), P("seq", "head"))
    return jax.shard_map(body, mesh=mesh, in_specs=in_specs, out_specs=out_specs, check_vma=False)
```

```python
import functools
import math

import jax
import jax.numpy as jnp
from jax import lax
from jax.experimental import pallas as pl
from jax.experimental.pallas import tpu as pltpu
from jax.sharding import PartitionSpec as P

HEAD_DIM = 128
HIDDEN = -1e30
VMEM_BYTES = 64 * 1024 * 1024


def dot(left, right, left_dim, right_dim):
    return lax.dot_general(
        left, right, (((left_dim,), (right_dim,)), ((), ())), preferred_element_type=jnp.float32
    )


def kernel(
    dims,
    place_ref,
    lists_ref,
    q_in,
    k_in,
    v_in,
    cot_ref,
    att_ref,
    qg_out,
    kg_out,
    vg_out,
    half_tab,
    owner_tab,
    valid_tab,
    q_ref,
    k_ref,
    v_ref,
    qg_ref,
    kg_ref,
    vg_ref,
    do_buf,
    att_buf,
    kv_send,
    kv_recv,
    g_send,
    g_recv,
    parts,
    own_acc,
    local_sem,
    cot_ssem,
    cot_rsem,
    att_ssem,
    att_rsem,
    kv_ssem,
    kv_rsem,
    g_ssem,
    g_rsem,
    sel_tab,
    full_send,
    full_recv,
    fwd_send,
    col_recv,
    comb_send,
    comb_recv,
    full_sem,
    fwd_sem,
    col_rsem,
    comb_sem,
):
    n, heads, span, picks, kv_local, group = dims
    me = lax.axis_index("seq")
    hd = lax.axis_index("head")
    rows = 2 * span // heads
    width = kv_local * group * HEAD_DIM
    gwidth = group * HEAD_DIM
    scale = 1.0 / math.sqrt(HEAD_DIM)

    relay = n == 8
    z, y = me // 2, lax.rem(me, 2)
    is_end = (z == 0) | (z == 3)
    is_inner = jnp.logical_not(is_end)
    via = jnp.where(z == 0, 4, 2) + y
    served = jnp.where(z == 2, 0, 6) + y
    far_end = jnp.where(z == 2, 6, 0)
    helped = (2 * z + 1 - y, far_end + y, far_end + 1 - y)

    def far(peer):
        apart = peer // 2 - z
        return (apart >= 2) | (apart <= -2)

    def peer_is_end(peer):
        return (peer // 2 == 0) | (peer // 2 == 3)

    def only(condition, action):
        if relay:
            pl.when(condition)(action)
        else:
            action()

    fetches = [
        pltpu.make_async_copy(source, target, local_sem.at[at])
        for at, (source, target) in enumerate(((k_in, k_ref), (v_in, v_ref), (q_in, q_ref)))
    ]
    fetches.append(
        pltpu.make_async_copy(
            cot_ref.at[:, pl.ds(pl.multiple_of(hd * width, width), width)],
            do_buf.at[pl.ds(pl.multiple_of(hd * rows, rows), rows), :],
            local_sem.at[3],
        )
    )
    for fetch in fetches:
        fetch.start()

    barrier = pltpu.get_barrier_semaphore()

    def greet_seq(step, carry):
        peer = lax.rem(me + step, n)
        pl.semaphore_signal(barrier, inc=1, device_id={"seq": peer})
        return carry

    def greet_head(step, carry):
        peer = lax.rem(hd + step, heads)
        pl.semaphore_signal(barrier, inc=1, device_id={"head": peer})
        return carry

    lax.fori_loop(1, n, greet_seq, 0)
    lax.fori_loop(1, heads, greet_head, 0)

    my_second = place_ref[2 * me + 1]

    def fill_half(peer, carry):
        wants = jnp.int32(0)
        for side in range(2):
            block = place_ref[2 * peer + side]
            for pick in range(picks):
                wants = jnp.where(lists_ref[pick, block] == my_second, 1, wants)
        half_tab[peer] = wants
        return carry

    lax.fori_loop(0, n, fill_half, 0)

    if relay:
        end_second = place_ref[2 * served + 1]
        for at, who in enumerate(helped + (me,)):
            wants = jnp.int32(0)
            for side in range(2):
                block = place_ref[2 * who + side]
                for pick in range(picks):
                    wants = jnp.where(lists_ref[pick, block] == end_second, 1, wants)
            sel_tab[at] = wants

    spare = lax.rem(me + 1, n)
    for side in range(2):
        own = place_ref[2 * me + side]
        blocks = [lists_ref[pick, own] for pick in range(picks)]
        for pick in range(picks):
            block = blocks[pick]
            valid = jnp.where(block != own, 1, 0)
            for before in range(pick):
                valid = jnp.where(block == blocks[before], 0, valid)

            def find(at, owner, block=block):
                hit = (place_ref[2 * at] == block) | (place_ref[2 * at + 1] == block)
                return jnp.where(hit, at, owner)

            owner = lax.fori_loop(0, n, find, jnp.int32(0))
            owner_tab[side * picks + pick] = jnp.where(valid == 1, owner, spare)
            valid_tab[side * picks + pick] = valid

    pl.semaphore_wait(barrier, n - 1 + heads - 1)

    def cot_copy(peer, slot):
        return pltpu.make_async_remote_copy(
            src_ref=cot_ref.at[:, pl.ds(pl.multiple_of(peer * width, width), width)],
            dst_ref=do_buf.at[pl.ds(pl.multiple_of(slot * rows, rows), rows), :],
            send_sem=cot_ssem.at[peer],
            recv_sem=cot_rsem.at[slot],
            device_id={"head": peer},
        )

    def att_copy(peer, slot, g):
        return pltpu.make_async_remote_copy(
            src_ref=att_buf.at[
                pl.ds(pl.multiple_of(peer * rows, rows), rows), pl.ds(g * gwidth, gwidth)
            ],
            dst_ref=att_ref.at[
                :, pl.ds(pl.multiple_of(slot * width + g * gwidth, gwidth), gwidth)
            ],
            send_sem=att_ssem.at[g, peer],
            recv_sem=att_rsem.at[g, slot],
            device_id={"head": peer},
        )

    def kv_copy(peer, slot, g):
        return pltpu.make_async_remote_copy(
            src_ref=kv_send.at[g, peer],
            dst_ref=kv_recv[g].at[slot],
            send_sem=kv_ssem.at[g, peer],
            recv_sem=kv_rsem.at[g, slot],
            device_id={"seq": peer},
        )

    def grad_copy(peer, slot, g):
        return pltpu.make_async_remote_copy(
            src_ref=g_send.at[g, peer],
            dst_ref=g_recv.at[g, slot],
            send_sem=g_ssem.at[g, peer],
            recv_sem=g_rsem.at[g, slot],
            device_id={"seq": peer},
        )

    def full_copy(g):
        return pltpu.make_async_remote_copy(
            src_ref=full_send.at[g],
            dst_ref=full_recv.at[g],
            send_sem=full_sem.at[0, g],
            recv_sem=full_sem.at[1, g],
            device_id={"seq": via},
        )

    def forward_copy(g, at):
        return pltpu.make_async_remote_copy(
            src_ref=fwd_send.at[g, at],
            dst_ref=kv_recv[g].at[served],
            send_sem=fwd_sem.at[g, at],
            recv_sem=kv_rsem.at[g, served],
            device_id={"seq": helped[at]},
        )

    def collect_copy(peer, slot, g):
        through = jnp.where(peer // 2 == 0, 4, 2) + lax.rem(peer, 2)
        return pltpu.make_async_remote_copy(
            src_ref=g_send.at[g, peer],
            dst_ref=col_recv.at[g, slot],
            send_sem=g_ssem.at[g, peer],
            recv_sem=col_rsem.at[g, slot],
            device_id={"seq": through},
        )

    def combined_copy(g):
        return pltpu.make_async_remote_copy(
            src_ref=comb_send.at[g],
            dst_ref=comb_recv.at[g],
            send_sem=comb_sem.at[0, g],
            recv_sem=comb_sem.at[1, g],
            device_id={"seq": served},
        )

    def over_seq(action):
        def one(step, carry):
            action(lax.rem(me + step, n))
            return carry

        lax.fori_loop(1, n, one, 0)

    def over_head(action):
        def one(step, carry):
            action(lax.rem(hd + step, heads))
            return carry

        lax.fori_loop(1, heads, one, 0)

    over_head(lambda peer: cot_copy(peer, hd).start())
    fetches[0].wait()
    fetches[1].wait()

    def send_keys(g):
        cols = slice(g * HEAD_DIM, (g + 1) * HEAD_DIM)
        if relay:

            @pl.when(is_end)
            def _():
                full_send[g, :, :HEAD_DIM] = k_ref[:, cols]
                full_send[g, :, HEAD_DIM:] = v_ref[:, cols]
                if g > 0:
                    full_copy(g - 1).wait_send()
                full_copy(g).start()

        def send_kv(peer):
            second = half_tab[peer] == 1
            kv_send[g, peer, :, :HEAD_DIM] = jnp.where(second, k_ref[span:, cols], k_ref[:span, cols])
            kv_send[g, peer, :, HEAD_DIM:] = jnp.where(second, v_ref[span:, cols], v_ref[:span, cols])

            def go():
                if g > 0:
                    kv_copy(peer, me, g - 1).wait_send()
                kv_copy(peer, me, g).start()

            only(jnp.logical_not(is_end & far(peer)), go)

        over_seq(send_kv)

    def relay_keys(g):
        if relay:

            @pl.when(is_inner)
            def _():
                full_copy(g).wait_recv()
                for at in range(4):
                    second = sel_tab[at] == 1
                    block = jnp.where(second, full_recv[g, span:], full_recv[g, :span])
                    if at < 3:
                        fwd_send[g, at] = block
                        forward_copy(g, at).start()
                    else:
                        kv_recv[g][served] = block

    send_keys(0)
    relay_keys(0)
    for g in range(1, kv_local):
        send_keys(g)
    fetches[2].wait()
    fetches[3].wait()
    over_head(lambda peer: cot_copy(hd, peer).wait_recv())

    pair = 2
    lanes = pair * span
    key_at = lax.broadcasted_iota(jnp.int32, (span, lanes), 0)
    query_at = lax.rem(lax.broadcasted_iota(jnp.int32, (span, lanes), 1), span)
    causal = key_at <= query_at

    for g in range(kv_local):
        cols = slice(g * HEAD_DIM, (g + 1) * HEAD_DIM)
        if g > 0:
            relay_keys(g)
        over_seq(
            lambda peer, g=g: only(
                jnp.logical_not(is_inner & (peer == served)), kv_copy(me, peer, g).wait_recv
            )
        )

        def attend(side, carry, g=g, cols=cols):
            base = pl.multiple_of(side * span, span)
            here = pl.ds(base, span)
            keys = [k_ref[here, cols]]
            values = [v_ref[here, cols]]
            valid = []
            for pick in range(picks):
                owner = owner_tab[side * picks + pick]
                keys.append(kv_recv[g][owner, :, :HEAD_DIM])
                values.append(kv_recv[g][owner, :, HEAD_DIM:])
                valid.append(valid_tab[side * picks + pick] == 1)
            keys = jnp.concatenate(keys, axis=0)
            values = jnp.concatenate(values, axis=0)
            key_sum = None
            for chunk in range(group // pair):
                first = g * group + chunk * pair
                spots = [
                    slice((first + at) * HEAD_DIM, (first + at + 1) * HEAD_DIM)
                    for at in range(pair)
                ]
                query = jnp.concatenate([q_ref[here, spot] for spot in spots], axis=0)
                grad = jnp.concatenate([do_buf[here, spot] for spot in spots], axis=0)
                scores = dot(keys, query, 1, 1) * scale
                masked = [jnp.where(causal, scores[:span], HIDDEN)]
                for pick in range(picks):
                    piece = scores[(pick + 1) * span : (pick + 2) * span]
                    masked.append(jnp.where(valid[pick], piece, HIDDEN))
                scores = jnp.concatenate(masked, axis=0)
                top = jnp.max(scores, axis=0, keepdims=True)
                probs = jnp.exp(scores - top)
                total = jnp.sum(probs, axis=0, keepdims=True)
                probs = probs * (1.0 / total)
                weights = probs.astype(jnp.bfloat16)
                attended = dot(values, weights, 0, 0)
                slopes = dot(values, grad, 1, 1)
                delta = jnp.sum(probs * slopes, axis=0, keepdims=True)
                dscores = (probs * ((slopes - delta) * scale)).astype(jnp.bfloat16)
                query_grad = dot(keys, dscores, 0, 0)
                attended = attended.T.astype(jnp.bfloat16)
                query_grad = query_grad.T.astype(jnp.bfloat16)
                for at in range(pair):
                    att_buf[here, spots[at]] = attended[at * span : (at + 1) * span]
                    qg_ref[here, spots[at]] = query_grad[at * span : (at + 1) * span]
                key_part = dot(dscores, query, 1, 0)
                value_part = dot(weights, grad, 1, 0)
                if key_sum is None:
                    key_sum, value_sum = key_part, value_part
                else:
                    key_sum, value_sum = key_sum + key_part, value_sum + value_part
            own_acc[g, side, :, :HEAD_DIM] = key_sum[:span]
            own_acc[g, side, :, HEAD_DIM:] = value_sum[:span]
            for pick in range(picks):
                piece = slice((pick + 1) * span, (pick + 2) * span)
                parts[g, side * picks + pick, :, :HEAD_DIM] = key_sum[piece].astype(jnp.bfloat16)
                parts[g, side * picks + pick, :, HEAD_DIM:] = value_sum[piece].astype(jnp.bfloat16)
            return carry

        lax.fori_loop(0, 2, attend, 0)

        def send_grad(peer, g=g):
            spot = jnp.int32(0)
            found = jnp.int32(0)
            for at in range(2 * picks):
                hit = (owner_tab[at] == peer) & (valid_tab[at] == 1)
                spot = jnp.where(hit, at, spot)
                found = jnp.where(hit, 1, found)
            part = parts[g, spot]
            g_send[g, peer] = jnp.where(found == 1, part, jnp.zeros_like(part))
            through_other = peer_is_end(peer) & far(peer)
            only(jnp.logical_not(through_other), grad_copy(peer, me, g).start)
            if relay:
                slot = jnp.where(is_inner, 0, jnp.where(lax.rem(peer, 2) == y, 1, 2))
                here = is_inner & (peer == served)

                @pl.when(through_other & jnp.logical_not(here))
                def _():
                    collect_copy(peer, slot, g).start()

        over_seq(send_grad)
        over_head(lambda peer, g=g: att_copy(peer, hd, g).start())

    if relay:
        for g in range(kv_local):

            @pl.when(is_inner)
            def _(g=g):
                sums = [jnp.zeros((span, 2 * HEAD_DIM), jnp.float32)] * 2
                for at in range(4):
                    if at < 3:
                        collect_copy(served, at, g).wait_recv()
                        part = col_recv[g, at].astype(jnp.float32)
                    else:
                        part = g_send[g, served].astype(jnp.float32)
                    second = sel_tab[at] == 1
                    sums[0] = sums[0] + jnp.where(second, 0.0, part)
                    sums[1] = sums[1] + jnp.where(second, part, 0.0)
                for side in range(2):
                    comb_send[g, side] = sums[side].astype(jnp.bfloat16)
                combined_copy(g).start()

    leaving = [
        pltpu.make_async_copy(source, target, local_sem.at[at])
        for at, (source, target) in enumerate(
            (
                (
                    att_buf.at[pl.ds(pl.multiple_of(hd * rows, rows), rows), :],
                    att_ref.at[:, pl.ds(pl.multiple_of(hd * width, width), width)],
                ),
                (qg_ref, qg_out),
                (kg_ref, kg_out),
                (vg_ref, vg_out),
            )
        )
    ]
    leaving[0].start()
    leaving[1].start()

    for g in range(kv_local):
        cols = slice(g * HEAD_DIM, (g + 1) * HEAD_DIM)

        def add_grad(peer, g=g):
            def arrived():
                grad_copy(me, peer, g).wait_recv()
                part = g_recv[g, peer].astype(jnp.float32)
                second = half_tab[peer] == 1
                own_acc[g, 0] += jnp.where(second, 0.0, part)
                own_acc[g, 1] += jnp.where(second, part, 0.0)

            only(jnp.logical_not(is_end & far(peer)), arrived)

        over_seq(add_grad)
        if relay:

            @pl.when(is_end)
            def _(g=g):
                combined_copy(g).wait_recv()
                for side in range(2):
                    own_acc[g, side] += comb_recv[g, side].astype(jnp.float32)

        for side in range(2):
            here = slice(side * span, (side + 1) * span)
            kg_ref[here, cols] = own_acc[g, side, :, :HEAD_DIM].astype(jnp.bfloat16)
            vg_ref[here, cols] = own_acc[g, side, :, HEAD_DIM:].astype(jnp.bfloat16)

    leaving[2].start()
    leaving[3].start()
    last = kv_local - 1
    over_seq(
        lambda peer: only(
            jnp.logical_not(is_end & far(peer)), kv_copy(peer, me, last).wait_send
        )
    )
    if relay:
        pl.when(is_end)(full_copy(last).wait_send)
    over_head(lambda peer: cot_copy(peer, hd).wait_send())
    for g in range(kv_local):
        over_head(lambda peer, g=g: att_copy(hd, peer, g).wait_recv())
        over_head(lambda peer, g=g: att_copy(peer, hd, g).wait_send())
        over_seq(
            lambda peer, g=g: only(
                jnp.logical_not(is_inner & (peer == served)), grad_copy(peer, me, g).wait_send
            )
        )
        if relay:

            @pl.when(is_inner)
            def _(g=g):
                for at in range(3):
                    forward_copy(g, at).wait_send()
                combined_copy(g).wait_send()

    for copy in leaving:
        copy.wait()


def write_out(*refs):
    sources, targets, stages, sems = refs[:4], refs[4:8], refs[8:12], refs[12]
    arrive = [
        pltpu.make_async_copy(source, stage, sems.at[0, at])
        for at, (source, stage) in enumerate(zip(sources, stages))
    ]
    leave = [
        pltpu.make_async_copy(stage, target, sems.at[1, at])
        for at, (stage, target) in enumerate(zip(stages, targets))
    ]
    for copy in arrive:
        copy.start()
    for at in range(4):
        arrive[at].wait()
        leave[at].start()
    for copy in leave:
        copy.wait()


def body(queries, key_rows, value_rows, span_place, block_lists, cotangent):
    n = lax.axis_size("seq")
    heads = lax.axis_size("head")
    span = queries.shape[0] // 2
    picks = block_lists.shape[1]
    kv_local = key_rows.shape[1] // HEAD_DIM
    group = queries.shape[1] // key_rows.shape[1]
    bf16 = jnp.bfloat16
    hbm = pl.BlockSpec(memory_space=pltpu.HBM)
    smem = pl.BlockSpec(memory_space=pltpu.SMEM)
    box = (kv_local, n, span, 2 * HEAD_DIM)
    dma = pltpu.SemaphoreType.DMA
    flops = 6 * 2 * 2 * span * span * (picks + 1) * queries.shape[1]
    results = pl.pallas_call(
        functools.partial(kernel, (n, heads, span, picks, kv_local, group)),
        out_shape=[
            jax.ShapeDtypeStruct(cotangent.shape, bf16),
            jax.ShapeDtypeStruct(queries.shape, bf16),
            jax.ShapeDtypeStruct(key_rows.shape, bf16),
            jax.ShapeDtypeStruct(value_rows.shape, bf16),
        ],
        in_specs=[smem, smem, hbm, hbm, hbm, hbm],
        out_specs=[hbm] * 4,
        scratch_shapes=[
            pltpu.SMEM((n,), jnp.int32),
            pltpu.SMEM((2 * picks,), jnp.int32),
            pltpu.SMEM((2 * picks,), jnp.int32),
            pltpu.VMEM(queries.shape, bf16),
            pltpu.VMEM(key_rows.shape, bf16),
            pltpu.VMEM(value_rows.shape, bf16),
            pltpu.VMEM(queries.shape, bf16),
            pltpu.VMEM(key_rows.shape, bf16),
            pltpu.VMEM(value_rows.shape, bf16),
            pltpu.VMEM(queries.shape, bf16),
            pltpu.VMEM(queries.shape, bf16),
            pltpu.VMEM(box, bf16),
            [pltpu.VMEM(box[1:], bf16)] * kv_local,
            pltpu.VMEM(box, bf16),
            pltpu.VMEM(box, bf16),
            pltpu.VMEM((kv_local, 2 * picks, span, 2 * HEAD_DIM), bf16),
            pltpu.VMEM((kv_local, 2, span, 2 * HEAD_DIM), jnp.float32),
            dma((4,)),
            dma((heads,)),
            dma((heads,)),
            dma((kv_local, heads)),
            dma((kv_local, heads)),
            dma((kv_local, n)),
            dma((kv_local, n)),
            dma((kv_local, n)),
            dma((kv_local, n)),
            pltpu.SMEM((4,), jnp.int32),
            pltpu.VMEM((kv_local, 2 * span, 2 * HEAD_DIM), bf16),
            pltpu.VMEM((kv_local, 2 * span, 2 * HEAD_DIM), bf16),
            pltpu.VMEM((kv_local, 3, span, 2 * HEAD_DIM), bf16),
            pltpu.VMEM((kv_local, 3, span, 2 * HEAD_DIM), bf16),
            pltpu.VMEM((kv_local, 2, span, 2 * HEAD_DIM), bf16),
            pltpu.VMEM((kv_local, 2, span, 2 * HEAD_DIM), bf16),
            dma((2, kv_local)),
            dma((kv_local, 3)),
            dma((kv_local, 3)),
            dma((2, kv_local)),
        ],
        compiler_params=pltpu.CompilerParams(
            collective_id=0, has_side_effects=True, vmem_limit_bytes=VMEM_BYTES
        ),
        cost_estimate=pl.CostEstimate(
            flops=flops, bytes_accessed=4 * queries.size * 2, transcendentals=flops // 1536
        ),
    )(span_place, block_lists.T, queries, key_rows, value_rows, cotangent)
    return tuple(
        pl.pallas_call(
            write_out,
            out_shape=[jax.ShapeDtypeStruct(item.shape, item.dtype) for item in results],
            in_specs=[hbm] * 4,
            out_specs=[hbm] * 4,
            scratch_shapes=[pltpu.VMEM(item.shape, item.dtype) for item in results]
            + [dma((2, 4))],
            compiler_params=pltpu.CompilerParams(vmem_limit_bytes=VMEM_BYTES),
        )(*results)
    )


def solution(mesh):
    in_specs = (
        P("seq", "head"),
        P("seq", "head"),
        P("seq", "head"),
        P(),
        P(),
        P(("seq", "head"), None),
    )
    out_specs = (P(("seq", "head"), None), P("seq", "head"), P("seq", "head"), P("seq", "head"))
    return jax.shard_map(body, mesh=mesh, in_specs=in_specs, out_specs=out_specs, check_vma=False)
```

```python
import functools
import math

import jax
import jax.numpy as jnp
from jax import lax
from jax.experimental import pallas as pl
from jax.experimental.pallas import tpu as pltpu
from jax.sharding import PartitionSpec as P

HEAD_DIM = 128
HIDDEN = -1e30
VMEM_BYTES = 64 * 1024 * 1024


def dot(left, right, left_dim, right_dim):
    return lax.dot_general(
        left, right, (((left_dim,), (right_dim,)), ((), ())), preferred_element_type=jnp.float32
    )


def kernel(
    dims,
    place_ref,
    lists_ref,
    q_in,
    k_in,
    v_in,
    cot_ref,
    att_ref,
    qg_out,
    kg_out,
    vg_out,
    half_tab,
    owner_tab,
    valid_tab,
    q_ref,
    k_ref,
    v_ref,
    qg_ref,
    kg_ref,
    vg_ref,
    do_buf,
    att_buf,
    kv_send,
    kv_recv,
    g_send,
    g_recv,
    parts,
    own_acc,
    local_sem,
    cot_ssem,
    cot_rsem,
    att_ssem,
    att_rsem,
    kv_ssem,
    kv_rsem,
    g_ssem,
    g_rsem,
    sel_tab,
    full_send,
    full_recv,
    fwd_send,
    col_recv,
    comb_send,
    comb_recv,
    full_sem,
    fwd_sem,
    col_rsem,
    comb_sem,
):
    n, heads, span, picks, kv_local, group = dims
    me = lax.axis_index("seq")
    hd = lax.axis_index("head")
    rows = 2 * span // heads
    width = kv_local * group * HEAD_DIM
    gwidth = group * HEAD_DIM
    scale = 1.0 / math.sqrt(HEAD_DIM)

    relay = n == 8
    z, y = me // 2, lax.rem(me, 2)
    is_end = (z == 0) | (z == 3)
    is_inner = jnp.logical_not(is_end)
    via = jnp.where(z == 0, 4, 2) + y
    served = jnp.where(z == 2, 0, 6) + y
    far_end = jnp.where(z == 2, 6, 0)
    helped = (2 * z + 1 - y, far_end + y, far_end + 1 - y)

    def far(peer):
        apart = peer // 2 - z
        return (apart >= 2) | (apart <= -2)

    def peer_is_end(peer):
        return (peer // 2 == 0) | (peer // 2 == 3)

    def only(condition, action):
        if relay:
            pl.when(condition)(action)
        else:
            action()

    fetches = [
        pltpu.make_async_copy(source, target, local_sem.at[at])
        for at, (source, target) in enumerate(((k_in, k_ref), (v_in, v_ref), (q_in, q_ref)))
    ]
    fetches.append(
        pltpu.make_async_copy(
            cot_ref.at[:, pl.ds(pl.multiple_of(hd * width, width), width)],
            do_buf.at[pl.ds(pl.multiple_of(hd * rows, rows), rows), :],
            local_sem.at[3],
        )
    )
    for fetch in fetches:
        fetch.start()

    barrier = pltpu.get_barrier_semaphore()

    def greet_seq(step, carry):
        peer = lax.rem(me + step, n)
        pl.semaphore_signal(barrier, inc=1, device_id={"seq": peer})
        return carry

    def greet_head(step, carry):
        peer = lax.rem(hd + step, heads)
        pl.semaphore_signal(barrier, inc=1, device_id={"head": peer})
        return carry

    lax.fori_loop(1, n, greet_seq, 0)
    lax.fori_loop(1, heads, greet_head, 0)

    my_second = place_ref[2 * me + 1]

    def fill_half(peer, carry):
        wants = jnp.int32(0)
        for side in range(2):
            block = place_ref[2 * peer + side]
            for pick in range(picks):
                wants = jnp.where(lists_ref[pick, block] == my_second, 1, wants)
        half_tab[peer] = wants
        return carry

    lax.fori_loop(0, n, fill_half, 0)

    if relay:
        end_second = place_ref[2 * served + 1]
        for at, who in enumerate(helped + (me,)):
            wants = jnp.int32(0)
            for side in range(2):
                block = place_ref[2 * who + side]
                for pick in range(picks):
                    wants = jnp.where(lists_ref[pick, block] == end_second, 1, wants)
            sel_tab[at] = wants

    spare = lax.rem(me + 1, n)
    for side in range(2):
        own = place_ref[2 * me + side]
        blocks = [lists_ref[pick, own] for pick in range(picks)]
        for pick in range(picks):
            block = blocks[pick]
            valid = jnp.where(block != own, 1, 0)
            for before in range(pick):
                valid = jnp.where(block == blocks[before], 0, valid)

            def find(at, owner, block=block):
                hit = (place_ref[2 * at] == block) | (place_ref[2 * at + 1] == block)
                return jnp.where(hit, at, owner)

            owner = lax.fori_loop(0, n, find, jnp.int32(0))
            owner_tab[side * picks + pick] = jnp.where(valid == 1, owner, spare)
            valid_tab[side * picks + pick] = valid

    pl.semaphore_wait(barrier, n - 1 + heads - 1)

    def cot_copy(peer, slot):
        return pltpu.make_async_remote_copy(
            src_ref=cot_ref.at[:, pl.ds(pl.multiple_of(peer * width, width), width)],
            dst_ref=do_buf.at[pl.ds(pl.multiple_of(slot * rows, rows), rows), :],
            send_sem=cot_ssem.at[peer],
            recv_sem=cot_rsem.at[slot],
            device_id={"head": peer},
        )

    def att_copy(peer, slot, g):
        return pltpu.make_async_remote_copy(
            src_ref=att_buf.at[
                pl.ds(pl.multiple_of(peer * rows, rows), rows), pl.ds(g * gwidth, gwidth)
            ],
            dst_ref=att_ref.at[
                :, pl.ds(pl.multiple_of(slot * width + g * gwidth, gwidth), gwidth)
            ],
            send_sem=att_ssem.at[g, peer],
            recv_sem=att_rsem.at[g, slot],
            device_id={"head": peer},
        )

    def kv_copy(peer, slot, g):
        return pltpu.make_async_remote_copy(
            src_ref=kv_send.at[g, peer],
            dst_ref=kv_recv[g].at[slot],
            send_sem=kv_ssem.at[g, peer],
            recv_sem=kv_rsem.at[g, slot],
            device_id={"seq": peer},
        )

    def grad_copy(peer, slot, g):
        return pltpu.make_async_remote_copy(
            src_ref=g_send.at[g, peer],
            dst_ref=g_recv.at[g, slot],
            send_sem=g_ssem.at[g, peer],
            recv_sem=g_rsem.at[g, slot],
            device_id={"seq": peer},
        )

    def full_copy(g):
        return pltpu.make_async_remote_copy(
            src_ref=full_send.at[g],
            dst_ref=full_recv.at[g],
            send_sem=full_sem.at[0, g],
            recv_sem=full_sem.at[1, g],
            device_id={"seq": via},
        )

    def forward_copy(g, at):
        return pltpu.make_async_remote_copy(
            src_ref=fwd_send.at[g, at],
            dst_ref=kv_recv[g].at[served],
            send_sem=fwd_sem.at[g, at],
            recv_sem=kv_rsem.at[g, served],
            device_id={"seq": helped[at]},
        )

    def collect_copy(peer, slot, g):
        through = jnp.where(peer // 2 == 0, 4, 2) + lax.rem(peer, 2)
        return pltpu.make_async_remote_copy(
            src_ref=g_send.at[g, peer],
            dst_ref=col_recv.at[g, slot],
            send_sem=g_ssem.at[g, peer],
            recv_sem=col_rsem.at[g, slot],
            device_id={"seq": through},
        )

    def combined_copy(g):
        return pltpu.make_async_remote_copy(
            src_ref=comb_send.at[g],
            dst_ref=comb_recv.at[g],
            send_sem=comb_sem.at[0, g],
            recv_sem=comb_sem.at[1, g],
            device_id={"seq": served},
        )

    def over_seq(action):
        def one(step, carry):
            action(lax.rem(me + step, n))
            return carry

        lax.fori_loop(1, n, one, 0)

    def over_head(action):
        def one(step, carry):
            action(lax.rem(hd + step, heads))
            return carry

        lax.fori_loop(1, heads, one, 0)

    over_head(lambda peer: cot_copy(peer, hd).start())
    fetches[0].wait()
    fetches[1].wait()

    def send_keys(g):
        cols = slice(g * HEAD_DIM, (g + 1) * HEAD_DIM)
        if relay:

            @pl.when(is_end)
            def _():
                full_send[g, :, :HEAD_DIM] = k_ref[:, cols]
                full_send[g, :, HEAD_DIM:] = v_ref[:, cols]
                full_copy(g).start()

        def send_kv(peer):
            second = half_tab[peer] == 1
            kv_send[g, peer, :, :HEAD_DIM] = jnp.where(second, k_ref[span:, cols], k_ref[:span, cols])
            kv_send[g, peer, :, HEAD_DIM:] = jnp.where(second, v_ref[span:, cols], v_ref[:span, cols])

            only(jnp.logical_not(is_end & far(peer)), kv_copy(peer, me, g).start)

        over_seq(send_kv)

    def relay_keys(g):
        if relay:

            @pl.when(is_inner)
            def _():
                full_copy(g).wait_recv()
                for at in range(4):
                    second = sel_tab[at] == 1
                    block = jnp.where(second, full_recv[g, span:], full_recv[g, :span])
                    if at < 3:
                        fwd_send[g, at] = block
                        forward_copy(g, at).start()
                    else:
                        kv_recv[g][served] = block

    for g in range(kv_local):
        send_keys(g)
    relay_keys(0)
    fetches[2].wait()
    fetches[3].wait()
    over_head(lambda peer: cot_copy(hd, peer).wait_recv())

    pair = 2
    lanes = pair * span
    key_at = lax.broadcasted_iota(jnp.int32, (span, lanes), 0)
    query_at = lax.rem(lax.broadcasted_iota(jnp.int32, (span, lanes), 1), span)
    causal = key_at <= query_at

    for g in range(kv_local):
        cols = slice(g * HEAD_DIM, (g + 1) * HEAD_DIM)
        if g > 0:
            relay_keys(g)
        over_seq(
            lambda peer, g=g: only(
                jnp.logical_not(is_inner & (peer == served)), kv_copy(me, peer, g).wait_recv
            )
        )

        def attend(side, carry, g=g, cols=cols):
            base = pl.multiple_of(side * span, span)
            here = pl.ds(base, span)
            keys = [k_ref[here, cols]]
            values = [v_ref[here, cols]]
            valid = []
            for pick in range(picks):
                owner = owner_tab[side * picks + pick]
                keys.append(kv_recv[g][owner, :, :HEAD_DIM])
                values.append(kv_recv[g][owner, :, HEAD_DIM:])
                valid.append(valid_tab[side * picks + pick] == 1)
            keys = jnp.concatenate(keys, axis=0)
            values = jnp.concatenate(values, axis=0)
            key_sum = None
            for chunk in range(group // pair):
                first = g * group + chunk * pair
                spots = [
                    slice((first + at) * HEAD_DIM, (first + at + 1) * HEAD_DIM)
                    for at in range(pair)
                ]
                query = jnp.concatenate([q_ref[here, spot] for spot in spots], axis=0)
                grad = jnp.concatenate([do_buf[here, spot] for spot in spots], axis=0)
                scores = dot(keys, query, 1, 1) * scale
                masked = [jnp.where(causal, scores[:span], HIDDEN)]
                for pick in range(picks):
                    piece = scores[(pick + 1) * span : (pick + 2) * span]
                    masked.append(jnp.where(valid[pick], piece, HIDDEN))
                scores = jnp.concatenate(masked, axis=0)
                top = jnp.max(scores, axis=0, keepdims=True)
                probs = jnp.exp(scores - top)
                total = jnp.sum(probs, axis=0, keepdims=True)
                probs = probs * (1.0 / total)
                weights = probs.astype(jnp.bfloat16)
                attended = dot(values, weights, 0, 0)
                slopes = dot(values, grad, 1, 1)
                delta = jnp.sum(probs * slopes, axis=0, keepdims=True)
                dscores = (probs * ((slopes - delta) * scale)).astype(jnp.bfloat16)
                query_grad = dot(keys, dscores, 0, 0)
                attended = attended.T.astype(jnp.bfloat16)
                query_grad = query_grad.T.astype(jnp.bfloat16)
                for at in range(pair):
                    att_buf[here, spots[at]] = attended[at * span : (at + 1) * span]
                    qg_ref[here, spots[at]] = query_grad[at * span : (at + 1) * span]
                key_part = dot(dscores, query, 1, 0)
                value_part = dot(weights, grad, 1, 0)
                if key_sum is None:
                    key_sum, value_sum = key_part, value_part
                else:
                    key_sum, value_sum = key_sum + key_part, value_sum + value_part
            own_acc[g, side, :, :HEAD_DIM] = key_sum[:span]
            own_acc[g, side, :, HEAD_DIM:] = value_sum[:span]
            for pick in range(picks):
                piece = slice((pick + 1) * span, (pick + 2) * span)
                parts[g, side * picks + pick, :, :HEAD_DIM] = key_sum[piece].astype(jnp.bfloat16)
                parts[g, side * picks + pick, :, HEAD_DIM:] = value_sum[piece].astype(jnp.bfloat16)
            return carry

        lax.fori_loop(0, 2, attend, 0)

        def stage_grad(peer, g=g):
            spot = jnp.int32(0)
            found = jnp.int32(0)
            for at in range(2 * picks):
                hit = (owner_tab[at] == peer) & (valid_tab[at] == 1)
                spot = jnp.where(hit, at, spot)
                found = jnp.where(hit, 1, found)
            part = parts[g, spot]
            g_send[g, peer] = jnp.where(found == 1, part, jnp.zeros_like(part))

        def send_through(peer, g=g):
            @pl.when(peer_is_end(peer) & far(peer))
            def _():
                stage_grad(peer)
                slot = jnp.where(is_inner, 0, jnp.where(lax.rem(peer, 2) == y, 1, 2))

                @pl.when(jnp.logical_not(is_inner & (peer == served)))
                def _():
                    collect_copy(peer, slot, g).start()

        def send_direct(peer, g=g):
            def go():
                stage_grad(peer)
                grad_copy(peer, me, g).start()

            only(jnp.logical_not(peer_is_end(peer) & far(peer)), go)

        if relay:
            over_seq(send_through)
        over_seq(send_direct)
        over_head(lambda peer, g=g: att_copy(peer, hd, g).start())

    if relay:
        for g in range(kv_local):

            @pl.when(is_inner)
            def _(g=g):
                sums = [jnp.zeros((span, 2 * HEAD_DIM), jnp.float32)] * 2
                for at in range(4):
                    if at < 3:
                        collect_copy(served, at, g).wait_recv()
                        part = col_recv[g, at].astype(jnp.float32)
                    else:
                        part = g_send[g, served].astype(jnp.float32)
                    second = sel_tab[at] == 1
                    sums[0] = sums[0] + jnp.where(second, 0.0, part)
                    sums[1] = sums[1] + jnp.where(second, part, 0.0)
                for side in range(2):
                    comb_send[g, side] = sums[side].astype(jnp.bfloat16)
                combined_copy(g).start()

    leaving = [
        pltpu.make_async_copy(source, target, local_sem.at[at])
        for at, (source, target) in enumerate(
            (
                (
                    att_buf.at[pl.ds(pl.multiple_of(hd * rows, rows), rows), :],
                    att_ref.at[:, pl.ds(pl.multiple_of(hd * width, width), width)],
                ),
                (qg_ref, qg_out),
                (kg_ref, kg_out),
                (vg_ref, vg_out),
            )
        )
    ]
    leaving[0].start()
    leaving[1].start()

    for g in range(kv_local):
        cols = slice(g * HEAD_DIM, (g + 1) * HEAD_DIM)

        def add_grad(peer, g=g):
            def arrived():
                grad_copy(me, peer, g).wait_recv()
                part = g_recv[g, peer].astype(jnp.float32)
                second = half_tab[peer] == 1
                own_acc[g, 0] += jnp.where(second, 0.0, part)
                own_acc[g, 1] += jnp.where(second, part, 0.0)

            only(jnp.logical_not(is_end & far(peer)), arrived)

        over_seq(add_grad)
        if relay:

            @pl.when(is_end)
            def _(g=g):
                combined_copy(g).wait_recv()
                for side in range(2):
                    own_acc[g, side] += comb_recv[g, side].astype(jnp.float32)

        for side in range(2):
            here = slice(side * span, (side + 1) * span)
            kg_ref[here, cols] = own_acc[g, side, :, :HEAD_DIM].astype(jnp.bfloat16)
            vg_ref[here, cols] = own_acc[g, side, :, HEAD_DIM:].astype(jnp.bfloat16)

    leaving[2].start()
    leaving[3].start()
    over_head(lambda peer: cot_copy(peer, hd).wait_send())
    for g in range(kv_local):
        over_head(lambda peer, g=g: att_copy(hd, peer, g).wait_recv())
        over_head(lambda peer, g=g: att_copy(peer, hd, g).wait_send())
        over_seq(
            lambda peer, g=g: only(
                jnp.logical_not(is_end & far(peer)), kv_copy(peer, me, g).wait_send
            )
        )
        over_seq(
            lambda peer, g=g: only(
                jnp.logical_not(is_inner & (peer == served)), grad_copy(peer, me, g).wait_send
            )
        )
        if relay:

            pl.when(is_end)(full_copy(g).wait_send)

            @pl.when(is_inner)
            def _(g=g):
                for at in range(3):
                    forward_copy(g, at).wait_send()
                combined_copy(g).wait_send()

    for copy in leaving:
        copy.wait()


def write_out(*refs):
    sources, targets, stages, sems = refs[:4], refs[4:8], refs[8:12], refs[12]
    arrive = [
        pltpu.make_async_copy(source, stage, sems.at[0, at])
        for at, (source, stage) in enumerate(zip(sources, stages))
    ]
    leave = [
        pltpu.make_async_copy(stage, target, sems.at[1, at])
        for at, (stage, target) in enumerate(zip(stages, targets))
    ]
    for copy in arrive:
        copy.start()
    for at in range(4):
        arrive[at].wait()
        leave[at].start()
    for copy in leave:
        copy.wait()


def body(queries, key_rows, value_rows, span_place, block_lists, cotangent):
    n = lax.axis_size("seq")
    heads = lax.axis_size("head")
    span = queries.shape[0] // 2
    picks = block_lists.shape[1]
    kv_local = key_rows.shape[1] // HEAD_DIM
    group = queries.shape[1] // key_rows.shape[1]
    bf16 = jnp.bfloat16
    hbm = pl.BlockSpec(memory_space=pltpu.HBM)
    smem = pl.BlockSpec(memory_space=pltpu.SMEM)
    box = (kv_local, n, span, 2 * HEAD_DIM)
    dma = pltpu.SemaphoreType.DMA
    flops = 6 * 2 * 2 * span * span * (picks + 1) * queries.shape[1]
    results = pl.pallas_call(
        functools.partial(kernel, (n, heads, span, picks, kv_local, group)),
        out_shape=[
            jax.ShapeDtypeStruct(cotangent.shape, bf16),
            jax.ShapeDtypeStruct(queries.shape, bf16),
            jax.ShapeDtypeStruct(key_rows.shape, bf16),
            jax.ShapeDtypeStruct(value_rows.shape, bf16),
        ],
        in_specs=[smem, smem, hbm, hbm, hbm, hbm],
        out_specs=[hbm] * 4,
        scratch_shapes=[
            pltpu.SMEM((n,), jnp.int32),
            pltpu.SMEM((2 * picks,), jnp.int32),
            pltpu.SMEM((2 * picks,), jnp.int32),
            pltpu.VMEM(queries.shape, bf16),
            pltpu.VMEM(key_rows.shape, bf16),
            pltpu.VMEM(value_rows.shape, bf16),
            pltpu.VMEM(queries.shape, bf16),
            pltpu.VMEM(key_rows.shape, bf16),
            pltpu.VMEM(value_rows.shape, bf16),
            pltpu.VMEM(queries.shape, bf16),
            pltpu.VMEM(queries.shape, bf16),
            pltpu.VMEM(box, bf16),
            [pltpu.VMEM(box[1:], bf16)] * kv_local,
            pltpu.VMEM(box, bf16),
            pltpu.VMEM(box, bf16),
            pltpu.VMEM((kv_local, 2 * picks, span, 2 * HEAD_DIM), bf16),
            pltpu.VMEM((kv_local, 2, span, 2 * HEAD_DIM), jnp.float32),
            dma((4,)),
            dma((heads,)),
            dma((heads,)),
            dma((kv_local, heads)),
            dma((kv_local, heads)),
            dma((kv_local, n)),
            dma((kv_local, n)),
            dma((kv_local, n)),
            dma((kv_local, n)),
            pltpu.SMEM((4,), jnp.int32),
            pltpu.VMEM((kv_local, 2 * span, 2 * HEAD_DIM), bf16),
            pltpu.VMEM((kv_local, 2 * span, 2 * HEAD_DIM), bf16),
            pltpu.VMEM((kv_local, 3, span, 2 * HEAD_DIM), bf16),
            pltpu.VMEM((kv_local, 3, span, 2 * HEAD_DIM), bf16),
            pltpu.VMEM((kv_local, 2, span, 2 * HEAD_DIM), bf16),
            pltpu.VMEM((kv_local, 2, span, 2 * HEAD_DIM), bf16),
            dma((2, kv_local)),
            dma((kv_local, 3)),
            dma((kv_local, 3)),
            dma((2, kv_local)),
        ],
        compiler_params=pltpu.CompilerParams(
            collective_id=0, has_side_effects=True, vmem_limit_bytes=VMEM_BYTES
        ),
        cost_estimate=pl.CostEstimate(
            flops=flops, bytes_accessed=4 * queries.size * 2, transcendentals=flops // 1536
        ),
    )(span_place, block_lists.T, queries, key_rows, value_rows, cotangent)
    return tuple(
        pl.pallas_call(
            write_out,
            out_shape=[jax.ShapeDtypeStruct(item.shape, item.dtype) for item in results],
            in_specs=[hbm] * 4,
            out_specs=[hbm] * 4,
            scratch_shapes=[pltpu.VMEM(item.shape, item.dtype) for item in results]
            + [dma((2, 4))],
            compiler_params=pltpu.CompilerParams(vmem_limit_bytes=VMEM_BYTES),
        )(*results)
    )


def solution(mesh):
    in_specs = (
        P("seq", "head"),
        P("seq", "head"),
        P("seq", "head"),
        P(),
        P(),
        P(("seq", "head"), None),
    )
    out_specs = (P(("seq", "head"), None), P("seq", "head"), P("seq", "head"), P("seq", "head"))
    return jax.shard_map(body, mesh=mesh, in_specs=in_specs, out_specs=out_specs, check_vma=False)
```

```python
import functools
import math

import jax
import jax.numpy as jnp
from jax import lax
from jax.experimental import pallas as pl
from jax.experimental.pallas import tpu as pltpu
from jax.sharding import PartitionSpec as P

HEAD_DIM = 128
HIDDEN = -1e30
VMEM_BYTES = 64 * 1024 * 1024


def dot(left, right, left_dim, right_dim):
    return lax.dot_general(
        left, right, (((left_dim,), (right_dim,)), ((), ())), preferred_element_type=jnp.float32
    )


def kernel(
    dims,
    place_ref,
    lists_ref,
    q_in,
    k_in,
    v_in,
    cot_ref,
    att_ref,
    qg_out,
    kg_out,
    vg_out,
    half_tab,
    owner_tab,
    valid_tab,
    q_ref,
    k_ref,
    v_ref,
    qg_ref,
    kg_ref,
    vg_ref,
    do_buf,
    att_buf,
    kv_send,
    kv_recv,
    g_send,
    g_recv,
    parts,
    own_acc,
    local_sem,
    cot_ssem,
    cot_rsem,
    att_ssem,
    att_rsem,
    kv_ssem,
    kv_rsem,
    g_ssem,
    g_rsem,
    sel_tab,
    full_send,
    full_recv,
    fwd_send,
    col_recv,
    comb_send,
    comb_recv,
    full_sem,
    fwd_sem,
    col_rsem,
    comb_sem,
):
    n, heads, span, picks, kv_local, group = dims
    me = lax.axis_index("seq")
    hd = lax.axis_index("head")
    rows = 2 * span // heads
    width = kv_local * group * HEAD_DIM
    gwidth = group * HEAD_DIM
    scale = 1.0 / math.sqrt(HEAD_DIM)

    relay = n == 8
    z, y = me // 2, lax.rem(me, 2)
    is_end = (z == 0) | (z == 3)
    is_inner = jnp.logical_not(is_end)
    via = jnp.where(z == 0, 4, 2) + y
    served = jnp.where(z == 2, 0, 6) + y
    far_end = jnp.where(z == 2, 6, 0)
    helped = (2 * z + 1 - y, far_end + y, far_end + 1 - y)

    def far(peer):
        apart = peer // 2 - z
        return (apart >= 2) | (apart <= -2)

    def peer_is_end(peer):
        return (peer // 2 == 0) | (peer // 2 == 3)

    def only(condition, action):
        if relay:
            pl.when(condition)(action)
        else:
            action()

    fetches = [
        pltpu.make_async_copy(source, target, local_sem.at[at])
        for at, (source, target) in enumerate(((k_in, k_ref), (v_in, v_ref), (q_in, q_ref)))
    ]
    fetches.append(
        pltpu.make_async_copy(
            cot_ref.at[:, pl.ds(pl.multiple_of(hd * width, width), width)],
            do_buf.at[pl.ds(pl.multiple_of(hd * rows, rows), rows), :],
            local_sem.at[3],
        )
    )
    for fetch in fetches:
        fetch.start()

    barrier = pltpu.get_barrier_semaphore()

    def greet_seq(step, carry):
        peer = lax.rem(me + step, n)
        pl.semaphore_signal(barrier, inc=1, device_id={"seq": peer})
        return carry

    def greet_head(step, carry):
        peer = lax.rem(hd + step, heads)
        pl.semaphore_signal(barrier, inc=1, device_id={"head": peer})
        return carry

    lax.fori_loop(1, n, greet_seq, 0)
    lax.fori_loop(1, heads, greet_head, 0)

    my_second = place_ref[2 * me + 1]

    def fill_half(peer, carry):
        wants = jnp.int32(0)
        for side in range(2):
            block = place_ref[2 * peer + side]
            for pick in range(picks):
                wants = jnp.where(lists_ref[pick, block] == my_second, 1, wants)
        half_tab[peer] = wants
        return carry

    lax.fori_loop(0, n, fill_half, 0)

    if relay:
        end_second = place_ref[2 * served + 1]
        for at, who in enumerate(helped + (me,)):
            wants = jnp.int32(0)
            for side in range(2):
                block = place_ref[2 * who + side]
                for pick in range(picks):
                    wants = jnp.where(lists_ref[pick, block] == end_second, 1, wants)
            sel_tab[at] = wants

    spare = lax.rem(me + 1, n)
    for side in range(2):
        own = place_ref[2 * me + side]
        blocks = [lists_ref[pick, own] for pick in range(picks)]
        for pick in range(picks):
            block = blocks[pick]
            valid = jnp.where(block != own, 1, 0)
            for before in range(pick):
                valid = jnp.where(block == blocks[before], 0, valid)

            def find(at, owner, block=block):
                hit = (place_ref[2 * at] == block) | (place_ref[2 * at + 1] == block)
                return jnp.where(hit, at, owner)

            owner = lax.fori_loop(0, n, find, jnp.int32(0))
            owner_tab[side * picks + pick] = jnp.where(valid == 1, owner, spare)
            valid_tab[side * picks + pick] = valid

    pl.semaphore_wait(barrier, n - 1 + heads - 1)

    def cot_copy(peer, slot):
        return pltpu.make_async_remote_copy(
            src_ref=cot_ref.at[:, pl.ds(pl.multiple_of(peer * width, width), width)],
            dst_ref=do_buf.at[pl.ds(pl.multiple_of(slot * rows, rows), rows), :],
            send_sem=cot_ssem.at[peer],
            recv_sem=cot_rsem.at[slot],
            device_id={"head": peer},
        )

    def att_copy(peer, slot, g):
        return pltpu.make_async_remote_copy(
            src_ref=att_buf.at[
                pl.ds(pl.multiple_of(peer * rows, rows), rows), pl.ds(g * gwidth, gwidth)
            ],
            dst_ref=att_ref.at[
                :, pl.ds(pl.multiple_of(slot * width + g * gwidth, gwidth), gwidth)
            ],
            send_sem=att_ssem.at[g, peer],
            recv_sem=att_rsem.at[g, slot],
            device_id={"head": peer},
        )

    def kv_copy(peer, slot, g):
        return pltpu.make_async_remote_copy(
            src_ref=kv_send.at[g, peer],
            dst_ref=kv_recv[g].at[slot],
            send_sem=kv_ssem.at[g, peer],
            recv_sem=kv_rsem.at[g, slot],
            device_id={"seq": peer},
        )

    def grad_copy(peer, slot, g):
        return pltpu.make_async_remote_copy(
            src_ref=g_send.at[g, peer],
            dst_ref=g_recv.at[g, slot],
            send_sem=g_ssem.at[g, peer],
            recv_sem=g_rsem.at[g, slot],
            device_id={"seq": peer},
        )

    def full_copy(g):
        return pltpu.make_async_remote_copy(
            src_ref=full_send.at[g],
            dst_ref=full_recv.at[g],
            send_sem=full_sem.at[0, g],
            recv_sem=full_sem.at[1, g],
            device_id={"seq": via},
        )

    def forward_copy(g, at):
        return pltpu.make_async_remote_copy(
            src_ref=fwd_send.at[g, at],
            dst_ref=kv_recv[g].at[served],
            send_sem=fwd_sem.at[g, at],
            recv_sem=kv_rsem.at[g, served],
            device_id={"seq": helped[at]},
        )

    def collect_copy(peer, slot, g):
        through = jnp.where(peer // 2 == 0, 4, 2) + lax.rem(peer, 2)
        return pltpu.make_async_remote_copy(
            src_ref=g_send.at[g, peer],
            dst_ref=col_recv.at[g, slot],
            send_sem=g_ssem.at[g, peer],
            recv_sem=col_rsem.at[g, slot],
            device_id={"seq": through},
        )

    def combined_copy(g):
        return pltpu.make_async_remote_copy(
            src_ref=comb_send.at[g],
            dst_ref=comb_recv.at[g],
            send_sem=comb_sem.at[0, g],
            recv_sem=comb_sem.at[1, g],
            device_id={"seq": served},
        )

    def over_seq(action):
        def one(step, carry):
            action(lax.rem(me + step, n))
            return carry

        lax.fori_loop(1, n, one, 0)

    def over_head(action):
        def one(step, carry):
            action(lax.rem(hd + step, heads))
            return carry

        lax.fori_loop(1, heads, one, 0)

    over_head(lambda peer: cot_copy(peer, hd).start())
    fetches[0].wait()
    fetches[1].wait()

    def send_full(g):
        cols = slice(g * HEAD_DIM, (g + 1) * HEAD_DIM)
        if relay:

            @pl.when(is_end)
            def _():
                full_send[g, :, :HEAD_DIM] = k_ref[:, cols]
                full_send[g, :, HEAD_DIM:] = v_ref[:, cols]
                full_copy(g).start()

    def send_keys(g):
        cols = slice(g * HEAD_DIM, (g + 1) * HEAD_DIM)

        def send_kv(peer):
            second = half_tab[peer] == 1
            kv_send[g, peer, :, :HEAD_DIM] = jnp.where(second, k_ref[span:, cols], k_ref[:span, cols])
            kv_send[g, peer, :, HEAD_DIM:] = jnp.where(second, v_ref[span:, cols], v_ref[:span, cols])

            only(jnp.logical_not(is_end & far(peer)), kv_copy(peer, me, g).start)

        over_seq(send_kv)

    def relay_keys(g):
        if relay:

            @pl.when(is_inner)
            def _():
                full_copy(g).wait_recv()
                for at in range(4):
                    second = sel_tab[at] == 1
                    block = jnp.where(second, full_recv[g, span:], full_recv[g, :span])
                    if at < 3:
                        fwd_send[g, at] = block
                        forward_copy(g, at).start()
                    else:
                        kv_recv[g][served] = block

    for g in range(kv_local):
        send_full(g)
    for g in range(kv_local):
        send_keys(g)
    for g in range(kv_local):
        relay_keys(g)
    fetches[2].wait()
    fetches[3].wait()
    over_head(lambda peer: cot_copy(hd, peer).wait_recv())

    pair = 2
    lanes = pair * span
    key_at = lax.broadcasted_iota(jnp.int32, (span, lanes), 0)
    query_at = lax.rem(lax.broadcasted_iota(jnp.int32, (span, lanes), 1), span)
    causal = key_at <= query_at

    for g in range(kv_local):
        cols = slice(g * HEAD_DIM, (g + 1) * HEAD_DIM)
        over_seq(
            lambda peer, g=g: only(
                jnp.logical_not(is_inner & (peer == served)), kv_copy(me, peer, g).wait_recv
            )
        )

        def attend(side, carry, g=g, cols=cols):
            base = pl.multiple_of(side * span, span)
            here = pl.ds(base, span)
            keys = [k_ref[here, cols]]
            values = [v_ref[here, cols]]
            valid = []
            for pick in range(picks):
                owner = owner_tab[side * picks + pick]
                keys.append(kv_recv[g][owner, :, :HEAD_DIM])
                values.append(kv_recv[g][owner, :, HEAD_DIM:])
                valid.append(valid_tab[side * picks + pick] == 1)
            keys = jnp.concatenate(keys, axis=0)
            values = jnp.concatenate(values, axis=0)
            key_sum = None
            for chunk in range(group // pair):
                first = g * group + chunk * pair
                spots = [
                    slice((first + at) * HEAD_DIM, (first + at + 1) * HEAD_DIM)
                    for at in range(pair)
                ]
                query = jnp.concatenate([q_ref[here, spot] for spot in spots], axis=0)
                grad = jnp.concatenate([do_buf[here, spot] for spot in spots], axis=0)
                scores = dot(keys, query, 1, 1) * scale
                masked = [jnp.where(causal, scores[:span], HIDDEN)]
                for pick in range(picks):
                    piece = scores[(pick + 1) * span : (pick + 2) * span]
                    masked.append(jnp.where(valid[pick], piece, HIDDEN))
                scores = jnp.concatenate(masked, axis=0)
                top = jnp.max(scores, axis=0, keepdims=True)
                probs = jnp.exp(scores - top)
                total = jnp.sum(probs, axis=0, keepdims=True)
                probs = probs * (1.0 / total)
                weights = probs.astype(jnp.bfloat16)
                attended = dot(values, weights, 0, 0)
                slopes = dot(values, grad, 1, 1)
                delta = jnp.sum(probs * slopes, axis=0, keepdims=True)
                dscores = (probs * ((slopes - delta) * scale)).astype(jnp.bfloat16)
                query_grad = dot(keys, dscores, 0, 0)
                attended = attended.T.astype(jnp.bfloat16)
                query_grad = query_grad.T.astype(jnp.bfloat16)
                for at in range(pair):
                    att_buf[here, spots[at]] = attended[at * span : (at + 1) * span]
                    qg_ref[here, spots[at]] = query_grad[at * span : (at + 1) * span]
                key_part = dot(dscores, query, 1, 0)
                value_part = dot(weights, grad, 1, 0)
                if key_sum is None:
                    key_sum, value_sum = key_part, value_part
                else:
                    key_sum, value_sum = key_sum + key_part, value_sum + value_part
            own_acc[g, side, :, :HEAD_DIM] = key_sum[:span]
            own_acc[g, side, :, HEAD_DIM:] = value_sum[:span]
            for pick in range(picks):
                piece = slice((pick + 1) * span, (pick + 2) * span)
                parts[g, side * picks + pick, :, :HEAD_DIM] = key_sum[piece].astype(jnp.bfloat16)
                parts[g, side * picks + pick, :, HEAD_DIM:] = value_sum[piece].astype(jnp.bfloat16)
            return carry

        lax.fori_loop(0, 2, attend, 0)

        def stage_grad(peer, g=g):
            spot = jnp.int32(0)
            found = jnp.int32(0)
            for at in range(2 * picks):
                hit = (owner_tab[at] == peer) & (valid_tab[at] == 1)
                spot = jnp.where(hit, at, spot)
                found = jnp.where(hit, 1, found)
            part = parts[g, spot]
            g_send[g, peer] = jnp.where(found == 1, part, jnp.zeros_like(part))

        def send_through(peer, g=g):
            @pl.when(peer_is_end(peer) & far(peer))
            def _():
                stage_grad(peer)
                slot = jnp.where(is_inner, 0, jnp.where(lax.rem(peer, 2) == y, 1, 2))

                @pl.when(jnp.logical_not(is_inner & (peer == served)))
                def _():
                    collect_copy(peer, slot, g).start()

        def send_direct(peer, g=g):
            def go():
                stage_grad(peer)
                grad_copy(peer, me, g).start()

            only(jnp.logical_not(peer_is_end(peer) & far(peer)), go)

        if relay:
            over_seq(send_through)
        over_seq(send_direct)
        over_head(lambda peer, g=g: att_copy(peer, hd, g).start())

    if relay:
        for g in range(kv_local):

            @pl.when(is_inner)
            def _(g=g):
                sums = [jnp.zeros((span, 2 * HEAD_DIM), jnp.float32)] * 2
                for at in range(4):
                    if at < 3:
                        collect_copy(served, at, g).wait_recv()
                        part = col_recv[g, at].astype(jnp.float32)
                    else:
                        part = g_send[g, served].astype(jnp.float32)
                    second = sel_tab[at] == 1
                    sums[0] = sums[0] + jnp.where(second, 0.0, part)
                    sums[1] = sums[1] + jnp.where(second, part, 0.0)
                for side in range(2):
                    comb_send[g, side] = sums[side].astype(jnp.bfloat16)
                combined_copy(g).start()

    leaving = [
        pltpu.make_async_copy(source, target, local_sem.at[at])
        for at, (source, target) in enumerate(
            (
                (
                    att_buf.at[pl.ds(pl.multiple_of(hd * rows, rows), rows), :],
                    att_ref.at[:, pl.ds(pl.multiple_of(hd * width, width), width)],
                ),
                (qg_ref, qg_out),
                (kg_ref, kg_out),
                (vg_ref, vg_out),
            )
        )
    ]
    leaving[0].start()
    leaving[1].start()

    for g in range(kv_local):
        cols = slice(g * HEAD_DIM, (g + 1) * HEAD_DIM)

        def add_grad(peer, g=g):
            def arrived():
                grad_copy(me, peer, g).wait_recv()
                part = g_recv[g, peer].astype(jnp.float32)
                second = half_tab[peer] == 1
                own_acc[g, 0] += jnp.where(second, 0.0, part)
                own_acc[g, 1] += jnp.where(second, part, 0.0)

            only(jnp.logical_not(is_end & far(peer)), arrived)

        over_seq(add_grad)
        if relay:

            @pl.when(is_end)
            def _(g=g):
                combined_copy(g).wait_recv()
                for side in range(2):
                    own_acc[g, side] += comb_recv[g, side].astype(jnp.float32)

        for side in range(2):
            here = slice(side * span, (side + 1) * span)
            kg_ref[here, cols] = own_acc[g, side, :, :HEAD_DIM].astype(jnp.bfloat16)
            vg_ref[here, cols] = own_acc[g, side, :, HEAD_DIM:].astype(jnp.bfloat16)

    leaving[2].start()
    leaving[3].start()
    over_head(lambda peer: cot_copy(peer, hd).wait_send())
    for g in range(kv_local):
        over_head(lambda peer, g=g: att_copy(hd, peer, g).wait_recv())
        over_head(lambda peer, g=g: att_copy(peer, hd, g).wait_send())
        over_seq(
            lambda peer, g=g: only(
                jnp.logical_not(is_end & far(peer)), kv_copy(peer, me, g).wait_send
            )
        )
        over_seq(
            lambda peer, g=g: only(
                jnp.logical_not(is_inner & (peer == served)), grad_copy(peer, me, g).wait_send
            )
        )
        if relay:

            pl.when(is_end)(full_copy(g).wait_send)

            @pl.when(is_inner)
            def _(g=g):
                for at in range(3):
                    forward_copy(g, at).wait_send()
                combined_copy(g).wait_send()

    for copy in leaving:
        copy.wait()


def write_out(*refs):
    sources, targets, stages, sems = refs[:4], refs[4:8], refs[8:12], refs[12]
    arrive = [
        pltpu.make_async_copy(source, stage, sems.at[0, at])
        for at, (source, stage) in enumerate(zip(sources, stages))
    ]
    leave = [
        pltpu.make_async_copy(stage, target, sems.at[1, at])
        for at, (stage, target) in enumerate(zip(stages, targets))
    ]
    for copy in arrive:
        copy.start()
    for at in range(4):
        arrive[at].wait()
        leave[at].start()
    for copy in leave:
        copy.wait()


def body(queries, key_rows, value_rows, span_place, block_lists, cotangent):
    n = lax.axis_size("seq")
    heads = lax.axis_size("head")
    span = queries.shape[0] // 2
    picks = block_lists.shape[1]
    kv_local = key_rows.shape[1] // HEAD_DIM
    group = queries.shape[1] // key_rows.shape[1]
    bf16 = jnp.bfloat16
    hbm = pl.BlockSpec(memory_space=pltpu.HBM)
    smem = pl.BlockSpec(memory_space=pltpu.SMEM)
    box = (kv_local, n, span, 2 * HEAD_DIM)
    dma = pltpu.SemaphoreType.DMA
    flops = 6 * 2 * 2 * span * span * (picks + 1) * queries.shape[1]
    results = pl.pallas_call(
        functools.partial(kernel, (n, heads, span, picks, kv_local, group)),
        out_shape=[
            jax.ShapeDtypeStruct(cotangent.shape, bf16),
            jax.ShapeDtypeStruct(queries.shape, bf16),
            jax.ShapeDtypeStruct(key_rows.shape, bf16),
            jax.ShapeDtypeStruct(value_rows.shape, bf16),
        ],
        in_specs=[smem, smem, hbm, hbm, hbm, hbm],
        out_specs=[hbm] * 4,
        scratch_shapes=[
            pltpu.SMEM((n,), jnp.int32),
            pltpu.SMEM((2 * picks,), jnp.int32),
            pltpu.SMEM((2 * picks,), jnp.int32),
            pltpu.VMEM(queries.shape, bf16),
            pltpu.VMEM(key_rows.shape, bf16),
            pltpu.VMEM(value_rows.shape, bf16),
            pltpu.VMEM(queries.shape, bf16),
            pltpu.VMEM(key_rows.shape, bf16),
            pltpu.VMEM(value_rows.shape, bf16),
            pltpu.VMEM(queries.shape, bf16),
            pltpu.VMEM(queries.shape, bf16),
            pltpu.VMEM(box, bf16),
            [pltpu.VMEM(box[1:], bf16)] * kv_local,
            pltpu.VMEM(box, bf16),
            pltpu.VMEM(box, bf16),
            pltpu.VMEM((kv_local, 2 * picks, span, 2 * HEAD_DIM), bf16),
            pltpu.VMEM((kv_local, 2, span, 2 * HEAD_DIM), jnp.float32),
            dma((4,)),
            dma((heads,)),
            dma((heads,)),
            dma((kv_local, heads)),
            dma((kv_local, heads)),
            dma((kv_local, n)),
            dma((kv_local, n)),
            dma((kv_local, n)),
            dma((kv_local, n)),
            pltpu.SMEM((4,), jnp.int32),
            pltpu.VMEM((kv_local, 2 * span, 2 * HEAD_DIM), bf16),
            pltpu.VMEM((kv_local, 2 * span, 2 * HEAD_DIM), bf16),
            pltpu.VMEM((kv_local, 3, span, 2 * HEAD_DIM), bf16),
            pltpu.VMEM((kv_local, 3, span, 2 * HEAD_DIM), bf16),
            pltpu.VMEM((kv_local, 2, span, 2 * HEAD_DIM), bf16),
            pltpu.VMEM((kv_local, 2, span, 2 * HEAD_DIM), bf16),
            dma((2, kv_local)),
            dma((kv_local, 3)),
            dma((kv_local, 3)),
            dma((2, kv_local)),
        ],
        compiler_params=pltpu.CompilerParams(
            collective_id=0, has_side_effects=True, vmem_limit_bytes=VMEM_BYTES
        ),
        cost_estimate=pl.CostEstimate(
            flops=flops, bytes_accessed=4 * queries.size * 2, transcendentals=flops // 1536
        ),
    )(span_place, block_lists.T, queries, key_rows, value_rows, cotangent)
    return tuple(
        pl.pallas_call(
            write_out,
            out_shape=[jax.ShapeDtypeStruct(item.shape, item.dtype) for item in results],
            in_specs=[hbm] * 4,
            out_specs=[hbm] * 4,
            scratch_shapes=[pltpu.VMEM(item.shape, item.dtype) for item in results]
            + [dma((2, 4))],
            compiler_params=pltpu.CompilerParams(vmem_limit_bytes=VMEM_BYTES),
        )(*results)
    )


def solution(mesh):
    in_specs = (
        P("seq", "head"),
        P("seq", "head"),
        P("seq", "head"),
        P(),
        P(),
        P(("seq", "head"), None),
    )
    out_specs = (P(("seq", "head"), None), P("seq", "head"), P("seq", "head"), P("seq", "head"))
    return jax.shard_map(body, mesh=mesh, in_specs=in_specs, out_specs=out_specs, check_vma=False)
```

```python
import functools
import math

import jax
import jax.numpy as jnp
from jax import lax
from jax.experimental import pallas as pl
from jax.experimental.pallas import tpu as pltpu
from jax.sharding import PartitionSpec as P

HEAD_DIM = 128
HIDDEN = -1e30
LOG2_E = math.log2(math.e)
VMEM_BYTES = 64 * 1024 * 1024


def dot(left, right, left_dim, right_dim):
    return lax.dot_general(
        left, right, (((left_dim,), (right_dim,)), ((), ())), preferred_element_type=jnp.float32
    )


def kernel(
    dims,
    place_ref,
    lists_ref,
    q_in,
    k_in,
    v_in,
    cot_ref,
    att_ref,
    qg_out,
    kg_out,
    vg_out,
    half_tab,
    owner_tab,
    valid_tab,
    q_ref,
    k_ref,
    v_ref,
    qg_ref,
    kg_ref,
    vg_ref,
    do_buf,
    att_buf,
    kv_send,
    kv_recv,
    g_send,
    g_recv,
    parts,
    own_acc,
    local_sem,
    cot_ssem,
    cot_rsem,
    att_ssem,
    att_rsem,
    kv_ssem,
    kv_rsem,
    g_ssem,
    g_rsem,
    sel_tab,
    full_send,
    full_recv,
    fwd_send,
    col_recv,
    comb_send,
    comb_recv,
    full_sem,
    fwd_sem,
    col_rsem,
    comb_sem,
):
    n, heads, span, picks, kv_local, group = dims
    me = lax.axis_index("seq")
    hd = lax.axis_index("head")
    rows = 2 * span // heads
    width = kv_local * group * HEAD_DIM
    gwidth = group * HEAD_DIM
    scale = 1.0 / math.sqrt(HEAD_DIM)

    relay = n == 8
    z, y = me // 2, lax.rem(me, 2)
    is_end = (z == 0) | (z == 3)
    is_inner = jnp.logical_not(is_end)
    via = jnp.where(z == 0, 4, 2) + y
    served = jnp.where(z == 2, 0, 6) + y
    far_end = jnp.where(z == 2, 6, 0)
    helped = (2 * z + 1 - y, far_end + y, far_end + 1 - y)

    def far(peer):
        apart = peer // 2 - z
        return (apart >= 2) | (apart <= -2)

    def peer_is_end(peer):
        return (peer // 2 == 0) | (peer // 2 == 3)

    def only(condition, action):
        if relay:
            pl.when(condition)(action)
        else:
            action()

    fetches = [
        pltpu.make_async_copy(source, target, local_sem.at[at])
        for at, (source, target) in enumerate(((k_in, k_ref), (v_in, v_ref), (q_in, q_ref)))
    ]
    fetches.append(
        pltpu.make_async_copy(
            cot_ref.at[:, pl.ds(pl.multiple_of(hd * width, width), width)],
            do_buf.at[pl.ds(pl.multiple_of(hd * rows, rows), rows), :],
            local_sem.at[3],
        )
    )
    for fetch in fetches:
        fetch.start()

    barrier = pltpu.get_barrier_semaphore()

    def greet_seq(step, carry):
        peer = lax.rem(me + step, n)
        pl.semaphore_signal(barrier, inc=1, device_id={"seq": peer})
        return carry

    def greet_head(step, carry):
        peer = lax.rem(hd + step, heads)
        pl.semaphore_signal(barrier, inc=1, device_id={"head": peer})
        return carry

    lax.fori_loop(1, n, greet_seq, 0)
    lax.fori_loop(1, heads, greet_head, 0)

    my_second = place_ref[2 * me + 1]

    def fill_half(peer, carry):
        wants = jnp.int32(0)
        for side in range(2):
            block = place_ref[2 * peer + side]
            for pick in range(picks):
                wants = jnp.where(lists_ref[pick, block] == my_second, 1, wants)
        half_tab[peer] = wants
        return carry

    lax.fori_loop(0, n, fill_half, 0)

    if relay:
        end_second = place_ref[2 * served + 1]
        for at, who in enumerate(helped + (me,)):
            wants = jnp.int32(0)
            for side in range(2):
                block = place_ref[2 * who + side]
                for pick in range(picks):
                    wants = jnp.where(lists_ref[pick, block] == end_second, 1, wants)
            sel_tab[at] = wants

    spare = lax.rem(me + 1, n)
    for side in range(2):
        own = place_ref[2 * me + side]
        blocks = [lists_ref[pick, own] for pick in range(picks)]
        for pick in range(picks):
            block = blocks[pick]
            valid = jnp.where(block != own, 1, 0)
            for before in range(pick):
                valid = jnp.where(block == blocks[before], 0, valid)

            def find(at, owner, block=block):
                hit = (place_ref[2 * at] == block) | (place_ref[2 * at + 1] == block)
                return jnp.where(hit, at, owner)

            owner = lax.fori_loop(0, n, find, jnp.int32(0))
            owner_tab[side * picks + pick] = jnp.where(valid == 1, owner, spare)
            valid_tab[side * picks + pick] = valid

    pl.semaphore_wait(barrier, n - 1 + heads - 1)

    def cot_copy(peer, slot):
        return pltpu.make_async_remote_copy(
            src_ref=cot_ref.at[:, pl.ds(pl.multiple_of(peer * width, width), width)],
            dst_ref=do_buf.at[pl.ds(pl.multiple_of(slot * rows, rows), rows), :],
            send_sem=cot_ssem.at[peer],
            recv_sem=cot_rsem.at[slot],
            device_id={"head": peer},
        )

    def att_copy(peer, slot, g):
        return pltpu.make_async_remote_copy(
            src_ref=att_buf.at[
                pl.ds(pl.multiple_of(peer * rows, rows), rows), pl.ds(g * gwidth, gwidth)
            ],
            dst_ref=att_ref.at[
                :, pl.ds(pl.multiple_of(slot * width + g * gwidth, gwidth), gwidth)
            ],
            send_sem=att_ssem.at[g, peer],
            recv_sem=att_rsem.at[g, slot],
            device_id={"head": peer},
        )

    def kv_copy(peer, slot, g):
        return pltpu.make_async_remote_copy(
            src_ref=kv_send.at[g, peer],
            dst_ref=kv_recv[g].at[slot],
            send_sem=kv_ssem.at[g, peer],
            recv_sem=kv_rsem.at[g, slot],
            device_id={"seq": peer},
        )

    def grad_copy(peer, slot, g):
        return pltpu.make_async_remote_copy(
            src_ref=g_send.at[g, peer],
            dst_ref=g_recv.at[g, slot],
            send_sem=g_ssem.at[g, peer],
            recv_sem=g_rsem.at[g, slot],
            device_id={"seq": peer},
        )

    def full_copy(g):
        return pltpu.make_async_remote_copy(
            src_ref=full_send.at[g],
            dst_ref=full_recv.at[g],
            send_sem=full_sem.at[0, g],
            recv_sem=full_sem.at[1, g],
            device_id={"seq": via},
        )

    def forward_copy(g, at):
        return pltpu.make_async_remote_copy(
            src_ref=fwd_send.at[g, at],
            dst_ref=kv_recv[g].at[served],
            send_sem=fwd_sem.at[g, at],
            recv_sem=kv_rsem.at[g, served],
            device_id={"seq": helped[at]},
        )

    def collect_copy(peer, slot, g):
        through = jnp.where(peer // 2 == 0, 4, 2) + lax.rem(peer, 2)
        return pltpu.make_async_remote_copy(
            src_ref=g_send.at[g, peer],
            dst_ref=col_recv.at[g, slot],
            send_sem=g_ssem.at[g, peer],
            recv_sem=col_rsem.at[g, slot],
            device_id={"seq": through},
        )

    def combined_copy(g):
        return pltpu.make_async_remote_copy(
            src_ref=comb_send.at[g],
            dst_ref=comb_recv.at[g],
            send_sem=comb_sem.at[0, g],
            recv_sem=comb_sem.at[1, g],
            device_id={"seq": served},
        )

    def over_seq(action):
        def one(step, carry):
            action(lax.rem(me + step, n))
            return carry

        lax.fori_loop(1, n, one, 0)

    def over_head(action):
        def one(step, carry):
            action(lax.rem(hd + step, heads))
            return carry

        lax.fori_loop(1, heads, one, 0)

    over_head(lambda peer: cot_copy(peer, hd).start())
    fetches[0].wait()
    fetches[1].wait()

    def send_full(g):
        cols = slice(g * HEAD_DIM, (g + 1) * HEAD_DIM)
        if relay:

            @pl.when(is_end)
            def _():
                full_send[g, :, :HEAD_DIM] = k_ref[:, cols]
                full_send[g, :, HEAD_DIM:] = v_ref[:, cols]
                full_copy(g).start()

    def send_keys(g):
        cols = slice(g * HEAD_DIM, (g + 1) * HEAD_DIM)

        def send_kv(peer):
            second = half_tab[peer] == 1
            kv_send[g, peer, :, :HEAD_DIM] = jnp.where(second, k_ref[span:, cols], k_ref[:span, cols])
            kv_send[g, peer, :, HEAD_DIM:] = jnp.where(second, v_ref[span:, cols], v_ref[:span, cols])

            only(jnp.logical_not(is_end & far(peer)), kv_copy(peer, me, g).start)

        def over_seq_back():
            def one(step, carry):
                send_kv(lax.rem(me + n - step, n))
                return carry

            lax.fori_loop(1, n, one, 0)

        if relay:
            pl.when(z == 1)(over_seq_back)
            pl.when(z != 1)(lambda: over_seq(send_kv))
        else:
            over_seq(send_kv)

    def relay_keys(g):
        if relay:

            @pl.when(is_inner)
            def _():
                full_copy(g).wait_recv()
                for at in range(4):
                    second = sel_tab[at] == 1
                    block = jnp.where(second, full_recv[g, span:], full_recv[g, :span])
                    if at < 3:
                        fwd_send[g, at] = block
                        forward_copy(g, at).start()
                    else:
                        kv_recv[g][served] = block

    for g in range(kv_local):
        send_full(g)
    for g in range(kv_local):
        send_keys(g)
    for g in range(kv_local):
        relay_keys(g)
    fetches[2].wait()
    fetches[3].wait()
    over_head(lambda peer: cot_copy(hd, peer).wait_recv())

    pair = 2
    lanes = pair * span
    key_at = lax.broadcasted_iota(jnp.int32, (span, lanes), 0)
    query_at = lax.rem(lax.broadcasted_iota(jnp.int32, (span, lanes), 1), span)
    causal = key_at <= query_at

    for g in range(kv_local):
        cols = slice(g * HEAD_DIM, (g + 1) * HEAD_DIM)
        over_seq(
            lambda peer, g=g: only(
                jnp.logical_not(is_inner & (peer == served)), kv_copy(me, peer, g).wait_recv
            )
        )

        def attend(side, carry, g=g, cols=cols):
            base = pl.multiple_of(side * span, span)
            here = pl.ds(base, span)
            keys = [k_ref[here, cols]]
            values = [v_ref[here, cols]]
            valid = []
            for pick in range(picks):
                owner = owner_tab[side * picks + pick]
                keys.append(kv_recv[g][owner, :, :HEAD_DIM])
                values.append(kv_recv[g][owner, :, HEAD_DIM:])
                valid.append(valid_tab[side * picks + pick] == 1)
            keys = jnp.concatenate(keys, axis=0)
            values = jnp.concatenate(values, axis=0)
            key_sum = None
            for chunk in range(group // pair):
                first = g * group + chunk * pair
                spots = [
                    slice((first + at) * HEAD_DIM, (first + at + 1) * HEAD_DIM)
                    for at in range(pair)
                ]
                query = jnp.concatenate([q_ref[here, spot] for spot in spots], axis=0)
                grad = jnp.concatenate([do_buf[here, spot] for spot in spots], axis=0)
                scores = dot(keys, query, 1, 1)
                pieces = [
                    scores[at * span : (at + 1) * span] for at in range(picks + 1)
                ]
                pieces[0] = jnp.where(causal, pieces[0], HIDDEN)
                tops = [jnp.max(piece, axis=0, keepdims=True) for piece in pieces]
                top = tops[0]
                for pick in range(picks):
                    top = jnp.maximum(top, jnp.where(valid[pick], tops[pick + 1], HIDDEN))
                probs = [jnp.exp2((pieces[0] - top) * (scale * LOG2_E))]
                for pick in range(picks):
                    above = jnp.where(valid[pick], top, -HIDDEN)
                    probs.append(jnp.exp2((pieces[pick + 1] - above) * (scale * LOG2_E)))
                probs = jnp.concatenate(probs, axis=0)
                total = jnp.sum(probs, axis=0, keepdims=True)
                probs = probs * (1.0 / total)
                weights = probs.astype(jnp.bfloat16)
                attended = dot(values, weights, 0, 0)
                slopes = dot(values, grad, 1, 1)
                delta = jnp.sum(probs * slopes, axis=0, keepdims=True)
                dscores = (probs * (slopes - delta)).astype(jnp.bfloat16)
                query_grad = dot(keys, dscores, 0, 0)
                attended = attended.T.astype(jnp.bfloat16)
                query_grad = (query_grad * scale).T.astype(jnp.bfloat16)
                for at in range(pair):
                    att_buf[here, spots[at]] = attended[at * span : (at + 1) * span]
                    qg_ref[here, spots[at]] = query_grad[at * span : (at + 1) * span]
                key_part = dot(dscores, query, 1, 0)
                value_part = dot(weights, grad, 1, 0)
                if key_sum is None:
                    key_sum, value_sum = key_part, value_part
                else:
                    key_sum, value_sum = key_sum + key_part, value_sum + value_part
            key_sum = key_sum * scale
            own_acc[g, side, :, :HEAD_DIM] = key_sum[:span]
            own_acc[g, side, :, HEAD_DIM:] = value_sum[:span]
            for pick in range(picks):
                piece = slice((pick + 1) * span, (pick + 2) * span)
                parts[g, side * picks + pick, :, :HEAD_DIM] = key_sum[piece].astype(jnp.bfloat16)
                parts[g, side * picks + pick, :, HEAD_DIM:] = value_sum[piece].astype(jnp.bfloat16)
            return carry

        lax.fori_loop(0, 2, attend, 0)

        def stage_grad(peer, g=g):
            spot = jnp.int32(0)
            found = jnp.int32(0)
            for at in range(2 * picks):
                hit = (owner_tab[at] == peer) & (valid_tab[at] == 1)
                spot = jnp.where(hit, at, spot)
                found = jnp.where(hit, 1, found)
            part = parts[g, spot]
            g_send[g, peer] = jnp.where(found == 1, part, jnp.zeros_like(part))

        def send_through(peer, g=g):
            @pl.when(peer_is_end(peer) & far(peer))
            def _():
                stage_grad(peer)
                slot = jnp.where(is_inner, 0, jnp.where(lax.rem(peer, 2) == y, 1, 2))

                @pl.when(jnp.logical_not(is_inner & (peer == served)))
                def _():
                    collect_copy(peer, slot, g).start()

        def send_direct(peer, g=g):
            def go():
                stage_grad(peer)
                grad_copy(peer, me, g).start()

            only(jnp.logical_not(peer_is_end(peer) & far(peer)), go)

        if relay:
            over_seq(send_through)
        over_seq(send_direct)
        over_head(lambda peer, g=g: att_copy(peer, hd, g).start())

    if relay:
        for g in range(kv_local):

            @pl.when(is_inner)
            def _(g=g):
                sums = [jnp.zeros((span, 2 * HEAD_DIM), jnp.float32)] * 2
                for at in range(4):
                    if at < 3:
                        collect_copy(served, at, g).wait_recv()
                        part = col_recv[g, at].astype(jnp.float32)
                    else:
                        part = g_send[g, served].astype(jnp.float32)
                    second = sel_tab[at] == 1
                    sums[0] = sums[0] + jnp.where(second, 0.0, part)
                    sums[1] = sums[1] + jnp.where(second, part, 0.0)
                for side in range(2):
                    comb_send[g, side] = sums[side].astype(jnp.bfloat16)
                combined_copy(g).start()

    leaving = [
        pltpu.make_async_copy(source, target, local_sem.at[at])
        for at, (source, target) in enumerate(
            (
                (
                    att_buf.at[pl.ds(pl.multiple_of(hd * rows, rows), rows), :],
                    att_ref.at[:, pl.ds(pl.multiple_of(hd * width, width), width)],
                ),
                (qg_ref, qg_out),
                (kg_ref, kg_out),
                (vg_ref, vg_out),
            )
        )
    ]
    leaving[0].start()
    leaving[1].start()

    for g in range(kv_local):
        cols = slice(g * HEAD_DIM, (g + 1) * HEAD_DIM)

        def add_grad(peer, g=g):
            def arrived():
                grad_copy(me, peer, g).wait_recv()
                part = g_recv[g, peer].astype(jnp.float32)
                second = half_tab[peer] == 1
                own_acc[g, 0] += jnp.where(second, 0.0, part)
                own_acc[g, 1] += jnp.where(second, part, 0.0)

            only(jnp.logical_not(is_end & far(peer)), arrived)

        over_seq(add_grad)
        if relay:

            @pl.when(is_end)
            def _(g=g):
                combined_copy(g).wait_recv()
                for side in range(2):
                    own_acc[g, side] += comb_recv[g, side].astype(jnp.float32)

        for side in range(2):
            here = slice(side * span, (side + 1) * span)
            kg_ref[here, cols] = own_acc[g, side, :, :HEAD_DIM].astype(jnp.bfloat16)
            vg_ref[here, cols] = own_acc[g, side, :, HEAD_DIM:].astype(jnp.bfloat16)

    leaving[2].start()
    leaving[3].start()
    over_head(lambda peer: cot_copy(peer, hd).wait_send())
    for g in range(kv_local):
        over_head(lambda peer, g=g: att_copy(hd, peer, g).wait_recv())
        over_head(lambda peer, g=g: att_copy(peer, hd, g).wait_send())
        over_seq(
            lambda peer, g=g: only(
                jnp.logical_not(is_end & far(peer)), kv_copy(peer, me, g).wait_send
            )
        )
        over_seq(
            lambda peer, g=g: only(
                jnp.logical_not(is_inner & (peer == served)), grad_copy(peer, me, g).wait_send
            )
        )
        if relay:

            pl.when(is_end)(full_copy(g).wait_send)

            @pl.when(is_inner)
            def _(g=g):
                for at in range(3):
                    forward_copy(g, at).wait_send()
                combined_copy(g).wait_send()

    for copy in leaving:
        copy.wait()


def write_out(*refs):
    sources, targets, stages, sems = refs[:4], refs[4:8], refs[8:12], refs[12]
    arrive = [
        pltpu.make_async_copy(source, stage, sems.at[0, at])
        for at, (source, stage) in enumerate(zip(sources, stages))
    ]
    leave = [
        pltpu.make_async_copy(stage, target, sems.at[1, at])
        for at, (stage, target) in enumerate(zip(stages, targets))
    ]
    for copy in arrive:
        copy.start()
    for at in range(4):
        arrive[at].wait()
        leave[at].start()
    for copy in leave:
        copy.wait()


def body(queries, key_rows, value_rows, span_place, block_lists, cotangent):
    n = lax.axis_size("seq")
    heads = lax.axis_size("head")
    span = queries.shape[0] // 2
    picks = block_lists.shape[1]
    kv_local = key_rows.shape[1] // HEAD_DIM
    group = queries.shape[1] // key_rows.shape[1]
    bf16 = jnp.bfloat16
    hbm = pl.BlockSpec(memory_space=pltpu.HBM)
    smem = pl.BlockSpec(memory_space=pltpu.SMEM)
    box = (kv_local, n, span, 2 * HEAD_DIM)
    dma = pltpu.SemaphoreType.DMA
    flops = 6 * 2 * 2 * span * span * (picks + 1) * queries.shape[1]
    results = pl.pallas_call(
        functools.partial(kernel, (n, heads, span, picks, kv_local, group)),
        out_shape=[
            jax.ShapeDtypeStruct(cotangent.shape, bf16),
            jax.ShapeDtypeStruct(queries.shape, bf16),
            jax.ShapeDtypeStruct(key_rows.shape, bf16),
            jax.ShapeDtypeStruct(value_rows.shape, bf16),
        ],
        in_specs=[smem, smem, hbm, hbm, hbm, hbm],
        out_specs=[hbm] * 4,
        scratch_shapes=[
            pltpu.SMEM((n,), jnp.int32),
            pltpu.SMEM((2 * picks,), jnp.int32),
            pltpu.SMEM((2 * picks,), jnp.int32),
            pltpu.VMEM(queries.shape, bf16),
            pltpu.VMEM(key_rows.shape, bf16),
            pltpu.VMEM(value_rows.shape, bf16),
            pltpu.VMEM(queries.shape, bf16),
            pltpu.VMEM(key_rows.shape, bf16),
            pltpu.VMEM(value_rows.shape, bf16),
            pltpu.VMEM(queries.shape, bf16),
            pltpu.VMEM(queries.shape, bf16),
            pltpu.VMEM(box, bf16),
            [pltpu.VMEM(box[1:], bf16)] * kv_local,
            pltpu.VMEM(box, bf16),
            pltpu.VMEM(box, bf16),
            pltpu.VMEM((kv_local, 2 * picks, span, 2 * HEAD_DIM), bf16),
            pltpu.VMEM((kv_local, 2, span, 2 * HEAD_DIM), jnp.float32),
            dma((4,)),
            dma((heads,)),
            dma((heads,)),
            dma((kv_local, heads)),
            dma((kv_local, heads)),
            dma((kv_local, n)),
            dma((kv_local, n)),
            dma((kv_local, n)),
            dma((kv_local, n)),
            pltpu.SMEM((4,), jnp.int32),
            pltpu.VMEM((kv_local, 2 * span, 2 * HEAD_DIM), bf16),
            pltpu.VMEM((kv_local, 2 * span, 2 * HEAD_DIM), bf16),
            pltpu.VMEM((kv_local, 3, span, 2 * HEAD_DIM), bf16),
            pltpu.VMEM((kv_local, 3, span, 2 * HEAD_DIM), bf16),
            pltpu.VMEM((kv_local, 2, span, 2 * HEAD_DIM), bf16),
            pltpu.VMEM((kv_local, 2, span, 2 * HEAD_DIM), bf16),
            dma((2, kv_local)),
            dma((kv_local, 3)),
            dma((kv_local, 3)),
            dma((2, kv_local)),
        ],
        compiler_params=pltpu.CompilerParams(
            collective_id=0, has_side_effects=True, vmem_limit_bytes=VMEM_BYTES
        ),
        cost_estimate=pl.CostEstimate(
            flops=flops, bytes_accessed=4 * queries.size * 2, transcendentals=flops // 1536
        ),
    )(span_place, block_lists.T, queries, key_rows, value_rows, cotangent)
    return tuple(
        pl.pallas_call(
            write_out,
            out_shape=[jax.ShapeDtypeStruct(item.shape, item.dtype) for item in results],
            in_specs=[hbm] * 4,
            out_specs=[hbm] * 4,
            scratch_shapes=[pltpu.VMEM(item.shape, item.dtype) for item in results]
            + [dma((2, 4))],
            compiler_params=pltpu.CompilerParams(vmem_limit_bytes=VMEM_BYTES),
        )(*results)
    )


def solution(mesh):
    in_specs = (
        P("seq", "head"),
        P("seq", "head"),
        P("seq", "head"),
        P(),
        P(),
        P(("seq", "head"), None),
    )
    out_specs = (P(("seq", "head"), None), P("seq", "head"), P("seq", "head"), P("seq", "head"))
    return jax.shard_map(body, mesh=mesh, in_specs=in_specs, out_specs=out_specs, check_vma=False)
```

```python
import functools
import math

import jax
import jax.numpy as jnp
from jax import lax
from jax.experimental import pallas as pl
from jax.experimental.pallas import tpu as pltpu
from jax.sharding import PartitionSpec as P

HEAD_DIM = 128
HIDDEN = -1e30
CHUNKS = 4
LOG2_E = math.log2(math.e)
VMEM_BYTES = 64 * 1024 * 1024


def dot(left, right, left_dim, right_dim):
    return lax.dot_general(
        left, right, (((left_dim,), (right_dim,)), ((), ())), preferred_element_type=jnp.float32
    )


def kernel(
    dims,
    place_ref,
    lists_ref,
    q_in,
    k_in,
    v_in,
    cot_ref,
    att_ref,
    qg_out,
    kg_out,
    vg_out,
    half_tab,
    owner_tab,
    valid_tab,
    q_ref,
    k_ref,
    v_ref,
    qg_ref,
    kg_ref,
    vg_ref,
    do_buf,
    att_buf,
    kv_send,
    kv_recv,
    g_send,
    g_recv,
    parts,
    own_acc,
    local_sem,
    cot_ssem,
    cot_rsem,
    att_ssem,
    att_rsem,
    kv_ssem,
    kv_rsem,
    g_ssem,
    g_rsem,
    sel_tab,
    full_send,
    full_recv,
    fwd_send,
    col_recv,
    comb_send,
    comb_recv,
    full_sem,
    fwd_sem,
    col_rsem,
    comb_sem,
):
    n, heads, span, picks, kv_local, group = dims
    me = lax.axis_index("seq")
    hd = lax.axis_index("head")
    rows = 2 * span // heads
    width = kv_local * group * HEAD_DIM
    gwidth = group * HEAD_DIM
    scale = 1.0 / math.sqrt(HEAD_DIM)

    relay = n == 8
    z, y = me // 2, lax.rem(me, 2)
    is_end = (z == 0) | (z == 3)
    is_inner = jnp.logical_not(is_end)
    via = jnp.where(z == 0, 4, 2) + y
    served = jnp.where(z == 2, 0, 6) + y
    far_end = jnp.where(z == 2, 6, 0)
    helped = (2 * z + 1 - y, far_end + y, far_end + 1 - y)

    def far(peer):
        apart = peer // 2 - z
        return (apart >= 2) | (apart <= -2)

    def peer_is_end(peer):
        return (peer // 2 == 0) | (peer // 2 == 3)

    def only(condition, action):
        if relay:
            pl.when(condition)(action)
        else:
            action()

    fetches = [
        pltpu.make_async_copy(source, target, local_sem.at[at])
        for at, (source, target) in enumerate(((k_in, k_ref), (v_in, v_ref), (q_in, q_ref)))
    ]
    fetches.append(
        pltpu.make_async_copy(
            cot_ref.at[:, pl.ds(pl.multiple_of(hd * width, width), width)],
            do_buf.at[pl.ds(pl.multiple_of(hd * rows, rows), rows), :],
            local_sem.at[3],
        )
    )
    for fetch in fetches:
        fetch.start()

    barrier = pltpu.get_barrier_semaphore()

    def greet_seq(step, carry):
        peer = lax.rem(me + step, n)
        pl.semaphore_signal(barrier, inc=1, device_id={"seq": peer})
        return carry

    def greet_head(step, carry):
        peer = lax.rem(hd + step, heads)
        pl.semaphore_signal(barrier, inc=1, device_id={"head": peer})
        return carry

    lax.fori_loop(1, n, greet_seq, 0)
    lax.fori_loop(1, heads, greet_head, 0)

    my_second = place_ref[2 * me + 1]

    def fill_half(peer, carry):
        wants = jnp.int32(0)
        for side in range(2):
            block = place_ref[2 * peer + side]
            for pick in range(picks):
                wants = jnp.where(lists_ref[pick, block] == my_second, 1, wants)
        half_tab[peer] = wants
        return carry

    lax.fori_loop(0, n, fill_half, 0)

    if relay:
        end_second = place_ref[2 * served + 1]
        for at, who in enumerate(helped + (me,)):
            wants = jnp.int32(0)
            for side in range(2):
                block = place_ref[2 * who + side]
                for pick in range(picks):
                    wants = jnp.where(lists_ref[pick, block] == end_second, 1, wants)
            sel_tab[at] = wants

    spare = lax.rem(me + 1, n)
    for side in range(2):
        own = place_ref[2 * me + side]
        blocks = [lists_ref[pick, own] for pick in range(picks)]
        for pick in range(picks):
            block = blocks[pick]
            valid = jnp.where(block != own, 1, 0)
            for before in range(pick):
                valid = jnp.where(block == blocks[before], 0, valid)

            def find(at, owner, block=block):
                hit = (place_ref[2 * at] == block) | (place_ref[2 * at + 1] == block)
                return jnp.where(hit, at, owner)

            owner = lax.fori_loop(0, n, find, jnp.int32(0))
            owner_tab[side * picks + pick] = jnp.where(valid == 1, owner, spare)
            valid_tab[side * picks + pick] = valid

    pl.semaphore_wait(barrier, n - 1 + heads - 1)

    def cot_copy(peer, slot):
        return pltpu.make_async_remote_copy(
            src_ref=cot_ref.at[:, pl.ds(pl.multiple_of(peer * width, width), width)],
            dst_ref=do_buf.at[pl.ds(pl.multiple_of(slot * rows, rows), rows), :],
            send_sem=cot_ssem.at[peer],
            recv_sem=cot_rsem.at[slot],
            device_id={"head": peer},
        )

    def att_copy(peer, slot, g):
        return pltpu.make_async_remote_copy(
            src_ref=att_buf.at[
                pl.ds(pl.multiple_of(peer * rows, rows), rows), pl.ds(g * gwidth, gwidth)
            ],
            dst_ref=att_ref.at[
                :, pl.ds(pl.multiple_of(slot * width + g * gwidth, gwidth), gwidth)
            ],
            send_sem=att_ssem.at[g, peer],
            recv_sem=att_rsem.at[g, slot],
            device_id={"head": peer},
        )

    def kv_copy(peer, slot, g):
        return pltpu.make_async_remote_copy(
            src_ref=kv_send.at[g, peer],
            dst_ref=kv_recv[g].at[slot],
            send_sem=kv_ssem.at[g, peer],
            recv_sem=kv_rsem.at[g, slot],
            device_id={"seq": peer},
        )

    def grad_copy(peer, slot, g):
        return pltpu.make_async_remote_copy(
            src_ref=g_send.at[g, peer],
            dst_ref=g_recv.at[g, slot],
            send_sem=g_ssem.at[g, peer],
            recv_sem=g_rsem.at[g, slot],
            device_id={"seq": peer},
        )

    def full_copy(g):
        return pltpu.make_async_remote_copy(
            src_ref=full_send.at[g],
            dst_ref=full_recv.at[g],
            send_sem=full_sem.at[0, g],
            recv_sem=full_sem.at[1, g],
            device_id={"seq": via},
        )

    def forward_copy(g, at):
        return pltpu.make_async_remote_copy(
            src_ref=fwd_send.at[g, at],
            dst_ref=kv_recv[g].at[served],
            send_sem=fwd_sem.at[g, at],
            recv_sem=kv_rsem.at[g, served],
            device_id={"seq": helped[at]},
        )

    def collect_copy(peer, slot, g):
        through = jnp.where(peer // 2 == 0, 4, 2) + lax.rem(peer, 2)
        return pltpu.make_async_remote_copy(
            src_ref=g_send.at[g, peer],
            dst_ref=col_recv.at[g, slot],
            send_sem=g_ssem.at[g, peer],
            recv_sem=col_rsem.at[g, slot],
            device_id={"seq": through},
        )

    def combined_copy(g):
        return pltpu.make_async_remote_copy(
            src_ref=comb_send.at[g],
            dst_ref=comb_recv.at[g],
            send_sem=comb_sem.at[0, g],
            recv_sem=comb_sem.at[1, g],
            device_id={"seq": served},
        )

    def over_seq(action):
        def one(step, carry):
            action(lax.rem(me + step, n))
            return carry

        lax.fori_loop(1, n, one, 0)

    def over_head(action):
        def one(step, carry):
            action(lax.rem(hd + step, heads))
            return carry

        lax.fori_loop(1, heads, one, 0)

    over_head(lambda peer: cot_copy(peer, hd).start())
    fetches[0].wait()
    fetches[1].wait()

    def send_full(g):
        cols = slice(g * HEAD_DIM, (g + 1) * HEAD_DIM)
        if relay:

            @pl.when(is_end)
            def _():
                full_send[g, :, :HEAD_DIM] = k_ref[:, cols]
                full_send[g, :, HEAD_DIM:] = v_ref[:, cols]
                full_copy(g).start()

    def send_keys(g):
        cols = slice(g * HEAD_DIM, (g + 1) * HEAD_DIM)

        def send_kv(peer):
            second = half_tab[peer] == 1
            kv_send[g, peer, :, :HEAD_DIM] = jnp.where(second, k_ref[span:, cols], k_ref[:span, cols])
            kv_send[g, peer, :, HEAD_DIM:] = jnp.where(second, v_ref[span:, cols], v_ref[:span, cols])

            only(jnp.logical_not(is_end & far(peer)), kv_copy(peer, me, g).start)

        over_seq(send_kv)

    def relay_keys(g):
        if relay:

            @pl.when(is_inner)
            def _():
                full_copy(g).wait_recv()
                for at in range(4):
                    second = sel_tab[at] == 1
                    block = jnp.where(second, full_recv[g, span:], full_recv[g, :span])
                    if at < 3:
                        fwd_send[g, at] = block
                        forward_copy(g, at).start()
                    else:
                        kv_recv[g][served] = block

    for g in range(kv_local):
        send_full(g)
    for g in range(kv_local):
        send_keys(g)
    for g in range(kv_local):
        relay_keys(g)
    fetches[2].wait()
    fetches[3].wait()
    over_head(lambda peer: cot_copy(hd, peer).wait_recv())

    pair = 2
    lanes = pair * span
    key_at = lax.broadcasted_iota(jnp.int32, (span, lanes), 0)
    query_at = lax.rem(lax.broadcasted_iota(jnp.int32, (span, lanes), 1), span)
    causal = key_at <= query_at

    for g in range(kv_local):
        cols = slice(g * HEAD_DIM, (g + 1) * HEAD_DIM)
        over_seq(
            lambda peer, g=g: only(
                jnp.logical_not(is_inner & (peer == served)), kv_copy(me, peer, g).wait_recv
            )
        )

        def attend(side, carry, g=g, cols=cols):
            base = pl.multiple_of(side * span, span)
            here = pl.ds(base, span)
            keys = [k_ref[here, cols]]
            values = [v_ref[here, cols]]
            valid = []
            for pick in range(picks):
                owner = owner_tab[side * picks + pick]
                keys.append(kv_recv[g][owner, :, :HEAD_DIM])
                values.append(kv_recv[g][owner, :, HEAD_DIM:])
                valid.append(valid_tab[side * picks + pick] == 1)
            keys = jnp.concatenate(keys, axis=0)
            values = jnp.concatenate(values, axis=0)
            key_sum = None
            for chunk in range(group // pair):
                first = g * group + chunk * pair
                spots = [
                    slice((first + at) * HEAD_DIM, (first + at + 1) * HEAD_DIM)
                    for at in range(pair)
                ]
                query = jnp.concatenate([q_ref[here, spot] for spot in spots], axis=0)
                grad = jnp.concatenate([do_buf[here, spot] for spot in spots], axis=0)
                scores = dot(keys, query, 1, 1)
                pieces = [
                    scores[at * span : (at + 1) * span] for at in range(picks + 1)
                ]
                pieces[0] = jnp.where(causal, pieces[0], HIDDEN)
                tops = [jnp.max(piece, axis=0, keepdims=True) for piece in pieces]
                top = tops[0]
                for pick in range(picks):
                    top = jnp.maximum(top, jnp.where(valid[pick], tops[pick + 1], HIDDEN))
                probs = [jnp.exp2((pieces[0] - top) * (scale * LOG2_E))]
                for pick in range(picks):
                    above = jnp.where(valid[pick], top, -HIDDEN)
                    probs.append(jnp.exp2((pieces[pick + 1] - above) * (scale * LOG2_E)))
                probs = jnp.concatenate(probs, axis=0)
                total = jnp.sum(probs, axis=0, keepdims=True)
                probs = probs * (1.0 / total)
                weights = probs.astype(jnp.bfloat16)
                attended = dot(values, weights, 0, 0)
                slopes = dot(values, grad, 1, 1)
                delta = jnp.sum(probs * slopes, axis=0, keepdims=True)
                dscores = (probs * (slopes - delta)).astype(jnp.bfloat16)
                query_grad = dot(keys, dscores, 0, 0)
                attended = attended.T.astype(jnp.bfloat16)
                query_grad = (query_grad * scale).T.astype(jnp.bfloat16)
                for at in range(pair):
                    att_buf[here, spots[at]] = attended[at * span : (at + 1) * span]
                    qg_ref[here, spots[at]] = query_grad[at * span : (at + 1) * span]
                key_part = dot(dscores, query, 1, 0)
                value_part = dot(weights, grad, 1, 0)
                if key_sum is None:
                    key_sum, value_sum = key_part, value_part
                else:
                    key_sum, value_sum = key_sum + key_part, value_sum + value_part
            key_sum = key_sum * scale
            own_acc[g, side, :, :HEAD_DIM] = key_sum[:span]
            own_acc[g, side, :, HEAD_DIM:] = value_sum[:span]
            for pick in range(picks):
                piece = slice((pick + 1) * span, (pick + 2) * span)
                parts[g, side * picks + pick, :, :HEAD_DIM] = key_sum[piece].astype(jnp.bfloat16)
                parts[g, side * picks + pick, :, HEAD_DIM:] = value_sum[piece].astype(jnp.bfloat16)
            return carry

        lax.fori_loop(0, 2, attend, 0)

        def stage_grad(peer, g=g):
            spot = jnp.int32(0)
            found = jnp.int32(0)
            for at in range(2 * picks):
                hit = (owner_tab[at] == peer) & (valid_tab[at] == 1)
                spot = jnp.where(hit, at, spot)
                found = jnp.where(hit, 1, found)
            part = parts[g, spot]
            g_send[g, peer] = jnp.where(found == 1, part, jnp.zeros_like(part))

        def send_through(peer, g=g):
            @pl.when(peer_is_end(peer) & far(peer))
            def _():
                stage_grad(peer)
                slot = jnp.where(is_inner, 0, jnp.where(lax.rem(peer, 2) == y, 1, 2))

                @pl.when(jnp.logical_not(is_inner & (peer == served)))
                def _():
                    collect_copy(peer, slot, g).start()

        def send_direct(peer, g=g):
            def go():
                stage_grad(peer)
                grad_copy(peer, me, g).start()

            only(jnp.logical_not(peer_is_end(peer) & far(peer)), go)

        if relay:
            over_seq(send_through)
        over_seq(send_direct)
        over_head(lambda peer, g=g: att_copy(peer, hd, g).start())

    if relay:
        for g in range(kv_local):

            @pl.when(is_inner)
            def _(g=g):
                sums = [jnp.zeros((span, 2 * HEAD_DIM), jnp.float32)] * 2
                for at in range(4):
                    if at < 3:
                        collect_copy(served, at, g).wait_recv()
                        part = col_recv[g, at].astype(jnp.float32)
                    else:
                        part = g_send[g, served].astype(jnp.float32)
                    second = sel_tab[at] == 1
                    sums[0] = sums[0] + jnp.where(second, 0.0, part)
                    sums[1] = sums[1] + jnp.where(second, part, 0.0)
                for side in range(2):
                    comb_send[g, side] = sums[side].astype(jnp.bfloat16)
                combined_copy(g).start()

    leaving = [
        pltpu.make_async_copy(source, target, local_sem.at[at])
        for at, (source, target) in enumerate(
            (
                (
                    att_buf.at[pl.ds(pl.multiple_of(hd * rows, rows), rows), :],
                    att_ref.at[:, pl.ds(pl.multiple_of(hd * width, width), width)],
                ),
                (qg_ref, qg_out),
                (kg_ref, kg_out),
                (vg_ref, vg_out),
            )
        )
    ]
    leaving[0].start()
    leaving[1].start()

    for g in range(kv_local):
        cols = slice(g * HEAD_DIM, (g + 1) * HEAD_DIM)

        def add_grad(peer, g=g):
            def arrived():
                grad_copy(me, peer, g).wait_recv()
                part = g_recv[g, peer].astype(jnp.float32)
                second = half_tab[peer] == 1
                own_acc[g, 0] += jnp.where(second, 0.0, part)
                own_acc[g, 1] += jnp.where(second, part, 0.0)

            only(jnp.logical_not(is_end & far(peer)), arrived)

        over_seq(add_grad)
        if relay:

            @pl.when(is_end)
            def _(g=g):
                combined_copy(g).wait_recv()
                for side in range(2):
                    own_acc[g, side] += comb_recv[g, side].astype(jnp.float32)

        for side in range(2):
            here = slice(side * span, (side + 1) * span)
            kg_ref[here, cols] = own_acc[g, side, :, :HEAD_DIM].astype(jnp.bfloat16)
            vg_ref[here, cols] = own_acc[g, side, :, HEAD_DIM:].astype(jnp.bfloat16)

    leaving[2].start()
    leaving[3].start()
    over_head(lambda peer: cot_copy(peer, hd).wait_send())
    for g in range(kv_local):
        over_head(lambda peer, g=g: att_copy(hd, peer, g).wait_recv())
        over_head(lambda peer, g=g: att_copy(peer, hd, g).wait_send())
        over_seq(
            lambda peer, g=g: only(
                jnp.logical_not(is_end & far(peer)), kv_copy(peer, me, g).wait_send
            )
        )
        over_seq(
            lambda peer, g=g: only(
                jnp.logical_not(is_inner & (peer == served)), grad_copy(peer, me, g).wait_send
            )
        )
        if relay:

            pl.when(is_end)(full_copy(g).wait_send)

            @pl.when(is_inner)
            def _(g=g):
                for at in range(3):
                    forward_copy(g, at).wait_send()
                combined_copy(g).wait_send()

    for copy in leaving:
        copy.wait()


def write_out(*refs):
    sources, targets, stages, sems = refs[:4], refs[4:8], refs[8:12], refs[12]
    arrive = []
    leave = []
    for source, target, stage in zip(sources, targets, stages):
        piece = source.shape[0] // CHUNKS
        for at in range(CHUNKS):
            rows = slice(at * piece, (at + 1) * piece)
            spot = len(arrive)
            arrive.append(
                pltpu.make_async_copy(source.at[rows], stage.at[rows], sems.at[0, spot])
            )
            leave.append(
                pltpu.make_async_copy(stage.at[rows], target.at[rows], sems.at[1, spot])
            )
    for copy in arrive:
        copy.start()
    for came, goes in zip(arrive, leave):
        came.wait()
        goes.start()
    for copy in leave:
        copy.wait()


def body(queries, key_rows, value_rows, span_place, block_lists, cotangent):
    n = lax.axis_size("seq")
    heads = lax.axis_size("head")
    span = queries.shape[0] // 2
    picks = block_lists.shape[1]
    kv_local = key_rows.shape[1] // HEAD_DIM
    group = queries.shape[1] // key_rows.shape[1]
    bf16 = jnp.bfloat16
    hbm = pl.BlockSpec(memory_space=pltpu.HBM)
    smem = pl.BlockSpec(memory_space=pltpu.SMEM)
    box = (kv_local, n, span, 2 * HEAD_DIM)
    dma = pltpu.SemaphoreType.DMA
    flops = 6 * 2 * 2 * span * span * (picks + 1) * queries.shape[1]
    results = pl.pallas_call(
        functools.partial(kernel, (n, heads, span, picks, kv_local, group)),
        out_shape=[
            jax.ShapeDtypeStruct(cotangent.shape, bf16),
            jax.ShapeDtypeStruct(queries.shape, bf16),
            jax.ShapeDtypeStruct(key_rows.shape, bf16),
            jax.ShapeDtypeStruct(value_rows.shape, bf16),
        ],
        in_specs=[smem, smem, hbm, hbm, hbm, hbm],
        out_specs=[hbm] * 4,
        scratch_shapes=[
            pltpu.SMEM((n,), jnp.int32),
            pltpu.SMEM((2 * picks,), jnp.int32),
            pltpu.SMEM((2 * picks,), jnp.int32),
            pltpu.VMEM(queries.shape, bf16),
            pltpu.VMEM(key_rows.shape, bf16),
            pltpu.VMEM(value_rows.shape, bf16),
            pltpu.VMEM(queries.shape, bf16),
            pltpu.VMEM(key_rows.shape, bf16),
            pltpu.VMEM(value_rows.shape, bf16),
            pltpu.VMEM(queries.shape, bf16),
            pltpu.VMEM(queries.shape, bf16),
            pltpu.VMEM(box, bf16),
            [pltpu.VMEM(box[1:], bf16)] * kv_local,
            pltpu.VMEM(box, bf16),
            pltpu.VMEM(box, bf16),
            pltpu.VMEM((kv_local, 2 * picks, span, 2 * HEAD_DIM), bf16),
            pltpu.VMEM((kv_local, 2, span, 2 * HEAD_DIM), jnp.float32),
            dma((4,)),
            dma((heads,)),
            dma((heads,)),
            dma((kv_local, heads)),
            dma((kv_local, heads)),
            dma((kv_local, n)),
            dma((kv_local, n)),
            dma((kv_local, n)),
            dma((kv_local, n)),
            pltpu.SMEM((4,), jnp.int32),
            pltpu.VMEM((kv_local, 2 * span, 2 * HEAD_DIM), bf16),
            pltpu.VMEM((kv_local, 2 * span, 2 * HEAD_DIM), bf16),
            pltpu.VMEM((kv_local, 3, span, 2 * HEAD_DIM), bf16),
            pltpu.VMEM((kv_local, 3, span, 2 * HEAD_DIM), bf16),
            pltpu.VMEM((kv_local, 2, span, 2 * HEAD_DIM), bf16),
            pltpu.VMEM((kv_local, 2, span, 2 * HEAD_DIM), bf16),
            dma((2, kv_local)),
            dma((kv_local, 3)),
            dma((kv_local, 3)),
            dma((2, kv_local)),
        ],
        compiler_params=pltpu.CompilerParams(
            collective_id=0, has_side_effects=True, vmem_limit_bytes=VMEM_BYTES
        ),
        cost_estimate=pl.CostEstimate(
            flops=flops, bytes_accessed=4 * queries.size * 2, transcendentals=flops // 1536
        ),
    )(span_place, block_lists.T, queries, key_rows, value_rows, cotangent)
    return tuple(
        pl.pallas_call(
            write_out,
            out_shape=[jax.ShapeDtypeStruct(item.shape, item.dtype) for item in results],
            in_specs=[hbm] * 4,
            out_specs=[hbm] * 4,
            scratch_shapes=[pltpu.VMEM(item.shape, item.dtype) for item in results]
            + [dma((2, 4 * CHUNKS))],
            compiler_params=pltpu.CompilerParams(vmem_limit_bytes=VMEM_BYTES),
        )(*results)
    )


def solution(mesh):
    in_specs = (
        P("seq", "head"),
        P("seq", "head"),
        P("seq", "head"),
        P(),
        P(),
        P(("seq", "head"), None),
    )
    out_specs = (P(("seq", "head"), None), P("seq", "head"), P("seq", "head"), P("seq", "head"))
    return jax.shard_map(body, mesh=mesh, in_specs=in_specs, out_specs=out_specs, check_vma=False)
```

```python
import functools
import math

import jax
import jax.numpy as jnp
from jax import lax
from jax.experimental import pallas as pl
from jax.experimental.pallas import tpu as pltpu
from jax.sharding import PartitionSpec as P

HEAD_DIM = 128
HIDDEN = -1e30
CHUNKS = 4
LOG2_E = math.log2(math.e)
VMEM_BYTES = 64 * 1024 * 1024


def dot(left, right, left_dim, right_dim):
    return lax.dot_general(
        left, right, (((left_dim,), (right_dim,)), ((), ())), preferred_element_type=jnp.float32
    )


def kernel(
    dims,
    place_ref,
    lists_ref,
    q_in,
    k_in,
    v_in,
    cot_ref,
    att_ref,
    qg_out,
    kg_out,
    vg_out,
    half_tab,
    owner_tab,
    valid_tab,
    q_ref,
    k_ref,
    v_ref,
    qg_ref,
    kg_ref,
    vg_ref,
    do_buf,
    att_buf,
    kv_send,
    kv_recv,
    g_send,
    g_recv,
    parts,
    own_acc,
    local_sem,
    cot_ssem,
    cot_rsem,
    att_ssem,
    att_rsem,
    kv_ssem,
    kv_rsem,
    g_ssem,
    g_rsem,
    sel_tab,
    full_send,
    full_recv,
    fwd_send,
    col_recv,
    comb_send,
    comb_recv,
    full_sem,
    fwd_sem,
    col_rsem,
    comb_sem,
):
    n, heads, span, picks, kv_local, group = dims
    me = lax.axis_index("seq")
    hd = lax.axis_index("head")
    rows = 2 * span // heads
    width = kv_local * group * HEAD_DIM
    gwidth = group * HEAD_DIM
    scale = 1.0 / math.sqrt(HEAD_DIM)

    relay = n == 8
    z, y = me // 2, lax.rem(me, 2)
    is_end = (z == 0) | (z == 3)
    is_inner = jnp.logical_not(is_end)
    via = jnp.where(z == 0, 4, 2) + y
    served = jnp.where(z == 2, 0, 6) + y
    far_end = jnp.where(z == 2, 6, 0)
    helped = (2 * z + 1 - y, far_end + y, far_end + 1 - y)

    def far(peer):
        apart = peer // 2 - z
        return (apart >= 2) | (apart <= -2)

    def peer_is_end(peer):
        return (peer // 2 == 0) | (peer // 2 == 3)

    def only(condition, action):
        if relay:
            pl.when(condition)(action)
        else:
            action()

    fetches = [
        pltpu.make_async_copy(source, target, local_sem.at[at])
        for at, (source, target) in enumerate(((k_in, k_ref), (v_in, v_ref), (q_in, q_ref)))
    ]
    fetches.append(
        pltpu.make_async_copy(
            cot_ref.at[:, pl.ds(pl.multiple_of(hd * width, width), width)],
            do_buf.at[pl.ds(pl.multiple_of(hd * rows, rows), rows), :],
            local_sem.at[3],
        )
    )
    for fetch in fetches:
        fetch.start()

    barrier = pltpu.get_barrier_semaphore()

    def greet_seq(step, carry):
        peer = lax.rem(me + step, n)
        pl.semaphore_signal(barrier, inc=1, device_id={"seq": peer})
        return carry

    def greet_head(step, carry):
        peer = lax.rem(hd + step, heads)
        pl.semaphore_signal(barrier, inc=1, device_id={"head": peer})
        return carry

    lax.fori_loop(1, n, greet_seq, 0)
    lax.fori_loop(1, heads, greet_head, 0)

    my_second = place_ref[2 * me + 1]

    def fill_half(peer, carry):
        wants = jnp.int32(0)
        for side in range(2):
            block = place_ref[2 * peer + side]
            for pick in range(picks):
                wants = jnp.where(lists_ref[pick, block] == my_second, 1, wants)
        half_tab[peer] = wants
        return carry

    lax.fori_loop(0, n, fill_half, 0)

    pl.semaphore_wait(barrier, n - 1 + heads - 1)

    def cot_copy(peer, slot):
        return pltpu.make_async_remote_copy(
            src_ref=cot_ref.at[:, pl.ds(pl.multiple_of(peer * width, width), width)],
            dst_ref=do_buf.at[pl.ds(pl.multiple_of(slot * rows, rows), rows), :],
            send_sem=cot_ssem.at[peer],
            recv_sem=cot_rsem.at[slot],
            device_id={"head": peer},
        )

    def att_copy(peer, slot, g):
        return pltpu.make_async_remote_copy(
            src_ref=att_buf.at[
                pl.ds(pl.multiple_of(peer * rows, rows), rows), pl.ds(g * gwidth, gwidth)
            ],
            dst_ref=att_ref.at[
                :, pl.ds(pl.multiple_of(slot * width + g * gwidth, gwidth), gwidth)
            ],
            send_sem=att_ssem.at[g, peer],
            recv_sem=att_rsem.at[g, slot],
            device_id={"head": peer},
        )

    def kv_copy(peer, slot, g):
        return pltpu.make_async_remote_copy(
            src_ref=kv_send.at[g, peer],
            dst_ref=kv_recv[g].at[slot],
            send_sem=kv_ssem.at[g, peer],
            recv_sem=kv_rsem.at[g, slot],
            device_id={"seq": peer},
        )

    def grad_copy(peer, slot, g):
        return pltpu.make_async_remote_copy(
            src_ref=g_send.at[g, peer],
            dst_ref=g_recv.at[g, slot],
            send_sem=g_ssem.at[g, peer],
            recv_sem=g_rsem.at[g, slot],
            device_id={"seq": peer},
        )

    def full_copy(g):
        return pltpu.make_async_remote_copy(
            src_ref=full_send.at[g],
            dst_ref=full_recv.at[g],
            send_sem=full_sem.at[0, g],
            recv_sem=full_sem.at[1, g],
            device_id={"seq": via},
        )

    def forward_copy(g, at):
        return pltpu.make_async_remote_copy(
            src_ref=fwd_send.at[g, at],
            dst_ref=kv_recv[g].at[served],
            send_sem=fwd_sem.at[g, at],
            recv_sem=kv_rsem.at[g, served],
            device_id={"seq": helped[at]},
        )

    def collect_copy(peer, slot, g):
        through = jnp.where(peer // 2 == 0, 4, 2) + lax.rem(peer, 2)
        return pltpu.make_async_remote_copy(
            src_ref=g_send.at[g, peer],
            dst_ref=col_recv.at[g, slot],
            send_sem=g_ssem.at[g, peer],
            recv_sem=col_rsem.at[g, slot],
            device_id={"seq": through},
        )

    def combined_copy(g):
        return pltpu.make_async_remote_copy(
            src_ref=comb_send.at[g],
            dst_ref=comb_recv.at[g],
            send_sem=comb_sem.at[0, g],
            recv_sem=comb_sem.at[1, g],
            device_id={"seq": served},
        )

    def over_seq(action):
        def one(step, carry):
            action(lax.rem(me + step, n))
            return carry

        lax.fori_loop(1, n, one, 0)

    def over_head(action):
        def one(step, carry):
            action(lax.rem(hd + step, heads))
            return carry

        lax.fori_loop(1, heads, one, 0)

    over_head(lambda peer: cot_copy(peer, hd).start())
    fetches[0].wait()
    fetches[1].wait()

    def send_full(g):
        cols = slice(g * HEAD_DIM, (g + 1) * HEAD_DIM)
        if relay:

            @pl.when(is_end)
            def _():
                full_send[g, :, :HEAD_DIM] = k_ref[:, cols]
                full_send[g, :, HEAD_DIM:] = v_ref[:, cols]
                full_copy(g).start()

    def send_keys(g):
        cols = slice(g * HEAD_DIM, (g + 1) * HEAD_DIM)

        def send_kv(peer):
            second = half_tab[peer] == 1
            kv_send[g, peer, :, :HEAD_DIM] = jnp.where(second, k_ref[span:, cols], k_ref[:span, cols])
            kv_send[g, peer, :, HEAD_DIM:] = jnp.where(second, v_ref[span:, cols], v_ref[:span, cols])

            only(jnp.logical_not(is_end & far(peer)), kv_copy(peer, me, g).start)

        over_seq(send_kv)

    def relay_keys(g):
        if relay:

            @pl.when(is_inner)
            def _():
                full_copy(g).wait_recv()
                for at in range(4):
                    second = sel_tab[at] == 1
                    block = jnp.where(second, full_recv[g, span:], full_recv[g, :span])
                    if at < 3:
                        fwd_send[g, at] = block
                        forward_copy(g, at).start()
                    else:
                        kv_recv[g][served] = block

    for g in range(kv_local):
        send_full(g)
    for g in range(kv_local):
        send_keys(g)

    if relay:
        end_second = place_ref[2 * served + 1]
        for at, who in enumerate(helped + (me,)):
            wants = jnp.int32(0)
            for side in range(2):
                block = place_ref[2 * who + side]
                for pick in range(picks):
                    wants = jnp.where(lists_ref[pick, block] == end_second, 1, wants)
            sel_tab[at] = wants

    spare = lax.rem(me + 1, n)
    for side in range(2):
        own = place_ref[2 * me + side]
        blocks = [lists_ref[pick, own] for pick in range(picks)]
        for pick in range(picks):
            block = blocks[pick]
            valid = jnp.where(block != own, 1, 0)
            for before in range(pick):
                valid = jnp.where(block == blocks[before], 0, valid)

            def find(at, owner, block=block):
                hit = (place_ref[2 * at] == block) | (place_ref[2 * at + 1] == block)
                return jnp.where(hit, at, owner)

            owner = lax.fori_loop(0, n, find, jnp.int32(0))
            owner_tab[side * picks + pick] = jnp.where(valid == 1, owner, spare)
            valid_tab[side * picks + pick] = valid

    for g in range(kv_local):
        relay_keys(g)
    fetches[2].wait()
    fetches[3].wait()
    over_head(lambda peer: cot_copy(hd, peer).wait_recv())

    pair = 2
    lanes = pair * span
    key_at = lax.broadcasted_iota(jnp.int32, (span, lanes), 0)
    query_at = lax.rem(lax.broadcasted_iota(jnp.int32, (span, lanes), 1), span)
    causal = key_at <= query_at

    for g in range(kv_local):
        cols = slice(g * HEAD_DIM, (g + 1) * HEAD_DIM)
        over_seq(
            lambda peer, g=g: only(
                jnp.logical_not(is_inner & (peer == served)), kv_copy(me, peer, g).wait_recv
            )
        )

        def attend(side, carry, g=g, cols=cols):
            base = pl.multiple_of(side * span, span)
            here = pl.ds(base, span)
            keys = [k_ref[here, cols]]
            values = [v_ref[here, cols]]
            valid = []
            for pick in range(picks):
                owner = owner_tab[side * picks + pick]
                keys.append(kv_recv[g][owner, :, :HEAD_DIM])
                values.append(kv_recv[g][owner, :, HEAD_DIM:])
                valid.append(valid_tab[side * picks + pick] == 1)
            keys = jnp.concatenate(keys, axis=0)
            values = jnp.concatenate(values, axis=0)
            key_sum = None
            for chunk in range(group // pair):
                first = g * group + chunk * pair
                spots = [
                    slice((first + at) * HEAD_DIM, (first + at + 1) * HEAD_DIM)
                    for at in range(pair)
                ]
                query = jnp.concatenate([q_ref[here, spot] for spot in spots], axis=0)
                grad = jnp.concatenate([do_buf[here, spot] for spot in spots], axis=0)
                scores = dot(keys, query, 1, 1)
                pieces = [
                    scores[at * span : (at + 1) * span] for at in range(picks + 1)
                ]
                pieces[0] = jnp.where(causal, pieces[0], HIDDEN)
                tops = [jnp.max(piece, axis=0, keepdims=True) for piece in pieces]
                top = tops[0]
                for pick in range(picks):
                    top = jnp.maximum(top, jnp.where(valid[pick], tops[pick + 1], HIDDEN))
                probs = [jnp.exp2((pieces[0] - top) * (scale * LOG2_E))]
                for pick in range(picks):
                    above = jnp.where(valid[pick], top, -HIDDEN)
                    probs.append(jnp.exp2((pieces[pick + 1] - above) * (scale * LOG2_E)))
                probs = jnp.concatenate(probs, axis=0)
                total = jnp.sum(probs, axis=0, keepdims=True)
                probs = probs * (1.0 / total)
                weights = probs.astype(jnp.bfloat16)
                attended = dot(values, weights, 0, 0)
                slopes = dot(values, grad, 1, 1)
                delta = jnp.sum(probs * slopes, axis=0, keepdims=True)
                dscores = (probs * (slopes - delta)).astype(jnp.bfloat16)
                query_grad = dot(keys, dscores, 0, 0)
                attended = attended.T.astype(jnp.bfloat16)
                query_grad = (query_grad * scale).T.astype(jnp.bfloat16)
                for at in range(pair):
                    att_buf[here, spots[at]] = attended[at * span : (at + 1) * span]
                    qg_ref[here, spots[at]] = query_grad[at * span : (at + 1) * span]
                key_part = dot(dscores, query, 1, 0)
                value_part = dot(weights, grad, 1, 0)
                if key_sum is None:
                    key_sum, value_sum = key_part, value_part
                else:
                    key_sum, value_sum = key_sum + key_part, value_sum + value_part
            key_sum = key_sum * scale
            own_acc[g, side, :, :HEAD_DIM] = key_sum[:span]
            own_acc[g, side, :, HEAD_DIM:] = value_sum[:span]
            for pick in range(picks):
                piece = slice((pick + 1) * span, (pick + 2) * span)
                parts[g, side * picks + pick, :, :HEAD_DIM] = key_sum[piece].astype(jnp.bfloat16)
                parts[g, side * picks + pick, :, HEAD_DIM:] = value_sum[piece].astype(jnp.bfloat16)
            return carry

        for side in range(2):
            attend(side, 0)

        def stage_grad(peer, g=g):
            spot = jnp.int32(0)
            found = jnp.int32(0)
            for at in range(2 * picks):
                hit = (owner_tab[at] == peer) & (valid_tab[at] == 1)
                spot = jnp.where(hit, at, spot)
                found = jnp.where(hit, 1, found)
            part = parts[g, spot]
            g_send[g, peer] = jnp.where(found == 1, part, jnp.zeros_like(part))

        def send_through(peer, g=g):
            @pl.when(peer_is_end(peer) & far(peer))
            def _():
                stage_grad(peer)
                slot = jnp.where(is_inner, 0, jnp.where(lax.rem(peer, 2) == y, 1, 2))

                @pl.when(jnp.logical_not(is_inner & (peer == served)))
                def _():
                    collect_copy(peer, slot, g).start()

        def send_direct(peer, g=g):
            def go():
                stage_grad(peer)
                grad_copy(peer, me, g).start()

            only(jnp.logical_not(peer_is_end(peer) & far(peer)), go)

        if relay:
            over_seq(send_through)
        over_seq(send_direct)
        over_head(lambda peer, g=g: att_copy(peer, hd, g).start())

    if relay:
        for g in range(kv_local):

            @pl.when(is_inner)
            def _(g=g):
                sums = [jnp.zeros((span, 2 * HEAD_DIM), jnp.float32)] * 2
                for at in range(4):
                    if at < 3:
                        collect_copy(served, at, g).wait_recv()
                        part = col_recv[g, at].astype(jnp.float32)
                    else:
                        part = g_send[g, served].astype(jnp.float32)
                    second = sel_tab[at] == 1
                    sums[0] = sums[0] + jnp.where(second, 0.0, part)
                    sums[1] = sums[1] + jnp.where(second, part, 0.0)
                for side in range(2):
                    comb_send[g, side] = sums[side].astype(jnp.bfloat16)
                combined_copy(g).start()

    leaving = [
        pltpu.make_async_copy(source, target, local_sem.at[at])
        for at, (source, target) in enumerate(
            (
                (
                    att_buf.at[pl.ds(pl.multiple_of(hd * rows, rows), rows), :],
                    att_ref.at[:, pl.ds(pl.multiple_of(hd * width, width), width)],
                ),
                (qg_ref, qg_out),
                (kg_ref, kg_out),
                (vg_ref, vg_out),
            )
        )
    ]
    leaving[0].start()
    leaving[1].start()

    for g in range(kv_local):
        cols = slice(g * HEAD_DIM, (g + 1) * HEAD_DIM)

        def add_grad(peer, g=g):
            def arrived():
                grad_copy(me, peer, g).wait_recv()
                part = g_recv[g, peer].astype(jnp.float32)
                second = half_tab[peer] == 1
                own_acc[g, 0] += jnp.where(second, 0.0, part)
                own_acc[g, 1] += jnp.where(second, part, 0.0)

            only(jnp.logical_not(is_end & far(peer)), arrived)

        over_seq(add_grad)
        if relay:

            @pl.when(is_end)
            def _(g=g):
                combined_copy(g).wait_recv()
                for side in range(2):
                    own_acc[g, side] += comb_recv[g, side].astype(jnp.float32)

        for side in range(2):
            here = slice(side * span, (side + 1) * span)
            kg_ref[here, cols] = own_acc[g, side, :, :HEAD_DIM].astype(jnp.bfloat16)
            vg_ref[here, cols] = own_acc[g, side, :, HEAD_DIM:].astype(jnp.bfloat16)

    leaving[2].start()
    leaving[3].start()
    over_head(lambda peer: cot_copy(peer, hd).wait_send())
    for g in range(kv_local):
        over_head(lambda peer, g=g: att_copy(hd, peer, g).wait_recv())
        over_head(lambda peer, g=g: att_copy(peer, hd, g).wait_send())
        over_seq(
            lambda peer, g=g: only(
                jnp.logical_not(is_end & far(peer)), kv_copy(peer, me, g).wait_send
            )
        )
        over_seq(
            lambda peer, g=g: only(
                jnp.logical_not(is_inner & (peer == served)), grad_copy(peer, me, g).wait_send
            )
        )
        if relay:

            pl.when(is_end)(full_copy(g).wait_send)

            @pl.when(is_inner)
            def _(g=g):
                for at in range(3):
                    forward_copy(g, at).wait_send()
                combined_copy(g).wait_send()

    for copy in leaving:
        copy.wait()


def write_out(*refs):
    sources, targets, stages, sems = refs[:4], refs[4:8], refs[8:12], refs[12]
    arrive = []
    leave = []
    for source, target, stage in zip(sources, targets, stages):
        piece = source.shape[0] // CHUNKS
        for at in range(CHUNKS):
            rows = slice(at * piece, (at + 1) * piece)
            spot = len(arrive)
            arrive.append(
                pltpu.make_async_copy(source.at[rows], stage.at[rows], sems.at[0, spot])
            )
            leave.append(
                pltpu.make_async_copy(stage.at[rows], target.at[rows], sems.at[1, spot])
            )
    for copy in arrive:
        copy.start()
    for came, goes in zip(arrive, leave):
        came.wait()
        goes.start()
    for copy in leave:
        copy.wait()


def body(queries, key_rows, value_rows, span_place, block_lists, cotangent):
    n = lax.axis_size("seq")
    heads = lax.axis_size("head")
    span = queries.shape[0] // 2
    picks = block_lists.shape[1]
    kv_local = key_rows.shape[1] // HEAD_DIM
    group = queries.shape[1] // key_rows.shape[1]
    bf16 = jnp.bfloat16
    hbm = pl.BlockSpec(memory_space=pltpu.HBM)
    smem = pl.BlockSpec(memory_space=pltpu.SMEM)
    box = (kv_local, n, span, 2 * HEAD_DIM)
    dma = pltpu.SemaphoreType.DMA
    flops = 6 * 2 * 2 * span * span * (picks + 1) * queries.shape[1]
    results = pl.pallas_call(
        functools.partial(kernel, (n, heads, span, picks, kv_local, group)),
        out_shape=[
            jax.ShapeDtypeStruct(cotangent.shape, bf16),
            jax.ShapeDtypeStruct(queries.shape, bf16),
            jax.ShapeDtypeStruct(key_rows.shape, bf16),
            jax.ShapeDtypeStruct(value_rows.shape, bf16),
        ],
        in_specs=[smem, smem, hbm, hbm, hbm, hbm],
        out_specs=[hbm] * 4,
        scratch_shapes=[
            pltpu.SMEM((n,), jnp.int32),
            pltpu.SMEM((2 * picks,), jnp.int32),
            pltpu.SMEM((2 * picks,), jnp.int32),
            pltpu.VMEM(queries.shape, bf16),
            pltpu.VMEM(key_rows.shape, bf16),
            pltpu.VMEM(value_rows.shape, bf16),
            pltpu.VMEM(queries.shape, bf16),
            pltpu.VMEM(key_rows.shape, bf16),
            pltpu.VMEM(value_rows.shape, bf16),
            pltpu.VMEM(queries.shape, bf16),
            pltpu.VMEM(queries.shape, bf16),
            pltpu.VMEM(box, bf16),
            [pltpu.VMEM(box[1:], bf16)] * kv_local,
            pltpu.VMEM(box, bf16),
            pltpu.VMEM(box, bf16),
            pltpu.VMEM((kv_local, 2 * picks, span, 2 * HEAD_DIM), bf16),
            pltpu.VMEM((kv_local, 2, span, 2 * HEAD_DIM), jnp.float32),
            dma((4,)),
            dma((heads,)),
            dma((heads,)),
            dma((kv_local, heads)),
            dma((kv_local, heads)),
            dma((kv_local, n)),
            dma((kv_local, n)),
            dma((kv_local, n)),
            dma((kv_local, n)),
            pltpu.SMEM((4,), jnp.int32),
            pltpu.VMEM((kv_local, 2 * span, 2 * HEAD_DIM), bf16),
            pltpu.VMEM((kv_local, 2 * span, 2 * HEAD_DIM), bf16),
            pltpu.VMEM((kv_local, 3, span, 2 * HEAD_DIM), bf16),
            pltpu.VMEM((kv_local, 3, span, 2 * HEAD_DIM), bf16),
            pltpu.VMEM((kv_local, 2, span, 2 * HEAD_DIM), bf16),
            pltpu.VMEM((kv_local, 2, span, 2 * HEAD_DIM), bf16),
            dma((2, kv_local)),
            dma((kv_local, 3)),
            dma((kv_local, 3)),
            dma((2, kv_local)),
        ],
        compiler_params=pltpu.CompilerParams(
            collective_id=0, has_side_effects=True, vmem_limit_bytes=VMEM_BYTES
        ),
        cost_estimate=pl.CostEstimate(
            flops=flops, bytes_accessed=4 * queries.size * 2, transcendentals=flops // 1536
        ),
    )(span_place, block_lists.T, queries, key_rows, value_rows, cotangent)
    return tuple(
        pl.pallas_call(
            write_out,
            out_shape=[jax.ShapeDtypeStruct(item.shape, item.dtype) for item in results],
            in_specs=[hbm] * 4,
            out_specs=[hbm] * 4,
            scratch_shapes=[pltpu.VMEM(item.shape, item.dtype) for item in results]
            + [dma((2, 4 * CHUNKS))],
            compiler_params=pltpu.CompilerParams(vmem_limit_bytes=VMEM_BYTES),
        )(*results)
    )


def solution(mesh):
    in_specs = (
        P("seq", "head"),
        P("seq", "head"),
        P("seq", "head"),
        P(),
        P(),
        P(("seq", "head"), None),
    )
    out_specs = (P(("seq", "head"), None), P("seq", "head"), P("seq", "head"), P("seq", "head"))
    return jax.shard_map(body, mesh=mesh, in_specs=in_specs, out_specs=out_specs, check_vma=False)
```

```python
import functools
import math

import jax
import jax.numpy as jnp
from jax import lax
from jax.experimental import pallas as pl
from jax.experimental.pallas import tpu as pltpu
from jax.sharding import PartitionSpec as P

HEAD_DIM = 128
HIDDEN = -1e30
CHUNKS = 4
LOG2_E = math.log2(math.e)
VMEM_BYTES = 64 * 1024 * 1024


def dot(left, right, left_dim, right_dim):
    return lax.dot_general(
        left, right, (((left_dim,), (right_dim,)), ((), ())), preferred_element_type=jnp.float32
    )


def kernel(
    dims,
    place_ref,
    lists_ref,
    q_in,
    k_in,
    v_in,
    cot_ref,
    att_ref,
    qg_out,
    kg_out,
    vg_out,
    half_tab,
    owner_tab,
    valid_tab,
    q_ref,
    k_ref,
    v_ref,
    qg_ref,
    kg_ref,
    vg_ref,
    do_buf,
    att_buf,
    kv_send,
    kv_recv,
    g_send,
    g_recv,
    parts,
    own_acc,
    local_sem,
    cot_ssem,
    cot_rsem,
    att_ssem,
    att_rsem,
    kv_ssem,
    kv_rsem,
    g_ssem,
    g_rsem,
    sel_tab,
    full_send,
    full_recv,
    fwd_send,
    col_recv,
    comb_send,
    comb_recv,
    full_sem,
    fwd_sem,
    col_rsem,
    comb_sem,
):
    n, heads, span, picks, kv_local, group = dims
    me = lax.axis_index("seq")
    hd = lax.axis_index("head")
    rows = 2 * span // heads
    width = kv_local * group * HEAD_DIM
    gwidth = group * HEAD_DIM
    scale = 1.0 / math.sqrt(HEAD_DIM)

    relay = n == 8
    z, y = me // 2, lax.rem(me, 2)
    is_end = (z == 0) | (z == 3)
    is_inner = jnp.logical_not(is_end)
    via = jnp.where(z == 0, 4, 2) + y
    served = jnp.where(z == 2, 0, 6) + y
    far_end = jnp.where(z == 2, 6, 0)
    helped = (2 * z + 1 - y, far_end + y, far_end + 1 - y)

    def far(peer):
        apart = peer // 2 - z
        return (apart >= 2) | (apart <= -2)

    def peer_is_end(peer):
        return (peer // 2 == 0) | (peer // 2 == 3)

    def only(condition, action):
        if relay:
            pl.when(condition)(action)
        else:
            action()

    fetches = [
        pltpu.make_async_copy(source, target, local_sem.at[at])
        for at, (source, target) in enumerate(((k_in, k_ref), (v_in, v_ref), (q_in, q_ref)))
    ]
    fetches.append(
        pltpu.make_async_copy(
            cot_ref.at[:, pl.ds(pl.multiple_of(hd * width, width), width)],
            do_buf.at[pl.ds(pl.multiple_of(hd * rows, rows), rows), :],
            local_sem.at[3],
        )
    )
    for fetch in fetches:
        fetch.start()

    barrier = pltpu.get_barrier_semaphore()

    def greet_seq(step, carry):
        peer = lax.rem(me + step, n)
        pl.semaphore_signal(barrier, inc=1, device_id={"seq": peer})
        return carry

    def greet_head(step, carry):
        peer = lax.rem(hd + step, heads)
        pl.semaphore_signal(barrier, inc=1, device_id={"head": peer})
        return carry

    lax.fori_loop(1, n, greet_seq, 0)
    lax.fori_loop(1, heads, greet_head, 0)

    my_second = place_ref[2 * me + 1]

    def fill_half(peer, carry):
        wants = jnp.int32(0)
        for side in range(2):
            block = place_ref[2 * peer + side]
            for pick in range(picks):
                wants = jnp.where(lists_ref[pick, block] == my_second, 1, wants)
        half_tab[peer] = wants
        return carry

    lax.fori_loop(0, n, fill_half, 0)

    pl.semaphore_wait(barrier, n - 1 + heads - 1)

    def cot_copy(peer, slot):
        return pltpu.make_async_remote_copy(
            src_ref=cot_ref.at[:, pl.ds(pl.multiple_of(peer * width, width), width)],
            dst_ref=do_buf.at[pl.ds(pl.multiple_of(slot * rows, rows), rows), :],
            send_sem=cot_ssem.at[peer],
            recv_sem=cot_rsem.at[slot],
            device_id={"head": peer},
        )

    def att_copy(peer, slot, g):
        return pltpu.make_async_remote_copy(
            src_ref=att_buf.at[
                pl.ds(pl.multiple_of(peer * rows, rows), rows), pl.ds(g * gwidth, gwidth)
            ],
            dst_ref=att_ref.at[
                :, pl.ds(pl.multiple_of(slot * width + g * gwidth, gwidth), gwidth)
            ],
            send_sem=att_ssem.at[g, peer],
            recv_sem=att_rsem.at[g, slot],
            device_id={"head": peer},
        )

    def kv_copy(peer, slot, g):
        return pltpu.make_async_remote_copy(
            src_ref=kv_send.at[g, peer],
            dst_ref=kv_recv[g].at[slot],
            send_sem=kv_ssem.at[g, peer],
            recv_sem=kv_rsem.at[g, slot],
            device_id={"seq": peer},
        )

    def grad_copy(peer, slot, g):
        return pltpu.make_async_remote_copy(
            src_ref=g_send.at[g, peer],
            dst_ref=g_recv.at[g, slot],
            send_sem=g_ssem.at[g, peer],
            recv_sem=g_rsem.at[g, slot],
            device_id={"seq": peer},
        )

    def full_copy(g):
        return pltpu.make_async_remote_copy(
            src_ref=full_send.at[g],
            dst_ref=full_recv.at[g],
            send_sem=full_sem.at[0, g],
            recv_sem=full_sem.at[1, g],
            device_id={"seq": via},
        )

    def forward_copy(g, at):
        return pltpu.make_async_remote_copy(
            src_ref=fwd_send.at[g, at],
            dst_ref=kv_recv[g].at[served],
            send_sem=fwd_sem.at[g, at],
            recv_sem=kv_rsem.at[g, served],
            device_id={"seq": helped[at]},
        )

    def collect_copy(peer, slot, g):
        through = jnp.where(peer // 2 == 0, 4, 2) + lax.rem(peer, 2)
        return pltpu.make_async_remote_copy(
            src_ref=g_send.at[g, peer],
            dst_ref=col_recv.at[g, slot],
            send_sem=g_ssem.at[g, peer],
            recv_sem=col_rsem.at[g, slot],
            device_id={"seq": through},
        )

    def combined_copy(g):
        return pltpu.make_async_remote_copy(
            src_ref=comb_send.at[g],
            dst_ref=comb_recv.at[g],
            send_sem=comb_sem.at[0, g],
            recv_sem=comb_sem.at[1, g],
            device_id={"seq": served},
        )

    def over_seq(action):
        def one(step, carry):
            action(lax.rem(me + step, n))
            return carry

        lax.fori_loop(1, n, one, 0)

    def over_head(action):
        def one(step, carry):
            action(lax.rem(hd + step, heads))
            return carry

        lax.fori_loop(1, heads, one, 0)

    over_head(lambda peer: cot_copy(peer, hd).start())
    fetches[0].wait()
    fetches[1].wait()

    def send_full(g):
        cols = slice(g * HEAD_DIM, (g + 1) * HEAD_DIM)
        if relay:

            @pl.when(is_end)
            def _():
                full_send[g, :, :HEAD_DIM] = k_ref[:, cols]
                full_send[g, :, HEAD_DIM:] = v_ref[:, cols]
                full_copy(g).start()

    def send_keys(g):
        cols = slice(g * HEAD_DIM, (g + 1) * HEAD_DIM)

        def send_kv(peer):
            second = half_tab[peer] == 1
            kv_send[g, peer, :, :HEAD_DIM] = jnp.where(second, k_ref[span:, cols], k_ref[:span, cols])
            kv_send[g, peer, :, HEAD_DIM:] = jnp.where(second, v_ref[span:, cols], v_ref[:span, cols])

            only(jnp.logical_not(is_end & far(peer)), kv_copy(peer, me, g).start)

        over_seq(send_kv)

    def relay_keys(g):
        if relay:

            @pl.when(is_inner)
            def _():
                full_copy(g).wait_recv()
                for at in range(4):
                    second = sel_tab[at] == 1
                    block = jnp.where(second, full_recv[g, span:], full_recv[g, :span])
                    if at < 3:
                        fwd_send[g, at] = block
                        forward_copy(g, at).start()
                    else:
                        kv_recv[g][served] = block

    for g in range(kv_local):
        send_full(g)
    for g in range(kv_local):
        send_keys(g)

    if relay:
        end_second = place_ref[2 * served + 1]
        for at, who in enumerate(helped + (me,)):
            wants = jnp.int32(0)
            for side in range(2):
                block = place_ref[2 * who + side]
                for pick in range(picks):
                    wants = jnp.where(lists_ref[pick, block] == end_second, 1, wants)
            sel_tab[at] = wants

    spare = lax.rem(me + 1, n)
    for side in range(2):
        own = place_ref[2 * me + side]
        blocks = [lists_ref[pick, own] for pick in range(picks)]
        for pick in range(picks):
            block = blocks[pick]
            valid = jnp.where(block != own, 1, 0)
            for before in range(pick):
                valid = jnp.where(block == blocks[before], 0, valid)

            def find(at, owner, block=block):
                hit = (place_ref[2 * at] == block) | (place_ref[2 * at + 1] == block)
                return jnp.where(hit, at, owner)

            owner = lax.fori_loop(0, n, find, jnp.int32(0))
            owner_tab[side * picks + pick] = jnp.where(valid == 1, owner, spare)
            valid_tab[side * picks + pick] = valid

    for g in range(kv_local):
        relay_keys(g)
    fetches[2].wait()
    fetches[3].wait()
    over_head(lambda peer: cot_copy(hd, peer).wait_recv())

    pair = 2
    lanes = pair * span
    key_at = lax.broadcasted_iota(jnp.int32, (span, lanes), 0)
    query_at = lax.rem(lax.broadcasted_iota(jnp.int32, (span, lanes), 1), span)
    causal = key_at <= query_at

    for g in range(kv_local):
        cols = slice(g * HEAD_DIM, (g + 1) * HEAD_DIM)
        over_seq(
            lambda peer, g=g: only(
                jnp.logical_not(is_inner & (peer == served)), kv_copy(me, peer, g).wait_recv
            )
        )

        def attend(side, carry, g=g, cols=cols):
            base = pl.multiple_of(side * span, span)
            here = pl.ds(base, span)
            keys = [k_ref[here, cols]]
            values = [v_ref[here, cols]]
            valid = []
            for pick in range(picks):
                owner = owner_tab[side * picks + pick]
                keys.append(kv_recv[g][owner, :, :HEAD_DIM])
                values.append(kv_recv[g][owner, :, HEAD_DIM:])
                valid.append(valid_tab[side * picks + pick] == 1)
            keys = jnp.concatenate(keys, axis=0)
            values = jnp.concatenate(values, axis=0)
            key_sum = None
            for chunk in range(group // pair):
                first = g * group + chunk * pair
                spots = [
                    slice((first + at) * HEAD_DIM, (first + at + 1) * HEAD_DIM)
                    for at in range(pair)
                ]
                query = jnp.concatenate([q_ref[here, spot] for spot in spots], axis=0)
                grad = jnp.concatenate([do_buf[here, spot] for spot in spots], axis=0)
                scores = dot(keys, query, 1, 1)
                pieces = [
                    scores[at * span : (at + 1) * span] for at in range(picks + 1)
                ]
                pieces[0] = jnp.where(causal, pieces[0], HIDDEN)
                tops = [jnp.max(piece, axis=0, keepdims=True) for piece in pieces]
                top = tops[0]
                for pick in range(picks):
                    top = jnp.maximum(top, jnp.where(valid[pick], tops[pick + 1], HIDDEN))
                probs = [jnp.exp2((pieces[0] - top) * (scale * LOG2_E))]
                for pick in range(picks):
                    above = jnp.where(valid[pick], top, -HIDDEN)
                    probs.append(jnp.exp2((pieces[pick + 1] - above) * (scale * LOG2_E)))
                probs = jnp.concatenate(probs, axis=0)
                total = jnp.sum(probs, axis=0, keepdims=True)
                probs = probs * (1.0 / total)
                weights = probs.astype(jnp.bfloat16)
                attended = dot(values, weights, 0, 0)
                slopes = dot(values, grad, 1, 1)
                delta = jnp.sum(probs * slopes, axis=0, keepdims=True)
                dscores = (probs * (slopes - delta)).astype(jnp.bfloat16)
                query_grad = dot(keys, dscores, 0, 0)
                attended = attended.T.astype(jnp.bfloat16)
                query_grad = (query_grad * scale).T.astype(jnp.bfloat16)
                for at in range(pair):
                    att_buf[here, spots[at]] = attended[at * span : (at + 1) * span]
                    qg_ref[here, spots[at]] = query_grad[at * span : (at + 1) * span]
                key_part = dot(dscores, query, 1, 0)
                value_part = dot(weights, grad, 1, 0)
                if key_sum is None:
                    key_sum, value_sum = key_part, value_part
                else:
                    key_sum, value_sum = key_sum + key_part, value_sum + value_part
            key_sum = key_sum * scale
            own_acc[g, side, :, :HEAD_DIM] = key_sum[:span]
            own_acc[g, side, :, HEAD_DIM:] = value_sum[:span]
            for pick in range(picks):
                piece = slice((pick + 1) * span, (pick + 2) * span)
                parts[g, side * picks + pick, :, :HEAD_DIM] = key_sum[piece].astype(jnp.bfloat16)
                parts[g, side * picks + pick, :, HEAD_DIM:] = value_sum[piece].astype(jnp.bfloat16)
            return carry

        lax.fori_loop(0, 2, attend, 0)

        def stage_grad(peer, g=g):
            spot = jnp.int32(0)
            found = jnp.int32(0)
            for at in range(2 * picks):
                hit = (owner_tab[at] == peer) & (valid_tab[at] == 1)
                spot = jnp.where(hit, at, spot)
                found = jnp.where(hit, 1, found)
            part = parts[g, spot]
            g_send[g, peer] = jnp.where(found == 1, part, jnp.zeros_like(part))

        def send_through(peer, g=g):
            @pl.when(peer_is_end(peer) & far(peer))
            def _():
                stage_grad(peer)
                slot = jnp.where(is_inner, 0, jnp.where(lax.rem(peer, 2) == y, 1, 2))

                @pl.when(jnp.logical_not(is_inner & (peer == served)))
                def _():
                    collect_copy(peer, slot, g).start()

        def send_direct(peer, g=g):
            def go():
                stage_grad(peer)
                grad_copy(peer, me, g).start()

            only(jnp.logical_not(peer_is_end(peer) & far(peer)), go)

        if relay:
            over_seq(send_through)
        over_seq(send_direct)
        over_head(lambda peer, g=g: att_copy(peer, hd, g).start())

    if relay:
        for g in range(kv_local):

            @pl.when(is_inner)
            def _(g=g):
                sums = [jnp.zeros((span, 2 * HEAD_DIM), jnp.float32)] * 2
                for at in range(4):
                    if at < 3:
                        collect_copy(served, at, g).wait_recv()
                        part = col_recv[g, at].astype(jnp.float32)
                    else:
                        part = g_send[g, served].astype(jnp.float32)
                    second = sel_tab[at] == 1
                    sums[0] = sums[0] + jnp.where(second, 0.0, part)
                    sums[1] = sums[1] + jnp.where(second, part, 0.0)
                for side in range(2):
                    comb_send[g, side] = sums[side].astype(jnp.bfloat16)
                combined_copy(g).start()

    leaving = [
        pltpu.make_async_copy(source, target, local_sem.at[at])
        for at, (source, target) in enumerate(
            (
                (
                    att_buf.at[pl.ds(pl.multiple_of(hd * rows, rows), rows), :],
                    att_ref.at[:, pl.ds(pl.multiple_of(hd * width, width), width)],
                ),
                (qg_ref, qg_out),
                (kg_ref, kg_out),
                (vg_ref, vg_out),
            )
        )
    ]
    leaving[0].start()
    leaving[1].start()

    for g in range(kv_local):
        cols = slice(g * HEAD_DIM, (g + 1) * HEAD_DIM)

        def add_grad(peer, g=g):
            def arrived():
                grad_copy(me, peer, g).wait_recv()
                part = g_recv[g, peer].astype(jnp.float32)
                second = half_tab[peer] == 1
                own_acc[g, 0] += jnp.where(second, 0.0, part)
                own_acc[g, 1] += jnp.where(second, part, 0.0)

            only(jnp.logical_not(is_end & far(peer)), arrived)

        over_seq(add_grad)
        if relay:

            @pl.when(is_end)
            def _(g=g):
                combined_copy(g).wait_recv()
                for side in range(2):
                    own_acc[g, side] += comb_recv[g, side].astype(jnp.float32)

        for side in range(2):
            here = slice(side * span, (side + 1) * span)
            kg_ref[here, cols] = own_acc[g, side, :, :HEAD_DIM].astype(jnp.bfloat16)
            vg_ref[here, cols] = own_acc[g, side, :, HEAD_DIM:].astype(jnp.bfloat16)

    leaving[2].start()
    leaving[3].start()
    over_head(lambda peer: cot_copy(peer, hd).wait_send())
    for g in range(kv_local):
        over_head(lambda peer, g=g: att_copy(hd, peer, g).wait_recv())
        over_head(lambda peer, g=g: att_copy(peer, hd, g).wait_send())
        over_seq(
            lambda peer, g=g: only(
                jnp.logical_not(is_end & far(peer)), kv_copy(peer, me, g).wait_send
            )
        )
        over_seq(
            lambda peer, g=g: only(
                jnp.logical_not(is_inner & (peer == served)), grad_copy(peer, me, g).wait_send
            )
        )
        if relay:

            pl.when(is_end)(full_copy(g).wait_send)

            @pl.when(is_inner)
            def _(g=g):
                for at in range(3):
                    forward_copy(g, at).wait_send()
                combined_copy(g).wait_send()

    for copy in leaving:
        copy.wait()


def write_out(*refs):
    sources, targets, stages, sems = refs[:4], refs[4:8], refs[8:12], refs[12]
    arrive = []
    leave = []
    for source, target, stage in zip(sources, targets, stages):
        piece = source.shape[0] // CHUNKS
        for at in range(CHUNKS):
            rows = slice(at * piece, (at + 1) * piece)
            spot = len(arrive)
            arrive.append(
                pltpu.make_async_copy(source.at[rows], stage.at[rows], sems.at[0, spot])
            )
            leave.append(
                pltpu.make_async_copy(stage.at[rows], target.at[rows], sems.at[1, spot])
            )
    for copy in arrive:
        copy.start()
    for came, goes in zip(arrive, leave):
        came.wait()
        goes.start()
    for copy in leave:
        copy.wait()


def body(queries, key_rows, value_rows, span_place, block_lists, cotangent):
    n = lax.axis_size("seq")
    heads = lax.axis_size("head")
    span = queries.shape[0] // 2
    picks = block_lists.shape[1]
    kv_local = key_rows.shape[1] // HEAD_DIM
    group = queries.shape[1] // key_rows.shape[1]
    bf16 = jnp.bfloat16
    hbm = pl.BlockSpec(memory_space=pltpu.HBM)
    smem = pl.BlockSpec(memory_space=pltpu.SMEM)
    box = (kv_local, n, span, 2 * HEAD_DIM)
    dma = pltpu.SemaphoreType.DMA
    flops = 6 * 2 * 2 * span * span * (picks + 1) * queries.shape[1]
    results = pl.pallas_call(
        functools.partial(kernel, (n, heads, span, picks, kv_local, group)),
        out_shape=[
            jax.ShapeDtypeStruct(cotangent.shape, bf16),
            jax.ShapeDtypeStruct(queries.shape, bf16),
            jax.ShapeDtypeStruct(key_rows.shape, bf16),
            jax.ShapeDtypeStruct(value_rows.shape, bf16),
        ],
        in_specs=[smem, smem, hbm, hbm, hbm, hbm],
        out_specs=[hbm] * 4,
        scratch_shapes=[
            pltpu.SMEM((n,), jnp.int32),
            pltpu.SMEM((2 * picks,), jnp.int32),
            pltpu.SMEM((2 * picks,), jnp.int32),
            pltpu.VMEM(queries.shape, bf16),
            pltpu.VMEM(key_rows.shape, bf16),
            pltpu.VMEM(value_rows.shape, bf16),
            pltpu.VMEM(queries.shape, bf16),
            pltpu.VMEM(key_rows.shape, bf16),
            pltpu.VMEM(value_rows.shape, bf16),
            pltpu.VMEM(queries.shape, bf16),
            pltpu.VMEM(queries.shape, bf16),
            pltpu.VMEM(box, bf16),
            [pltpu.VMEM(box[1:], bf16)] * kv_local,
            pltpu.VMEM(box, bf16),
            pltpu.VMEM(box, bf16),
            pltpu.VMEM((kv_local, 2 * picks, span, 2 * HEAD_DIM), bf16),
            pltpu.VMEM((kv_local, 2, span, 2 * HEAD_DIM), jnp.float32),
            dma((4,)),
            dma((heads,)),
            dma((heads,)),
            dma((kv_local, heads)),
            dma((kv_local, heads)),
            dma((kv_local, n)),
            dma((kv_local, n)),
            dma((kv_local, n)),
            dma((kv_local, n)),
            pltpu.SMEM((4,), jnp.int32),
            pltpu.VMEM((kv_local, 2 * span, 2 * HEAD_DIM), bf16),
            pltpu.VMEM((kv_local, 2 * span, 2 * HEAD_DIM), bf16),
            pltpu.VMEM((kv_local, 3, span, 2 * HEAD_DIM), bf16),
            pltpu.VMEM((kv_local, 3, span, 2 * HEAD_DIM), bf16),
            pltpu.VMEM((kv_local, 2, span, 2 * HEAD_DIM), bf16),
            pltpu.VMEM((kv_local, 2, span, 2 * HEAD_DIM), bf16),
            dma((2, kv_local)),
            dma((kv_local, 3)),
            dma((kv_local, 3)),
            dma((2, kv_local)),
        ],
        compiler_params=pltpu.CompilerParams(
            collective_id=0, has_side_effects=True, vmem_limit_bytes=VMEM_BYTES
        ),
        cost_estimate=pl.CostEstimate(
            flops=flops, bytes_accessed=4 * queries.size * 2, transcendentals=flops // 1536
        ),
    )(span_place, block_lists.T, queries, key_rows, value_rows, cotangent)
    return tuple(
        pl.pallas_call(
            write_out,
            out_shape=[jax.ShapeDtypeStruct(item.shape, item.dtype) for item in results],
            in_specs=[hbm] * 4,
            out_specs=[hbm] * 4,
            scratch_shapes=[pltpu.VMEM(item.shape, item.dtype) for item in results]
            + [dma((2, 4 * CHUNKS))],
            compiler_params=pltpu.CompilerParams(vmem_limit_bytes=VMEM_BYTES),
        )(*results)
    )


def solution(mesh):
    in_specs = (
        P("seq", "head"),
        P("seq", "head"),
        P("seq", "head"),
        P(),
        P(),
        P(("seq", "head"), None),
    )
    out_specs = (P(("seq", "head"), None), P("seq", "head"), P("seq", "head"), P("seq", "head"))
    return jax.shard_map(body, mesh=mesh, in_specs=in_specs, out_specs=out_specs, check_vma=False)
```
